32 devices in a mesh: ctx: 8 (over y, x, core), tp: 4 (over z).
Axes of the slice: x: 2, y: 2, z: 4, core: 2. Of those that a mesh axis runs over, the one named last changes fastest.
Arguments:
- upstream: bfloat16 [2048, 5120], P('ctx', 'tp'), may hold values from -6 to 6
- advantage: float32 [2048], P('ctx'), may hold values from -4 to 4
- out_weight: bfloat16 [8192, 5120], P('tp'), may hold values from -0.078125 to 0.078125
- query_heads: bfloat16 [2048, 8192], P('ctx', 'tp'), may hold values from -4 to 4
- key_heads: bfloat16 [2048, 1024], P('ctx', 'tp'), may hold values from -4 to 4
- value_heads: bfloat16 [2048, 1024], P('ctx', 'tp'), may hold values from -4 to 4
- segment_ids: int32 [2048], replicated, may hold values from 0 to 8, as said below
- tile_mask: int32 [16, 16], P('ctx'), may hold values from 0 to 1, as said below
Outputs:
- grad_queries: bfloat16 [2048, 8192], P('ctx', 'tp')
- grad_keys: bfloat16 [2048, 1024], P('ctx', 'tp')
- grad_values: bfloat16 [2048, 1024], P('ctx', 'tp')
The draws below stay inside these ranges and needn't reach their ends.
Inputs may be any that keep to these rules, and one draw needn't show every extreme that they name: `segment_ids`: the first 1024 tokens carry 0; after them come 8 runs carrying the numbers 1 to 8 in some order; run k (counted from 0) begins within 64 tokens of 1024 + k * 128, the first exactly at 1024. `tile_mask`: ones only where the key tile is not after the query tile; every tile lying wholly within the first 1024 tokens is marked for all query tiles at or after it; a marked key tile after the prompt begins no more than 384 tokens before the first token of the run that holds the query tile's first token.
All inputs are finite; a program needn't handle non-finite values.
Results may differ from the reference program's by a relative error of at most 0.0076.
Values may be sent and summed in bfloat16 or wider, within the bound.
No kernel may reach another device: no remote copies, remote signals or barrier semaphores. Data moves between devices by JAX's collectives and lax.ppermute only.
A program may use at most 128 MiB of HBM per device.

```python
import math
import jax
import jax.numpy as jnp
from jax import lax

D = 5120
HEADS = 64
KV_HEADS = 8
HD = 128
TILE = 128
ROLLOUTS = 8
TOKENS = 2048
PROMPT = 1024


def rollout_layout(key):
    span = (TOKENS - PROMPT) // ROLLOUTS
    labels = (jax.random.permutation(jax.random.fold_in(key, 5), ROLLOUTS) + 1).astype(jnp.int32)
    offsets = jax.random.randint(jax.random.fold_in(key, 6), (ROLLOUTS,), -(TILE // 2), TILE // 2).astype(jnp.int32)
    run_index = jnp.arange(ROLLOUTS, dtype=jnp.int32)
    offsets = jnp.where(run_index == 0, 0, offsets).astype(jnp.int32)
    bounds = (PROMPT + run_index * span + offsets).astype(jnp.int32)
    positions = jnp.arange(TOKENS, dtype=jnp.int32)
    slot = jnp.sum((positions[:, None] >= bounds[None, 1:]).astype(jnp.int32), axis=1).astype(jnp.int32)
    segments = jnp.where(positions >= PROMPT, labels[slot], 0).astype(jnp.int32)
    return (segments, span)


def draw_query_heads(key, part):
    key = jax.random.fold_in(key, 11)
    base = jax.random.truncated_normal(key, -4.0, 4.0, (TOKENS, HEADS * HD), jnp.float32)
    return base.astype(jnp.bfloat16)


def draw_key_heads(key, part):
    key = jax.random.fold_in(key, 12)
    base = jax.random.truncated_normal(key, -4.0, 4.0, (TOKENS, KV_HEADS * HD), jnp.float32)
    return base.astype(jnp.bfloat16)


def draw_segment_ids(key, part):
    segments, span = rollout_layout(key)
    return segments


def draw_tile_mask(key, part):
    segments, span = rollout_layout(key)
    key = jax.random.fold_in(key, 7)
    blocks = TOKENS // TILE
    tile_index = jnp.arange(blocks, dtype=jnp.int32)
    tile_start = tile_index * TILE
    slot = jnp.clip((tile_start - PROMPT) // span, 0, ROLLOUTS - 1).astype(jnp.int32)
    back_draw = jax.random.randint(jax.random.fold_in(key, 1), (ROLLOUTS,), 0, 3).astype(jnp.int32)
    back = jnp.where(jnp.arange(ROLLOUTS, dtype=jnp.int32) == 1, jnp.minimum(back_draw, 1), back_draw)
    back_tile = back[slot]
    parent = slot - back_tile
    has_parent = (tile_start >= PROMPT) & (back_tile > 0) & (parent >= 0)
    reach_tiles = max(span // TILE, 1)
    share_tiles = jax.random.randint(jax.random.fold_in(key, 2), (ROLLOUTS,), 1, reach_tiles + 1).astype(jnp.int32)
    share_rows = share_tiles[slot] * TILE
    parent_start = PROMPT + parent * span
    shared = has_parent[:, None] & (tile_start[None, :] >= parent_start[:, None]) & (tile_start[None, :] < (parent_start + share_rows)[:, None])
    prompt_tile = (tile_start + TILE <= PROMPT)[None, :]
    causal = tile_index[None, :] <= tile_index[:, None]
    return (causal & (prompt_tile | shared)).astype(jnp.int32)


def steps_of(rng, dims, pieces, low, largest):
    def one(axis_at, parts):
        draws = jax.random.uniform(jax.random.fold_in(jax.random.fold_in(rng, 6), axis_at), (parts,), jnp.float32, low / len(pieces), largest / len(pieces))
        return jnp.repeat(jnp.exp(draws), dims[axis_at] // parts).reshape((-1,) + (1,) * (len(dims) - axis_at - 1))

    factor_of = one(*pieces[0])
    for cut in pieces[1:]:
        factor_of = factor_of * one(*cut)
    return factor_of


def normal_values(key, dims, width, most, cuts=(), kind=jnp.bfloat16):
    entries = jax.random.normal(key, dims, jnp.float32) * width
    if len(cuts) > 0:
        entries = steps_of(key, dims, cuts, -0.22, 0.18) * entries
    return jnp.clip(entries, min=-most, max=most).astype(kind)


def setup_inputs(seed: int = 0) -> dict:
    streams_of = jax.random.split(jax.random.key(seed), 9)
    upstream = normal_values(streams_of[0], (TOKENS, D), 1.0, 6.0, ((0, 8), (1, 4)))
    advantage = normal_values(streams_of[1], (TOKENS,), 1.0, 4.0, ((0, 8),), jnp.float32)
    out_weight = normal_values(streams_of[2], (HEADS * HD, D), D ** -0.5, 0.078125, ((0, 4),))
    query_heads = draw_query_heads(jax.random.fold_in(streams_of[8], 71), 0)
    key_heads = draw_key_heads(jax.random.fold_in(streams_of[8], 71), 0)
    value_heads = normal_values(streams_of[5], (TOKENS, KV_HEADS * HD), 1.0, 4.0, ((0, 8), (1, 4)))
    segment_ids = draw_segment_ids(jax.random.fold_in(streams_of[8], 71), 0)
    tile_mask = draw_tile_mask(jax.random.fold_in(streams_of[8], 71), 0)
    return dict(upstream=upstream, advantage=advantage, out_weight=out_weight, query_heads=query_heads, key_heads=key_heads, value_heads=value_heads, segment_ids=segment_ids, tile_mask=tile_mask)


def reference(upstream, advantage, out_weight, query_heads, key_heads, value_heads, segment_ids, tile_mask):
    share = HEADS // KV_HEADS
    scale = 1.0 / math.sqrt(HD)
    projected = jnp.dot(upstream, out_weight.T, preferred_element_type=jnp.float32)
    grad_heads = (projected * advantage[:, None]).astype(jnp.bfloat16)
    positions = jnp.arange(TOKENS, dtype=jnp.int32)
    tiles = positions // TILE
    tile_full = tile_mask[tiles][:, tiles]
    visible = (positions[None, :] <= positions[:, None]) & ((segment_ids[:, None] == segment_ids[None, :]) | (tile_full == 1))

    def one_head(head_index):
        group_index = head_index // share
        query = lax.dynamic_slice_in_dim(query_heads, (head_index * HD).astype(jnp.int32), HD, 1)
        grad_rows = lax.dynamic_slice_in_dim(grad_heads, (head_index * HD).astype(jnp.int32), HD, 1)
        key_group = lax.dynamic_slice_in_dim(key_heads, (group_index * HD).astype(jnp.int32), HD, 1)
        value_group = lax.dynamic_slice_in_dim(value_heads, (group_index * HD).astype(jnp.int32), HD, 1)
        scores = jnp.dot(query, key_group.T, preferred_element_type=jnp.float32) * scale
        masked = jnp.where(visible, scores, -1e+30)
        row_max = lax.optimization_barrier(jnp.max(masked, axis=1))
        summed = lax.optimization_barrier(jnp.sum(jnp.where(visible, jnp.exp(masked - row_max[:, None]), 0.0), axis=1))
        log_total = row_max + jnp.log(summed)
        probs = jnp.where(visible, jnp.exp(masked - log_total[:, None]), 0.0)
        attn_out = jnp.dot(probs, value_group.astype(jnp.float32), precision=lax.Precision.HIGHEST)
        delta = lax.optimization_barrier(jnp.sum(grad_rows.astype(jnp.float32) * attn_out, axis=1))
        dprobs = jnp.dot(grad_rows, value_group.T, preferred_element_type=jnp.float32)
        dscores = (probs * (dprobs - delta[:, None])).astype(jnp.bfloat16)
        probs_low = probs.astype(jnp.bfloat16)
        grad_query = (jnp.dot(dscores, key_group, preferred_element_type=jnp.float32) * scale).astype(jnp.bfloat16)
        key_term = jnp.dot(dscores.T, query, preferred_element_type=jnp.float32) * scale
        value_term = jnp.dot(probs_low.T, grad_rows, preferred_element_type=jnp.float32)
        return (grad_query, key_term, value_term)
    query_parts, key_parts, value_parts = lax.map(one_head, jnp.arange(HEADS, dtype=jnp.int32))
    grad_queries = query_parts.transpose(1, 0, 2).reshape(TOKENS, HEADS * HD)
    grad_keys = key_parts.reshape(KV_HEADS, share, TOKENS, HD).sum(axis=1)
    grad_keys = grad_keys.transpose(1, 0, 2).reshape(TOKENS, KV_HEADS * HD).astype(jnp.bfloat16)
    grad_values = value_parts.reshape(KV_HEADS, share, TOKENS, HD).sum(axis=1)
    grad_values = grad_values.transpose(1, 0, 2).reshape(TOKENS, KV_HEADS * HD).astype(jnp.bfloat16)
    return (grad_queries, grad_keys, grad_values)
```

```python
import functools
import math

import jax
import jax.numpy as jnp
from jax import lax
from jax.experimental import pallas as pl
from jax.experimental.pallas import tpu as pltpu
from jax.sharding import PartitionSpec as P

HEADS = 64
KV_HEADS = 8
SHARE = HEADS // KV_HEADS
HD = 128
TILE = 128
ROLLOUTS = 8
JITTER = 64
KB = 256
SCALE = 1.0 / math.sqrt(HD)
LOG2E = 1.4426950408889634
F32 = jnp.float32
BF16 = jnp.bfloat16
NT = (((1,), (1,)), ((), ()))


def dot(a, b):
    return jnp.dot(a, b, preferred_element_type=F32)


def dot_nt(a, b):
    return lax.dot_general(a, b, NT, preferred_element_type=F32)


def probs_kernel(n_kb, slot_ref, q_ref, k_ref, v_ref, bias_ref, p_ref, o_ref, s_ref):
    q = q_ref[...]
    top = None
    for kb in range(n_kb):
        s = dot_nt(k_ref[slot_ref[kb]], q) * (SCALE * LOG2E) + bias_ref[kb]
        s_ref[kb] = s
        m = jnp.max(s, axis=0, keepdims=True)
        top = m if top is None else jnp.maximum(top, m)
    total = jnp.zeros_like(top)
    for kb in range(n_kb):
        e = jnp.exp2(s_ref[kb] - top)
        s_ref[kb] = e
        total += jnp.sum(e, axis=0, keepdims=True)
    inv = 1.0 / total
    low = jnp.zeros_like(top)
    acc = jnp.zeros((HD, q.shape[0]), F32)
    for kb in range(n_kb):
        p = (s_ref[kb] * inv).astype(BF16)
        p_ref[0, kb] = p
        low += jnp.sum(p.astype(F32), axis=0, keepdims=True)
        acc += dot(v_ref[slot_ref[kb]].T, p)
    o_ref[...] = (acc * (1.0 / low)).T


def probs_call(slots, q, kv, bias, groups, n_kb):
    rows = q.shape[0]
    rb = rows // KB
    n_slot = kv.shape[0]
    return pl.pallas_call(
        functools.partial(probs_kernel, n_kb),
        grid_spec=pltpu.PrefetchScalarGridSpec(
            num_scalar_prefetch=1,
            grid=(groups, SHARE, rb),
            in_specs=[
                pl.BlockSpec((KB, HD), lambda g, h, r, s: (r, g * SHARE + h)),
                pl.BlockSpec((n_slot, KB, HD), lambda g, h, r, s: (0, 0, g)),
                pl.BlockSpec((n_slot, KB, HD), lambda g, h, r, s: (0, 0, groups + g)),
                pl.BlockSpec((n_kb, KB, KB), lambda g, h, r, s: (0, 0, r)),
            ],
            out_specs=[
                pl.BlockSpec((1, n_kb, KB, KB), lambda g, h, r, s: (g, 0, 0, h * rb + r)),
                pl.BlockSpec((KB, HD), lambda g, h, r, s: (r, g * SHARE + h)),
            ],
            scratch_shapes=[pltpu.VMEM((n_kb, KB, KB), F32)],
        ),
        out_shape=[
            jax.ShapeDtypeStruct((groups, n_kb, KB, SHARE * rows), BF16),
            jax.ShapeDtypeStruct((rows, groups * SHARE * HD), F32),
        ],
        compiler_params=pltpu.CompilerParams(vmem_limit_bytes=48 << 20),
        cost_estimate=pl.CostEstimate(
            flops=4 * groups * SHARE * rows * n_kb * KB * HD,
            bytes_accessed=groups * SHARE * rows * n_kb * KB * 2,
            transcendentals=groups * SHARE * rows * n_kb * KB,
        ),
    )(slots, q, kv, kv, bias)


def back_kernel(
    n_kb, slot_ref, live_ref, proj_ref, adv_ref, o_ref, q_ref, k_ref, v_ref, p_ref,
    dq_ref, dkv_ref, dox_ref, qs_ref, ds_ref, dqt_ref,
):
    kb = pl.program_id(1)
    rows = proj_ref.shape[0]

    @pl.when(kb == 0)
    def _():
        dqt_ref[...] = jnp.zeros_like(dqt_ref)
        lane = lax.broadcasted_iota(jnp.int32, (rows, HD), 1)
        for h in range(SHARE):
            cols = pl.ds(h * HD, HD)
            here = pl.ds(h * rows, rows)
            grad = (proj_ref[:, cols] * adv_ref[...]).astype(BF16)
            delta = jnp.sum(grad.astype(F32) * o_ref[:, cols], axis=1, keepdims=True)
            one = delta.astype(BF16).astype(F32)
            two = (delta - one).astype(BF16).astype(F32)
            three = delta - one - two
            ext = jnp.where(
                lane == 0, one, jnp.where(lane == 1, two, jnp.where(lane == 2, three, 0.0))
            )
            dox_ref[here, :HD] = grad
            dox_ref[here, HD:] = ext.astype(BF16)
            qs_ref[here, :] = q_ref[:, cols]

    @pl.when(live_ref[kb] != 0)
    def _():
        lane = lax.broadcasted_iota(jnp.int32, (KB, HD), 1)
        ext = jnp.where(lane < 3, -1.0, 0.0).astype(BF16)
        vx = jnp.concatenate([v_ref[0], ext], axis=1)
        kt = k_ref[0].T
        for h in range(SHARE * rows // KB):
            here = pl.ds(h * KB, KB)
            dp = dot_nt(vx, dox_ref[here, :])
            ds_ref[:, here] = (p_ref[0, 0, :, here].astype(F32) * dp).astype(BF16)
        dkv_ref[0, 0] = dot(ds_ref[...], qs_ref[...]).astype(dkv_ref.dtype)
        dkv_ref[0, 1] = dot(p_ref[0, 0], dox_ref[:, :HD]).astype(dkv_ref.dtype)
        dqt_ref[...] += dot(kt, ds_ref[...])

    @pl.when(live_ref[kb] == 0)
    def _():
        dkv_ref[...] = jnp.zeros_like(dkv_ref)

    @pl.when(kb == n_kb - 1)
    def _():
        for h in range(SHARE):
            dq_ref[:, h * HD : (h + 1) * HD] = (
                (dqt_ref[:, h * rows : (h + 1) * rows] * SCALE).T.astype(BF16)
            )


def back_call(slots, live, proj, adv, o, q, kv, p, groups, n_kb, part_dtype):
    rows = q.shape[0]
    wide = SHARE * HD
    return pl.pallas_call(
        functools.partial(back_kernel, n_kb),
        grid_spec=pltpu.PrefetchScalarGridSpec(
            num_scalar_prefetch=2,
            grid=(groups, n_kb),
            in_specs=[
                pl.BlockSpec((rows, wide), lambda g, b, s, e: (0, g)),
                pl.BlockSpec((rows, 1), lambda g, b, s, e: (0, 0)),
                pl.BlockSpec((rows, wide), lambda g, b, s, e: (0, g)),
                pl.BlockSpec((rows, wide), lambda g, b, s, e: (0, g)),
                pl.BlockSpec((1, KB, HD), lambda g, b, s, e: (s[b], 0, g)),
                pl.BlockSpec((1, KB, HD), lambda g, b, s, e: (s[b], 0, groups + g)),
                pl.BlockSpec((1, 1, KB, SHARE * rows), lambda g, b, s, e: (g, b, 0, 0)),
            ],
            out_specs=[
                pl.BlockSpec((rows, wide), lambda g, b, s, e: (0, g)),
                pl.BlockSpec((1, 2, KB, HD), lambda g, b, s, e: (b, 0, 0, g)),
            ],
            scratch_shapes=[
                pltpu.VMEM((SHARE * rows, 2 * HD), BF16),
                pltpu.VMEM((SHARE * rows, HD), BF16),
                pltpu.VMEM((KB, SHARE * rows), BF16),
                pltpu.VMEM((HD, SHARE * rows), F32),
            ],
        ),
        out_shape=[
            jax.ShapeDtypeStruct((rows, groups * wide), BF16),
            jax.ShapeDtypeStruct((n_kb, 2, KB, groups * HD), part_dtype),
        ],
        compiler_params=pltpu.CompilerParams(vmem_limit_bytes=48 << 20),
        cost_estimate=pl.CostEstimate(
            flops=10 * groups * SHARE * rows * n_kb * KB * HD,
            bytes_accessed=groups * SHARE * rows * n_kb * KB * 2,
            transcendentals=0,
        ),
    )(slots, live, proj, adv, o, q, kv, kv, p)


def project_kernel(count, shard_ref, *refs):
    xs, ws, out_ref = refs[:count], refs[count : 2 * count], refs[-1]
    acc = dot_nt(xs[0][...], ws[0][...])
    for x, w in zip(xs[1:], ws[1:]):
        acc += dot_nt(x[...], w[...])
    out_ref[...] = acc


def project_last_kernel(shard_ref, acc_ref, c_ref, d_ref, w_ref, out_ref):
    out_ref[...] = acc_ref[...] + dot_nt(c_ref[...] + d_ref[...], w_ref[...])


def project_call(shards_of, xs, weight):
    rows, depth = xs[0].shape
    wide = weight.shape[0]
    block = 512
    count = len(xs)
    return pl.pallas_call(
        functools.partial(project_kernel, count),
        grid_spec=pltpu.PrefetchScalarGridSpec(
            num_scalar_prefetch=1,
            grid=(wide // block,),
            in_specs=[pl.BlockSpec((rows, depth), lambda n, s: (0, 0))] * count
            + [pl.BlockSpec((block, depth), lambda n, s, i=i: (n, s[i])) for i in range(count)],
            out_specs=pl.BlockSpec((rows, block), lambda n, s: (0, n)),
        ),
        out_shape=jax.ShapeDtypeStruct((rows, wide), F32),
        compiler_params=pltpu.CompilerParams(vmem_limit_bytes=48 << 20),
        cost_estimate=pl.CostEstimate(
            flops=2 * rows * wide * depth * count,
            bytes_accessed=2 * wide * depth * count,
            transcendentals=0,
        ),
    )(shards_of, *xs, *([weight] * count))


def project_last_call(shards_of, acc, c, d, weight):
    rows, depth = c.shape
    wide = weight.shape[0]
    block = 512
    return pl.pallas_call(
        project_last_kernel,
        grid_spec=pltpu.PrefetchScalarGridSpec(
            num_scalar_prefetch=1,
            grid=(wide // block,),
            in_specs=[
                pl.BlockSpec((rows, block), lambda n, s: (0, n)),
                pl.BlockSpec((rows, depth), lambda n, s: (0, 0)),
                pl.BlockSpec((rows, depth), lambda n, s: (0, 0)),
                pl.BlockSpec((block, depth), lambda n, s: (n, s[0])),
            ],
            out_specs=pl.BlockSpec((rows, block), lambda n, s: (0, n)),
        ),
        out_shape=jax.ShapeDtypeStruct((rows, wide), F32),
        compiler_params=pltpu.CompilerParams(vmem_limit_bytes=48 << 20),
        cost_estimate=pl.CostEstimate(
            flops=2 * rows * wide * depth, bytes_accessed=2 * wide * depth, transcendentals=0
        ),
    )(shards_of, acc, c, d, weight)


def key_window(tok_rows, total):
    span = (total - total // 2) // ROLLOUTS
    reach = 3 * span + TILE + JITTER
    reach = reach // TILE * TILE
    return -(-reach // tok_rows)


def shards(
    upstream, advantage, out_weight, query_heads, key_heads, value_heads, segment_ids, tile_mask
):
    rows = query_heads.shape[0]
    n_ctx = lax.axis_size("ctx")
    n_tp = lax.axis_size("tp")
    total = rows * n_ctx
    prompt = total // 2
    groups = key_heads.shape[1] // HD
    me = lax.axis_index("ctx")
    z = lax.axis_index("tp")
    per = rows // KB
    back = key_window(rows, total)
    prompt_kb = prompt // KB
    n_kb = prompt_kb + (back + 1) * per
    fast = n_ctx == 8 and n_tp == 4 and per == 1 and back == 2
    part_dtype = BF16

    own = jnp.concatenate([key_heads, value_heads], axis=1)

    def hop(value, pairs):
        return lax.ppermute(value, "tp", pairs)

    def flip(value, bit, pairs=None):
        return lax.ppermute(value, "ctx", pairs or [(i, i ^ bit) for i in range(n_ctx)])

    if fast:
        near = jnp.stack([own] + [flip(own, d) for d in (2, 4, 6)])
        far = flip(near, 1)
        kv = jnp.stack([near, far], axis=1).reshape(n_ctx, rows, 2 * groups * HD)
        up_b = hop(upstream, [(0, 2), (2, 0), (1, 3), (3, 1)])
        up_a = hop(upstream, [(0, 1), (1, 0), (2, 3), (3, 2)])
        up_c = hop(upstream, [(1, 2), (2, 1)])
        up_d = hop(up_b, [(1, 0), (2, 3)])
    else:
        kv = lax.all_gather(own, "ctx", axis=0)

    row_start = me * rows
    behind = me - back
    roll = row_start >= prompt
    win_start = jnp.maximum(behind * rows, 0)
    win = (back + 1) * rows
    pos = jnp.concatenate(
        [jnp.arange(prompt, dtype=jnp.int32), win_start + jnp.arange(win, dtype=jnp.int32)]
    )
    seg_k = jnp.concatenate(
        [segment_ids[:prompt], lax.dynamic_slice_in_dim(segment_ids, win_start, win, 0)]
    )
    seg_q = lax.dynamic_slice_in_dim(segment_ids, row_start, rows, 0)
    marks = jnp.concatenate(
        [
            tile_mask[:, : prompt // TILE],
            lax.dynamic_slice_in_dim(tile_mask, win_start // TILE, win // TILE, 1),
        ],
        axis=1,
    )
    marks = jnp.repeat(jnp.repeat(marks.T, TILE, axis=0), TILE, axis=1) == 1
    query_pos = row_start + jnp.arange(rows, dtype=jnp.int32)
    counted = (jnp.arange(prompt + win) < prompt) | (roll & (pos >= prompt))
    visible = (
        (pos[:, None] <= query_pos[None, :])
        & ((seg_k[:, None] == seg_q[None, :]) | marks)
        & counted[:, None]
    )
    bias = jnp.where(visible, 0.0, -1e30).astype(F32).reshape(n_kb, KB, rows)
    live = jnp.any(visible.reshape(n_kb, KB * rows), axis=1).astype(jnp.int32)
    block = jnp.arange(n_kb, dtype=jnp.int32)
    holder = jnp.where(
        block < prompt_kb,
        block // per,
        jnp.where(roll, behind + (block - prompt_kb) // per, me),
    )
    slot = (holder ^ me) if fast else holder
    slots = (slot * per + block % per).astype(jnp.int32)
    kv = kv.reshape(n_ctx * per, KB, 2 * groups * HD)

    probs, attn = probs_call(slots, query_heads, kv, bias, groups, n_kb)

    if fast:
        three = jnp.stack([z, z ^ 1, z ^ 2]).astype(jnp.int32)
        acc = project_call(three, [upstream, up_a, up_b], out_weight)
        last = (z ^ 3).astype(jnp.int32)[None]
        proj = project_last_call(last, acc, up_c, up_d, out_weight)
    else:
        proj = lax.dot_general(
            lax.all_gather(upstream, "tp", axis=1, tiled=True), out_weight, NT,
            preferred_element_type=F32,
        )

    grad_queries, part = back_call(
        slots, live, proj, advantage[:, None], attn, query_heads, kv, probs, groups, n_kb,
        part_dtype,
    )

    if fast:
        core = me & 1
        side = (me >> 1) & 1
        pick = lambda i: lax.dynamic_index_in_dim(part, i, 0, keepdims=False)
        sent = jnp.stack([pick(1 - core), pick(3 - core), part[prompt_kb + 1]])
        got = flip(sent, 1).astype(F32)
        sums = jnp.stack([pick(core), pick(core + 2)]).astype(F32) + got[:2]
        here = lax.dynamic_index_in_dim(sums, side, 0, keepdims=False)
        there = lax.dynamic_index_in_dim(sums, 1 - side, 0, keepdims=False)
        older = part[prompt_kb].astype(F32) + jnp.where(core == 1, got[2], 0.0)
        mine = part[prompt_kb + 2].astype(F32) + jnp.where(core == 0, got[2], 0.0)
        low = there.astype(BF16)
        by_y = flip(here.astype(BF16), 4, [(4, 0), (5, 1), (6, 2), (7, 3)])
        by_d = flip(low, 6, [(4, 2), (5, 3), (6, 0), (7, 1)])
        by_x = flip(
            jnp.where(roll, older.astype(BF16), low), 2,
            [(0, 2), (2, 0), (1, 3), (3, 1), (6, 4), (7, 5)],
        )
        grads = (
            jnp.where(roll, mine, here)
            + by_x.astype(F32) + by_y.astype(F32) + by_d.astype(F32)
        )
        grad_keys, grad_values = grads[0], grads[1]
    else:
        width = groups * HD
        front = part[:prompt_kb].astype(F32).transpose(0, 2, 1, 3).reshape(prompt, 2, width)
        rear = part[prompt_kb:].astype(F32).transpose(0, 2, 1, 3).reshape(win, 2, width)
        whole = jnp.zeros((total, 2, width), F32).at[:prompt].set(front)
        old = lax.dynamic_slice_in_dim(whole, win_start, win, 0)
        whole = lax.dynamic_update_slice_in_dim(whole, old + rear, win_start, 0)
        reduced = lax.psum_scatter(whole, "ctx", scatter_dimension=0, tiled=True)
        grad_keys, grad_values = reduced[:, 0], reduced[:, 1]
    return (grad_queries, (grad_keys * SCALE).astype(BF16), grad_values.astype(BF16))


def solution(mesh):
    placed = (
        P("ctx", "tp"),
        P("ctx"),
        P("tp", None),
        P("ctx", "tp"),
        P("ctx", "tp"),
        P("ctx", "tp"),
        P(),
        P("ctx", None),
    )
    return jax.shard_map(
        shards,
        mesh=mesh,
        in_specs=placed,
        out_specs=(P("ctx", "tp"), P("ctx", "tp"), P("ctx", "tp")),
        check_vma=False,
    )
```

```python
import functools
import math

import jax
import jax.numpy as jnp
from jax import lax
from jax.experimental import pallas as pl
from jax.experimental.pallas import tpu as pltpu
from jax.sharding import PartitionSpec as P

HEADS = 64
KV_HEADS = 8
SHARE = HEADS // KV_HEADS
HD = 128
TILE = 128
ROLLOUTS = 8
JITTER = 64
KB = 256
VMEM_LIMIT = 24 << 20
SCALE = 1.0 / math.sqrt(HD)
LOG2E = 1.4426950408889634
F32 = jnp.float32
BF16 = jnp.bfloat16
NT = (((1,), (1,)), ((), ()))


def dot(a, b):
    return jnp.dot(a, b, preferred_element_type=F32)


def dot_nt(a, b):
    return lax.dot_general(a, b, NT, preferred_element_type=F32)


SMEM = pl.BlockSpec(memory_space=pltpu.SMEM)
VMEM = pl.BlockSpec(memory_space=pltpu.VMEM)


def at(start, size):
    return pl.ds(pl.multiple_of(start, size), size)


def call(kernel, ins, in_specs, outs, scratch=(), out_specs=None, flops=0, size=0, exps=0):
    return pl.pallas_call(
        kernel,
        in_specs=in_specs,
        out_specs=out_specs or [VMEM] * len(outs),
        out_shape=[jax.ShapeDtypeStruct(shape, dtype) for shape, dtype in outs],
        scratch_shapes=list(scratch),
        compiler_params=pltpu.CompilerParams(vmem_limit_bytes=VMEM_LIMIT),
        cost_estimate=pl.CostEstimate(flops=flops, bytes_accessed=size, transcendentals=exps),
    )(*ins)


def mask_kernel(n_kb, prompt, back, total, me_ref, seg_ref, tile_ref, bias_ref, live_ref):
    rows = bias_ref.shape[2]
    per = rows // KB
    me = me_ref[0]
    row_start = me * rows
    win_kb = jnp.maximum(me - back, 0) * per
    key_at = lax.broadcasted_iota(jnp.int32, (KB, KB), 0)
    query_at = lax.broadcasted_iota(jnp.int32, (KB, KB), 1)
    for kb in range(n_kb):
        window = kb >= prompt // KB
        block = win_kb + (kb - prompt // KB) if window else kb
        key_pos = block * KB + key_at
        seg_k = jnp.broadcast_to(seg_ref[block], (KB, KB)).T
        some = jnp.int32(0)
        for r in range(per):
            same = seg_k == jnp.broadcast_to(seg_ref[me * per + r], (KB, KB))
            for a in range(KB // TILE):
                for b in range(KB // TILE):
                    mark = tile_ref[r * (KB // TILE) + b, block * (KB // TILE) + a]
                    inside = (key_at // TILE == a) & (query_at // TILE == b)
                    same = same | (inside & (jnp.full((KB, KB), mark) == 1))
            seen = same & (key_pos <= row_start + r * KB + query_at)
            if window:
                seen = seen & (key_pos >= prompt) & (jnp.full((KB, KB), me) >= prompt // rows)
            bias_ref[kb, :, r * KB : (r + 1) * KB] = jnp.where(seen, 0.0, -1e30)
            some = jnp.maximum(some, jnp.max(seen.astype(jnp.int32)))
        live_ref[kb] = some


def mask_call(me, segment_ids, tile_mask, rows, n_kb, prompt, back):
    total = segment_ids.shape[0]
    return call(
        functools.partial(mask_kernel, n_kb, prompt, back, total),
        (me[None], segment_ids.reshape(total // KB, 1, KB), tile_mask),
        [SMEM, VMEM, SMEM],
        [((n_kb, KB, rows), F32), ((n_kb,), jnp.int32)],
        out_specs=[VMEM, SMEM],
        size=n_kb * KB * rows * 4,
    )


def probs_kernel(
    n_kb, groups, slot_ref, q_ref, near_ref, far_ref, bias_ref,
    p_ref, o_ref, inv_ref, k_ref, v_ref, kx_ref, vt_ref, s_ref,
):
    rows = q_ref.shape[0]
    per = rows // KB
    n_near = near_ref.shape[0]
    lane = lax.broadcasted_iota(jnp.int32, (KB, HD), 1)
    inv_ref[...] = jnp.zeros_like(inv_ref)
    vt_ref[:, HD:, :] = jnp.ones((groups, 16, n_kb * KB), BF16)
    for kb in range(n_kb):
        slot = slot_ref[kb]
        keys = pl.ds(kb * KB, KB)

        def place(source, index):
            for g in range(groups):
                k_ref[g, keys, :] = source[index, :, g * HD : (g + 1) * HD]
                v_ref[g, keys, :] = source[index, :, (groups + g) * HD : (groups + g + 1) * HD]

        @pl.when(slot < n_near)
        def _():
            place(near_ref, slot)

        @pl.when(slot >= n_near)
        def _():
            place(far_ref, slot - n_near)

    for g in range(groups):
        for kb in range(n_kb):
            keys = pl.ds(kb * KB, KB)
            k = k_ref[g, keys, :]
            kx_ref[g, keys, :HD] = k
            kx_ref[g, keys, HD:] = k
            vt_ref[g, :HD, keys] = v_ref[g, keys, :].T

    def step(i, carry):
        head, r = i // per, i % per
        g, h = head // SHARE, head % SHARE
        cols = at((h * per + r) * KB, KB)
        here = at(r * KB, KB)
        q = q_ref[here, at(head * HD, HD)].astype(F32) * (SCALE * LOG2E)
        q_hi = q.astype(BF16)
        q_lo = (q - q_hi.astype(F32)).astype(BF16)
        qx = jnp.concatenate([q_hi, q_lo], axis=1)
        s_ref[...] = dot_nt(kx_ref[g], qx) + bias_ref[:, :, here].reshape(n_kb * KB, KB)
        top = jnp.max(s_ref[...], axis=0, keepdims=True)
        p_ref[g, :, cols] = jnp.exp2(s_ref[...] - top).astype(BF16)
        acc = dot(vt_ref[g], p_ref[g, :, cols])
        inv = 1.0 / acc[HD : HD + 1, :]
        o_ref[here, at(head * HD, HD)] = (acc[:HD] * inv).T
        inv_ref[here, :] += jnp.where(lane == head, jnp.broadcast_to(inv, (HD, KB)).T, 0.0)
        return carry

    lax.fori_loop(0, groups * SHARE * per, step, 0, unroll=UNROLL)


UNROLL = 2


def probs_call(slots, q, near, far, bias, groups, n_kb):
    rows = q.shape[0]
    keys = n_kb * KB
    return call(
        functools.partial(probs_kernel, n_kb, groups),
        (slots, q, near, far, bias),
        [SMEM, VMEM, VMEM, VMEM, VMEM],
        [
            ((groups, keys, SHARE * rows), BF16),
            ((rows, groups * SHARE * HD), F32),
            ((rows, HD), F32),
            ((groups, keys, HD), BF16),
            ((groups, keys, HD), BF16),
        ],
        scratch=[
            pltpu.VMEM((groups, keys, 2 * HD), BF16),
            pltpu.VMEM((groups, HD + 16, keys), BF16),
            pltpu.VMEM((keys, KB), F32),
        ],
        flops=6 * groups * SHARE * rows * keys * HD,
        size=groups * SHARE * rows * keys * 2,
        exps=groups * SHARE * rows * keys,
    )


def back_kernel(
    n_kb, n_send, first, live_ref, pos_ref, proj_ref, x1_ref, x2_ref, w_ref, adv_ref, o_ref,
    inv_ref, q_ref, k_ref, v_ref, p_ref,
    dq_ref, send_ref, keep_ref, dox_ref, qs_ref, ds_ref, dqt_ref,
):
    rows = proj_ref.shape[0]
    group = first // SHARE
    lane = lax.broadcasted_iota(jnp.int32, (rows, HD), 1)
    minus = jnp.where(lax.broadcasted_iota(jnp.int32, (KB, HD), 1) < 3, -1.0, 0.0).astype(BF16)
    x = x1_ref[...] + x2_ref[...]
    dqt_ref[...] = jnp.zeros_like(dqt_ref)
    for h in range(SHARE):
        head = first + h
        cols = pl.ds(head * HD, HD)
        here = pl.ds(h * rows, rows)
        inv = inv_ref[:, head : head + 1]
        proj = proj_ref[:, cols] + dot_nt(x, w_ref[cols, :])
        grad = (proj * (adv_ref[...] * inv)).astype(BF16)
        delta = jnp.sum(grad.astype(F32) * o_ref[:, cols], axis=1, keepdims=True)
        one = delta.astype(BF16).astype(F32)
        two = (delta - one).astype(BF16).astype(F32)
        three = delta - one - two
        ext = jnp.where(
            lane == 0, one, jnp.where(lane == 1, two, jnp.where(lane == 2, three, 0.0))
        )
        dox_ref[here, :HD] = grad
        dox_ref[here, HD:] = ext.astype(BF16)
        qs_ref[here, :] = q_ref[:, cols]

    def step(kb, carry):
        pos = pos_ref[kb]

        def put(value):
            @pl.when(pos < n_send)
            def _():
                send_ref[pos] = value

            @pl.when(pos >= n_send)
            def _():
                keep_ref[pos - n_send] = value

        @pl.when(live_ref[kb] != 0)
        def _():
            keys = at(kb * KB, KB)
            vx = jnp.concatenate([v_ref[group, keys, :], minus], axis=1)
            kt = k_ref[group, keys, :].T
            dv = dot(p_ref[group, keys, :], dox_ref[:, :HD])
            for h in range(SHARE * rows // KB):
                here = pl.ds(h * KB, KB)
                dp = dot_nt(vx, dox_ref[here, :])
                ds_ref[:, here] = (p_ref[group, keys, here].astype(F32) * dp).astype(BF16)
            dqt_ref[...] += dot(kt, ds_ref[...])
            dk = dot(ds_ref[...], qs_ref[...])
            put(jnp.stack([dk, dv]).astype(BF16))

        @pl.when(live_ref[kb] == 0)
        def _():
            put(jnp.zeros((2, KB, HD), BF16))

        return carry

    lax.fori_loop(0, n_kb, step, 0)
    for h in range(SHARE):
        dq_ref[:, pl.ds(h * HD, HD)] = (
            (dqt_ref[:, h * rows : (h + 1) * rows] * SCALE).T.astype(BF16)
        )


def back_call(group, live, pos, proj, x1, x2, w, adv, o, inv, q, k, v, p, n_kb, n_send):
    rows = q.shape[0]
    wide = SHARE * HD
    return call(
        functools.partial(back_kernel, n_kb, n_send, group * SHARE),
        (live, pos, proj, x1, x2, w, adv, o, inv, q, k, v, p),
        [SMEM, SMEM] + [VMEM] * 11,
        [
            ((rows, wide), BF16),
            ((max(n_send, 1), 2, KB, HD), BF16),
            ((n_kb - n_send, 2, KB, HD), BF16),
        ],
        scratch=[
            pltpu.VMEM((SHARE * rows, 2 * HD), BF16),
            pltpu.VMEM((SHARE * rows, HD), BF16),
            pltpu.VMEM((KB, SHARE * rows), BF16),
            pltpu.VMEM((HD, SHARE * rows), F32),
        ],
        flops=10 * SHARE * rows * n_kb * KB * HD,
        size=SHARE * rows * n_kb * KB * 2,
    )


def middle_kernel(me_ref, got_ref, keep_ref, base_ref, x_ref, y_ref, d_ref):
    me = me_ref[0]
    core, side, roll = me & 1, (me >> 1) & 1, me >= 4
    here = keep_ref[side].astype(F32) + got_ref[side].astype(F32)
    there = keep_ref[1 - side].astype(F32) + got_ref[1 - side].astype(F32)
    y_ref[...] = here.astype(BF16)
    d_ref[...] = there.astype(BF16)
    got = got_ref[2].astype(F32)
    late = (jnp.full(got.shape, core) == 1)

    @pl.when(roll)
    def _():
        x_ref[...] = (keep_ref[2].astype(F32) + jnp.where(late, got, 0.0)).astype(BF16)
        base_ref[...] = keep_ref[3].astype(F32) + jnp.where(late, 0.0, got)

    @pl.when(jnp.logical_not(roll))
    def _():
        x_ref[...] = there.astype(BF16)
        base_ref[...] = here


def last_kernel(groups, *refs):
    dk_ref, dv_ref = refs[-2:]
    for g in range(groups):
        base, x, y, d = refs[4 * g : 4 * g + 4]
        total = base[...] + x[...].astype(F32) + y[...].astype(F32) + d[...].astype(F32)
        dk_ref[:, g * HD : (g + 1) * HD] = (total[0] * SCALE).astype(BF16)
        dv_ref[:, g * HD : (g + 1) * HD] = total[1].astype(BF16)


def project_kernel(shard_ref, *refs):
    out_ref = refs[-1]
    pairs = (len(refs) - 1) // 2
    acc = dot_nt(refs[0][...], refs[pairs][...])
    for i in range(1, pairs):
        acc += dot_nt(refs[i][...], refs[pairs + i][...])
    out_ref[...] = acc


def project_add_kernel(shard_ref, acc_ref, *refs):
    project_kernel(shard_ref, *refs)
    refs[-1][...] += acc_ref[...]


def project_call(shards_of, xs, weight, acc=None):
    rows, depth = xs[0].shape
    wide = weight.shape[0]
    block = 512
    count = len(xs)
    tile = pl.BlockSpec((rows, block), lambda n, s: (0, n))
    return pl.pallas_call(
        project_kernel if acc is None else project_add_kernel,
        grid_spec=pltpu.PrefetchScalarGridSpec(
            num_scalar_prefetch=1,
            grid=(wide // block,),
            in_specs=([] if acc is None else [tile])
            + [pl.BlockSpec((rows, depth), lambda n, s: (0, 0))] * count
            + [pl.BlockSpec((block, depth), lambda n, s, i=i: (n, s[i])) for i in range(count)],
            out_specs=tile,
        ),
        out_shape=jax.ShapeDtypeStruct((rows, wide), F32),
        compiler_params=pltpu.CompilerParams(vmem_limit_bytes=VMEM_LIMIT),
        cost_estimate=pl.CostEstimate(
            flops=2 * rows * wide * depth * count,
            bytes_accessed=2 * wide * depth * count,
            transcendentals=0,
        ),
    )(shards_of, *([] if acc is None else [acc]), *xs, *([weight] * count))


def key_window(tok_rows, total):
    span = (total - total // 2) // ROLLOUTS
    reach = 3 * span + TILE + JITTER
    reach = reach // TILE * TILE
    return -(-reach // tok_rows)


def shards(
    upstream, advantage, out_weight, query_heads, key_heads, value_heads, segment_ids, tile_mask
):
    rows = query_heads.shape[0]
    n_ctx = lax.axis_size("ctx")
    n_tp = lax.axis_size("tp")
    total = rows * n_ctx
    prompt = total // 2
    groups = key_heads.shape[1] // HD
    me = lax.axis_index("ctx").astype(jnp.int32)
    z = lax.axis_index("tp").astype(jnp.int32)
    per = rows // KB
    back = key_window(rows, total)
    prompt_kb = prompt // KB
    n_kb = prompt_kb + (back + 1) * per
    fast = n_ctx == 8 and n_tp == 4 and per == 1 and back == 2
    own = jnp.concatenate([key_heads, value_heads], axis=1)

    def hop(value, pairs):
        return lax.ppermute(value, "tp", pairs)

    def flip(value, bit, pairs=None):
        return lax.ppermute(value, "ctx", pairs or [(i, i ^ bit) for i in range(n_ctx)])

    if fast:
        near = jnp.stack([own] + [flip(own, d) for d in (2, 4, 6)])
        far = flip(near, 1)
        up_b = hop(upstream, [(0, 2), (2, 0), (1, 3), (3, 1)])
        up_a = hop(upstream, [(0, 1), (1, 0), (2, 3), (3, 2)])
        up_c = hop(upstream, [(1, 2), (2, 1)])
        up_d = hop(up_b, [(1, 0), (2, 3)])
    else:
        near = lax.all_gather(own, "ctx", axis=0)
        near = far = near.reshape(n_ctx * per, KB, 2 * groups * HD)

    bias, live = mask_call(me, segment_ids, tile_mask, rows, n_kb, prompt, back)
    block = jnp.arange(n_kb, dtype=jnp.int32)
    holder = jnp.where(
        block < prompt_kb,
        block // per,
        jnp.where(me * rows >= prompt, me - back + (block - prompt_kb) // per, me),
    )
    if fast:
        away = holder ^ me
        slots = away // 2 + (away % 2) * 4
        core = me & 1
        pos = jnp.where(
            block < 4,
            jnp.where(block % 2 == core, 3 + block // 2, block // 2),
            jnp.array([0, 0, 0, 0, 5, 2, 6], jnp.int32),
        )
        n_send = 3
        x1, x2, shard = up_c, up_d, z ^ 3
        first = project_call(z[None], [upstream], out_weight)
        acc = project_call(jnp.stack([z ^ 1, z ^ 2]), [up_a, up_b], out_weight, first)
    else:
        slots = holder * per + block % per
        pos = block
        n_send = 0
        whole = lax.all_gather(upstream, "tp", axis=0)
        shard = z
        acc = jnp.zeros((rows, out_weight.shape[0]), F32)
        for i in range(n_tp - 1):
            other = (z + 1 + i) % n_tp
            x = lax.dynamic_index_in_dim(whole, other, 0, keepdims=False)
            acc = project_call(other[None], [x], out_weight, acc)
        x1, x2 = upstream, jnp.zeros_like(upstream)
    depth = upstream.shape[1]
    w_last = lax.dynamic_slice_in_dim(out_weight, shard * depth, depth, 1)

    probs, attn, inv, keys, values = probs_call(
        slots.astype(jnp.int32), query_heads, near, far, bias, groups, n_kb
    )
    outs = [
        back_call(
            g, live, pos.astype(jnp.int32), acc, x1, x2, w_last, advantage[:, None], attn, inv,
            query_heads, keys, values, probs, n_kb, n_send,
        )
        for g in range(groups)
    ]
    grad_queries = jnp.concatenate([dq for dq, _, _ in outs], axis=1)

    if fast:
        final = []
        shape = (2, KB, HD)
        for _, send, keep in outs:
            base, to_x, to_y, to_d = call(
                middle_kernel,
                (me[None], flip(send, 1), keep),
                [SMEM, VMEM, VMEM],
                [(shape, F32), (shape, BF16), (shape, BF16), (shape, BF16)],
            )
            by_y = flip(to_y, 4, [(4, 0), (5, 1), (6, 2), (7, 3)])
            by_d = flip(to_d, 6, [(4, 2), (5, 3), (6, 0), (7, 1)])
            by_x = flip(to_x, 2, [(0, 2), (2, 0), (1, 3), (3, 1), (6, 4), (7, 5)])
            final += [base, by_x, by_y, by_d]
        grad_keys, grad_values = call(
            functools.partial(last_kernel, groups),
            final,
            [VMEM] * len(final),
            [((rows, groups * HD), BF16)] * 2,
        )
        return grad_queries, grad_keys, grad_values

    win = (back + 1) * rows
    win_start = jnp.maximum(me - back, 0) * rows
    part = jnp.concatenate([keep for _, _, keep in outs], axis=3).astype(F32)
    part = part.transpose(0, 2, 1, 3).reshape(prompt + win, 2, groups * HD)
    full = jnp.zeros((total, 2, groups * HD), F32).at[:prompt].set(part[:prompt])
    old = lax.dynamic_slice_in_dim(full, win_start, win, 0)
    full = lax.dynamic_update_slice_in_dim(full, old + part[prompt:], win_start, 0)
    reduced = lax.psum_scatter(full, "ctx", scatter_dimension=0, tiled=True)
    return (
        grad_queries,
        (reduced[:, 0] * SCALE).astype(BF16),
        reduced[:, 1].astype(BF16),
    )


def solution(mesh):
    placed = (
        P("ctx", "tp"),
        P("ctx"),
        P("tp", None),
        P("ctx", "tp"),
        P("ctx", "tp"),
        P("ctx", "tp"),
        P(),
        P("ctx", None),
    )
    return jax.shard_map(
        shards,
        mesh=mesh,
        in_specs=placed,
        out_specs=(P("ctx", "tp"), P("ctx", "tp"), P("ctx", "tp")),
        check_vma=False,
    )
```

```python
import functools
import math

import jax
import jax.numpy as jnp
from jax import lax
from jax.experimental import pallas as pl
from jax.experimental.pallas import tpu as pltpu
from jax.sharding import PartitionSpec as P

HEADS = 64
KV_HEADS = 8
SHARE = HEADS // KV_HEADS
HD = 128
TILE = 128
ROLLOUTS = 8
JITTER = 64
KB = 256
VMEM_LIMIT = 20 << 20
SCALE = 1.0 / math.sqrt(HD)
LOG2E = 1.4426950408889634
F32 = jnp.float32
BF16 = jnp.bfloat16
NT = (((1,), (1,)), ((), ()))


def dot(a, b):
    return jnp.dot(a, b, preferred_element_type=F32)


def dot_nt(a, b):
    return lax.dot_general(a, b, NT, preferred_element_type=F32)


SMEM = pl.BlockSpec(memory_space=pltpu.SMEM)
VMEM = pl.BlockSpec(memory_space=pltpu.VMEM)


def at(start, size):
    return pl.ds(pl.multiple_of(start, size), size)


def call(kernel, ins, in_specs, outs, scratch=(), out_specs=None, flops=0, size=0, exps=0):
    return pl.pallas_call(
        kernel,
        in_specs=in_specs,
        out_specs=out_specs or [VMEM] * len(outs),
        out_shape=[
            out if isinstance(out, pl.MemoryRef) else jax.ShapeDtypeStruct(*out) for out in outs
        ],
        scratch_shapes=list(scratch),
        compiler_params=pltpu.CompilerParams(vmem_limit_bytes=VMEM_LIMIT),
        cost_estimate=pl.CostEstimate(flops=flops, bytes_accessed=size, transcendentals=exps),
    )(*ins)


def mask_kernel(n_kb, prompt, back, total, me_ref, seg_ref, tile_ref, bias_ref, live_ref):
    rows = bias_ref.shape[2]
    per = rows // KB
    me = me_ref[0]
    row_start = me * rows
    win_kb = jnp.maximum(me - back, 0) * per
    key_at = lax.broadcasted_iota(jnp.int32, (KB, KB), 0)
    query_at = lax.broadcasted_iota(jnp.int32, (KB, KB), 1)
    for kb in range(n_kb):
        window = kb >= prompt // KB
        block = win_kb + (kb - prompt // KB) if window else kb
        key_pos = block * KB + key_at
        seg_k = jnp.broadcast_to(seg_ref[block], (KB, KB)).T
        some = jnp.int32(0)
        for r in range(per):
            same = seg_k == jnp.broadcast_to(seg_ref[me * per + r], (KB, KB))
            for a in range(KB // TILE):
                for b in range(KB // TILE):
                    mark = tile_ref[r * (KB // TILE) + b, block * (KB // TILE) + a]
                    inside = (key_at // TILE == a) & (query_at // TILE == b)
                    same = same | (inside & (jnp.full((KB, KB), mark) == 1))
            seen = same & (key_pos <= row_start + r * KB + query_at)
            if window:
                seen = seen & (key_pos >= prompt) & (jnp.full((KB, KB), me) >= prompt // rows)
            bias_ref[kb, :, r * KB : (r + 1) * KB] = jnp.where(seen, 0.0, -1e30)
            some = jnp.maximum(some, jnp.max(seen.astype(jnp.int32)))
        live_ref[kb] = some


def mask_call(me, segment_ids, tile_mask, rows, n_kb, prompt, back):
    total = segment_ids.shape[0]
    return call(
        functools.partial(mask_kernel, n_kb, prompt, back, total),
        (me[None], segment_ids.reshape(total // KB, 1, KB), tile_mask),
        [SMEM, VMEM, SMEM],
        [((n_kb, KB, rows), F32), ((n_kb,), jnp.int32)],
        out_specs=[VMEM, SMEM],
        size=n_kb * KB * rows * 4,
    )


def probs_kernel(
    n_kb, group, groups, slot_ref, q_ref, near_ref, far_ref, bias_ref,
    p_ref, o_ref, inv_ref, k_ref, v_ref, kx_ref, vt_ref, s_ref, t_ref, a_ref, b_ref, sems,
):
    rows = q_ref.shape[0]
    per = rows // KB
    n_near = near_ref.shape[0]
    lane = lax.broadcasted_iota(jnp.int32, (KB, HD), 1)
    inv_ref[...] = jnp.zeros_like(inv_ref)
    vt_ref[HD:, :] = jnp.ones((16, n_kb * KB), BF16)
    for kb in range(n_kb):
        slot = slot_ref[kb]
        keys = pl.ds(kb * KB, KB)

        def place(source, index):
            k_ref[keys, :] = source[index, :, group * HD : (group + 1) * HD]
            v_ref[keys, :] = source[index, :, (groups + group) * HD : (groups + group + 1) * HD]

        @pl.when(slot < n_near)
        def _():
            place(near_ref, slot)

        @pl.when(slot >= n_near)
        def _():
            place(far_ref, slot - n_near)

    for kb in range(n_kb):
        keys = pl.ds(kb * KB, KB)
        k = k_ref[keys, :]
        kx_ref[keys, :HD] = k
        kx_ref[keys, HD:] = k
        vt_ref[:HD, keys] = v_ref[keys, :].T

    count = SHARE * per

    def places(i):
        h, r = i // per, i % per
        return h, at(r * KB, KB), at((h * per + r) * KB, KB)

    def score(i, s_ref):
        h, here, _ = places(i)
        q = q_ref[here, at((group * SHARE + h) * HD, HD)].astype(F32) * (SCALE * LOG2E)
        q_hi = q.astype(BF16)
        q_lo = (q - q_hi.astype(F32)).astype(BF16)
        qx = jnp.concatenate([q_hi, q_lo], axis=1)
        s = dot_nt(kx_ref[...], qx) + bias_ref[:, :, here].reshape(n_kb * KB, KB)
        s_ref[...] = s
        return jnp.max(s, axis=0, keepdims=True)

    def out(i, e_ref, sem):
        return pltpu.make_async_copy(e_ref, p_ref.at[:, places(i)[2]], sem)

    def soften(i, s_ref, top, e_ref, sem):
        h, here, cols = places(i)
        e = jnp.exp2(s_ref[...] - top).astype(BF16)

        @pl.when(i >= 2)
        def _():
            out(i - 2, e_ref, sem).wait()

        e_ref[...] = e
        out(i, e_ref, sem).start()
        acc = dot(vt_ref[...], e)
        inv = 1.0 / acc[HD : HD + 1, :]
        o_ref[here, at(h * HD, HD)] = (acc[:HD] * inv).T
        inv_ref[here, :] += jnp.where(lane == h, jnp.broadcast_to(inv, (HD, KB)).T, 0.0)

    def step(j, top):
        later = score(2 * j + 1, t_ref)
        soften(2 * j, s_ref, top, a_ref, sems.at[0])
        top = score(jnp.minimum(2 * j + 2, count - 1), s_ref)
        soften(2 * j + 1, t_ref, later, b_ref, sems.at[1])
        return top

    lax.fori_loop(0, count // 2, step, score(0, s_ref))
    out(count - 2, a_ref, sems.at[0]).wait()
    out(count - 1, b_ref, sems.at[1]).wait()


def probs_call(group, groups, slots, q, near, far, bias, n_kb):
    rows = q.shape[0]
    keys = n_kb * KB
    return call(
        functools.partial(probs_kernel, n_kb, group, groups),
        (slots, q, near, far, bias),
        [SMEM, VMEM, VMEM, VMEM, VMEM],
        [
            pltpu.HBM((keys, SHARE * rows), BF16),
            ((rows, SHARE * HD), F32),
            ((rows, HD), F32),
            ((keys, HD), BF16),
            ((keys, HD), BF16),
        ],
        scratch=[
            pltpu.VMEM((keys, 2 * HD), BF16),
            pltpu.VMEM((HD + 16, keys), BF16),
            pltpu.VMEM((keys, KB), F32),
            pltpu.VMEM((keys, KB), F32),
            pltpu.VMEM((keys, KB), BF16),
            pltpu.VMEM((keys, KB), BF16),
            pltpu.SemaphoreType.DMA((2,)),
        ],
        out_specs=[pl.BlockSpec(memory_space=pltpu.HBM)] + [VMEM] * 4,
        flops=6 * SHARE * rows * keys * HD,
        size=SHARE * rows * keys * 2,
        exps=SHARE * rows * keys,
    )


def back_kernel(
    n_kb, n_send, first, live_ref, pos_ref, proj_ref, x1_ref, x2_ref, w_ref, adv_ref, o_ref,
    inv_ref, q_ref, k_ref, v_ref, p_ref,
    dq_ref, send_ref, keep_ref, dox_ref, qs_ref, ds_ref, dqt_ref,
):
    rows = proj_ref.shape[0]
    lane = lax.broadcasted_iota(jnp.int32, (rows, HD), 1)
    minus = jnp.where(lax.broadcasted_iota(jnp.int32, (KB, HD), 1) < 3, -1.0, 0.0).astype(BF16)
    x = x1_ref[...] + x2_ref[...]
    dqt_ref[...] = jnp.zeros_like(dqt_ref)
    for h in range(SHARE):
        head = first + h
        cols = pl.ds(head * HD, HD)
        here = pl.ds(h * rows, rows)
        inv = inv_ref[:, h : h + 1]
        proj = proj_ref[:, cols] + dot_nt(x, w_ref[cols, :])
        grad = (proj * (adv_ref[...] * inv)).astype(BF16)
        delta = jnp.sum(grad.astype(F32) * o_ref[:, h * HD : (h + 1) * HD], axis=1, keepdims=True)
        one = delta.astype(BF16).astype(F32)
        two = (delta - one).astype(BF16).astype(F32)
        three = delta - one - two
        ext = jnp.where(
            lane == 0, one, jnp.where(lane == 1, two, jnp.where(lane == 2, three, 0.0))
        )
        dox_ref[here, :HD] = grad
        dox_ref[here, HD:] = ext.astype(BF16)
        qs_ref[here, :] = q_ref[:, cols]

    def step(kb, carry):
        pos = pos_ref[kb]

        def put(value):
            @pl.when(pos < n_send)
            def _():
                send_ref[pos] = value

            @pl.when(pos >= n_send)
            def _():
                keep_ref[pos - n_send] = value

        @pl.when(live_ref[kb] != 0)
        def _():
            keys = at(kb * KB, KB)
            vx = jnp.concatenate([v_ref[keys, :], minus], axis=1)
            kt = k_ref[keys, :].T
            dv = dot(p_ref[keys, :], dox_ref[:, :HD])
            for h in range(SHARE * rows // KB):
                here = pl.ds(h * KB, KB)
                dp = dot_nt(vx, dox_ref[here, :])
                ds_ref[:, here] = (p_ref[keys, here].astype(F32) * dp).astype(BF16)
            dqt_ref[...] += dot(kt, ds_ref[...])
            dk = dot(ds_ref[...], qs_ref[...])
            put(jnp.stack([dk, dv]).astype(BF16))

        @pl.when(live_ref[kb] == 0)
        def _():
            put(jnp.zeros((2, KB, HD), BF16))

        return carry

    lax.fori_loop(0, n_kb, step, 0)
    for h in range(SHARE):
        dq_ref[:, pl.ds(h * HD, HD)] = (
            (dqt_ref[:, h * rows : (h + 1) * rows] * SCALE).T.astype(BF16)
        )


def back_call(group, live, pos, proj, x1, x2, w, adv, o, inv, q, k, v, p, n_kb, n_send):
    rows = q.shape[0]
    wide = SHARE * HD
    return call(
        functools.partial(back_kernel, n_kb, n_send, group * SHARE),
        (live, pos, proj, x1, x2, w, adv, o, inv, q, k, v, p),
        [SMEM, SMEM] + [VMEM] * 11,
        [
            ((rows, wide), BF16),
            ((max(n_send, 1), 2, KB, HD), BF16),
            ((n_kb - n_send, 2, KB, HD), BF16),
        ],
        scratch=[
            pltpu.VMEM((SHARE * rows, 2 * HD), BF16),
            pltpu.VMEM((SHARE * rows, HD), BF16),
            pltpu.VMEM((KB, SHARE * rows), BF16),
            pltpu.VMEM((HD, SHARE * rows), F32),
        ],
        flops=10 * SHARE * rows * n_kb * KB * HD,
        size=SHARE * rows * n_kb * KB * 2,
    )


def middle_kernel(me_ref, got_ref, keep_ref, base_ref, x_ref, y_ref, d_ref):
    me = me_ref[0]
    core, side, roll = me & 1, (me >> 1) & 1, me >= 4
    here = keep_ref[side].astype(F32) + got_ref[side].astype(F32)
    there = keep_ref[1 - side].astype(F32) + got_ref[1 - side].astype(F32)
    y_ref[...] = here.astype(BF16)
    d_ref[...] = there.astype(BF16)
    got = got_ref[2].astype(F32)
    late = (jnp.full(got.shape, core) == 1)

    @pl.when(roll)
    def _():
        x_ref[...] = (keep_ref[2].astype(F32) + jnp.where(late, got, 0.0)).astype(BF16)
        base_ref[...] = keep_ref[3].astype(F32) + jnp.where(late, 0.0, got)

    @pl.when(jnp.logical_not(roll))
    def _():
        x_ref[...] = there.astype(BF16)
        base_ref[...] = here


def last_kernel(groups, *refs):
    dk_ref, dv_ref = refs[-2:]
    for g in range(groups):
        base, x, y, d = refs[4 * g : 4 * g + 4]
        total = base[...] + x[...].astype(F32) + y[...].astype(F32) + d[...].astype(F32)
        dk_ref[:, g * HD : (g + 1) * HD] = (total[0] * SCALE).astype(BF16)
        dv_ref[:, g * HD : (g + 1) * HD] = total[1].astype(BF16)


def project_kernel(shard_ref, *refs):
    out_ref = refs[-1]
    pairs = (len(refs) - 1) // 2
    acc = dot_nt(refs[0][...], refs[pairs][...])
    for i in range(1, pairs):
        acc += dot_nt(refs[i][...], refs[pairs + i][...])
    out_ref[...] = acc


def project_add_kernel(shard_ref, acc_ref, *refs):
    project_kernel(shard_ref, *refs)
    refs[-1][...] += acc_ref[...]


def project_call(shards_of, xs, weight, acc=None):
    rows, depth = xs[0].shape
    wide = weight.shape[0]
    block = 512
    count = len(xs)
    tile = pl.BlockSpec((rows, block), lambda n, s: (0, n))
    return pl.pallas_call(
        project_kernel if acc is None else project_add_kernel,
        grid_spec=pltpu.PrefetchScalarGridSpec(
            num_scalar_prefetch=1,
            grid=(wide // block,),
            in_specs=([] if acc is None else [tile])
            + [pl.BlockSpec((rows, depth), lambda n, s: (0, 0))] * count
            + [pl.BlockSpec((block, depth), lambda n, s, i=i: (n, s[i])) for i in range(count)],
            out_specs=tile,
        ),
        out_shape=jax.ShapeDtypeStruct((rows, wide), F32),
        compiler_params=pltpu.CompilerParams(vmem_limit_bytes=VMEM_LIMIT),
        cost_estimate=pl.CostEstimate(
            flops=2 * rows * wide * depth * count,
            bytes_accessed=2 * wide * depth * count,
            transcendentals=0,
        ),
    )(shards_of, *([] if acc is None else [acc]), *xs, *([weight] * count))


def key_window(tok_rows, total):
    span = (total - total // 2) // ROLLOUTS
    reach = 3 * span + TILE + JITTER
    reach = reach // TILE * TILE
    return -(-reach // tok_rows)


def shards(
    upstream, advantage, out_weight, query_heads, key_heads, value_heads, segment_ids, tile_mask
):
    rows = query_heads.shape[0]
    n_ctx = lax.axis_size("ctx")
    n_tp = lax.axis_size("tp")
    total = rows * n_ctx
    prompt = total // 2
    groups = key_heads.shape[1] // HD
    me = lax.axis_index("ctx").astype(jnp.int32)
    z = lax.axis_index("tp").astype(jnp.int32)
    per = rows // KB
    back = key_window(rows, total)
    prompt_kb = prompt // KB
    n_kb = prompt_kb + (back + 1) * per
    fast = n_ctx == 8 and n_tp == 4 and per == 1 and back == 2
    own = jnp.concatenate([key_heads, value_heads], axis=1)
    weight = pltpu.with_memory_space_constraint(out_weight, pltpu.HBM)

    def hop(value, pairs):
        return lax.ppermute(value, "tp", pairs)

    def flip(value, bit, pairs=None):
        return lax.ppermute(value, "ctx", pairs or [(i, i ^ bit) for i in range(n_ctx)])

    if fast:
        near = jnp.stack([own] + [flip(own, d) for d in (2, 4, 6)])
        far = flip(near, 1)
        up_b = hop(upstream, [(0, 2), (2, 0), (1, 3), (3, 1)])
        up_a = hop(upstream, [(0, 1), (1, 0), (2, 3), (3, 2)])
    else:
        near = lax.all_gather(own, "ctx", axis=0)
        near = far = near.reshape(n_ctx * per, KB, 2 * groups * HD)

    bias, live = mask_call(me, segment_ids, tile_mask, rows, n_kb, prompt, back)
    block = jnp.arange(n_kb, dtype=jnp.int32)
    holder = jnp.where(
        block < prompt_kb,
        block // per,
        jnp.where(me * rows >= prompt, me - back + (block - prompt_kb) // per, me),
    )
    if fast:
        away = holder ^ me
        slots = away // 2 + (away % 2) * 4
        core = me & 1
        pos = jnp.where(
            block < 4,
            jnp.where(block % 2 == core, 3 + block // 2, block // 2),
            jnp.array([0, 0, 0, 0, 5, 2, 6], jnp.int32),
        )
        n_send = 3
        shard = z ^ 3
        acc = project_call(z[None], [upstream], weight)
    else:
        slots = holder * per + block % per
        pos = block
        n_send = 0
        whole = lax.all_gather(upstream, "tp", axis=0)
        shard = z
        acc = jnp.zeros((rows, out_weight.shape[0]), F32)
        for i in range(n_tp - 1):
            other = (z + 1 + i) % n_tp
            x = lax.dynamic_index_in_dim(whole, other, 0, keepdims=False)
            acc = project_call(other[None], [x], weight, acc)
        x1, x2 = upstream, jnp.zeros_like(upstream)
    depth = upstream.shape[1]
    w_last = lax.dynamic_slice_in_dim(out_weight, shard * depth, depth, 1)

    slots = slots.astype(jnp.int32)
    soft = [list(probs_call(0, groups, slots, query_heads, near, far, bias, n_kb))]
    if fast:
        up_b, later, head = lax.optimization_barrier((up_b, upstream, soft[0][2]))
        soft[0][2] = head
        up_c = hop(later, [(1, 2), (2, 1)])
        up_d = hop(up_b, [(1, 0), (2, 3)])
        x1, x2 = up_c, up_d
    soft += [
        list(probs_call(g, groups, slots, query_heads, near, far, bias, n_kb))
        for g in range(1, groups)
    ]
    if fast:
        acc, soft[-1][2] = lax.optimization_barrier((acc, soft[-1][2]))
        acc = project_call(jnp.stack([z ^ 1, z ^ 2]), [up_a, up_b], weight, acc)
    outs = []
    for g in range(groups):
        probs, attn, inv, keys, values = soft[g]
        outs.append(
            back_call(
                g, live, pos.astype(jnp.int32), acc, x1, x2, w_last, advantage[:, None], attn,
                inv, query_heads, keys, values, probs, n_kb, n_send,
            )
        )
    grad_queries = jnp.concatenate([dq for dq, _, _ in outs], axis=1)

    if fast:
        final = []
        shape = (2, KB, HD)
        for _, send, keep in outs:
            base, to_x, to_y, to_d = call(
                middle_kernel,
                (me[None], flip(send, 1), keep),
                [SMEM, VMEM, VMEM],
                [(shape, F32), (shape, BF16), (shape, BF16), (shape, BF16)],
            )
            by_y = flip(to_y, 4, [(4, 0), (5, 1), (6, 2), (7, 3)])
            by_d = flip(to_d, 6, [(4, 2), (5, 3), (6, 0), (7, 1)])
            by_x = flip(to_x, 2, [(0, 2), (2, 0), (1, 3), (3, 1), (6, 4), (7, 5)])
            final += [base, by_x, by_y, by_d]
        grad_keys, grad_values = call(
            functools.partial(last_kernel, groups),
            final,
            [VMEM] * len(final),
            [((rows, groups * HD), BF16)] * 2,
        )
        return grad_queries, grad_keys, grad_values

    win = (back + 1) * rows
    win_start = jnp.maximum(me - back, 0) * rows
    part = jnp.concatenate([keep for _, _, keep in outs], axis=3).astype(F32)
    part = part.transpose(0, 2, 1, 3).reshape(prompt + win, 2, groups * HD)
    full = jnp.zeros((total, 2, groups * HD), F32).at[:prompt].set(part[:prompt])
    old = lax.dynamic_slice_in_dim(full, win_start, win, 0)
    full = lax.dynamic_update_slice_in_dim(full, old + part[prompt:], win_start, 0)
    reduced = lax.psum_scatter(full, "ctx", scatter_dimension=0, tiled=True)
    return (
        grad_queries,
        (reduced[:, 0] * SCALE).astype(BF16),
        reduced[:, 1].astype(BF16),
    )


def solution(mesh):
    placed = (
        P("ctx", "tp"),
        P("ctx"),
        P("tp", None),
        P("ctx", "tp"),
        P("ctx", "tp"),
        P("ctx", "tp"),
        P(),
        P("ctx", None),
    )
    return jax.shard_map(
        shards,
        mesh=mesh,
        in_specs=placed,
        out_specs=(P("ctx", "tp"), P("ctx", "tp"), P("ctx", "tp")),
        check_vma=False,
    )
```

```python
import functools
import math

import jax
import jax.numpy as jnp
from jax import lax
from jax.experimental import pallas as pl
from jax.experimental.pallas import tpu as pltpu
from jax.sharding import PartitionSpec as P

HEADS = 64
KV_HEADS = 8
SHARE = HEADS // KV_HEADS
HD = 128
TILE = 128
ROLLOUTS = 8
JITTER = 64
KB = 256
VMEM_LIMIT = 26 << 20
SCALE = 1.0 / math.sqrt(HD)
LOG2E = 1.4426950408889634
F32 = jnp.float32
BF16 = jnp.bfloat16
NT = (((1,), (1,)), ((), ()))


def dot(a, b):
    return jnp.dot(a, b, preferred_element_type=F32)


def dot_nt(a, b):
    return lax.dot_general(a, b, NT, preferred_element_type=F32)


SMEM = pl.BlockSpec(memory_space=pltpu.SMEM)
VMEM = pl.BlockSpec(memory_space=pltpu.VMEM)


def at(start, size):
    return pl.ds(pl.multiple_of(start, size), size)


def call(kernel, ins, in_specs, outs, scratch=(), out_specs=None, flops=0, size=0, exps=0):
    return pl.pallas_call(
        kernel,
        in_specs=in_specs,
        out_specs=out_specs or [VMEM] * len(outs),
        out_shape=[
            out if isinstance(out, pl.MemoryRef) else jax.ShapeDtypeStruct(*out) for out in outs
        ],
        scratch_shapes=list(scratch),
        compiler_params=pltpu.CompilerParams(vmem_limit_bytes=VMEM_LIMIT),
        cost_estimate=pl.CostEstimate(flops=flops, bytes_accessed=size, transcendentals=exps),
    )(*ins)


def mask_kernel(n_kb, prompt, back, total, me_ref, seg_ref, tile_ref, bias_ref, live_ref):
    rows = bias_ref.shape[2]
    per = rows // KB
    me = me_ref[0]
    row_start = me * rows
    win_kb = jnp.maximum(me - back, 0) * per
    key_at = lax.broadcasted_iota(jnp.int32, (KB, KB), 0)
    query_at = lax.broadcasted_iota(jnp.int32, (KB, KB), 1)
    for kb in range(n_kb):
        window = kb >= prompt // KB
        block = win_kb + (kb - prompt // KB) if window else kb
        key_pos = block * KB + key_at
        seg_k = jnp.broadcast_to(seg_ref[block], (KB, KB)).T
        some = jnp.int32(0)
        for r in range(per):
            same = seg_k == jnp.broadcast_to(seg_ref[me * per + r], (KB, KB))
            for a in range(KB // TILE):
                for b in range(KB // TILE):
                    mark = tile_ref[r * (KB // TILE) + b, block * (KB // TILE) + a]
                    inside = (key_at // TILE == a) & (query_at // TILE == b)
                    same = same | (inside & (jnp.full((KB, KB), mark) == 1))
            seen = same & (key_pos <= row_start + r * KB + query_at)
            if window:
                seen = seen & (key_pos >= prompt) & (jnp.full((KB, KB), me) >= prompt // rows)
            bias_ref[kb, :, r * KB : (r + 1) * KB] = jnp.where(seen, 0.0, -1e30)
            some = jnp.maximum(some, jnp.max(seen.astype(jnp.int32)))
        live_ref[kb] = some


def mask_call(me, segment_ids, tile_mask, rows, n_kb, prompt, back):
    total = segment_ids.shape[0]
    return call(
        functools.partial(mask_kernel, n_kb, prompt, back, total),
        (me[None], segment_ids.reshape(total // KB, 1, KB), tile_mask),
        [SMEM, VMEM, SMEM],
        [((n_kb, KB, rows), F32), ((n_kb,), jnp.int32)],
        out_specs=[VMEM, SMEM],
        size=n_kb * KB * rows * 4,
    )


def probs_kernel(
    n_kb, group, groups, slot_ref, q_ref, near_ref, far_ref, bias_ref,
    p_ref, o_ref, k_ref, v_ref,
    ks_ref, vs_ref, kx_ref, vt_ref, s_ref, t_ref, pa_ref, pb_ref, oa_ref, ob_ref, sems,
):
    rows = q_ref.shape[0]
    per = rows // KB
    n_near = near_ref.shape[0]
    vt_ref[HD:, :] = jnp.ones((16, n_kb * KB), BF16)
    for kb in range(n_kb):
        slot = slot_ref[kb]
        keys = pl.ds(kb * KB, KB)

        def place(source, index):
            ks_ref[keys, :] = source[index, :, group * HD : (group + 1) * HD]
            vs_ref[keys, :] = source[index, :, (groups + group) * HD : (groups + group + 1) * HD]

        @pl.when(slot < n_near)
        def _():
            place(near_ref, slot)

        @pl.when(slot >= n_near)
        def _():
            place(far_ref, slot - n_near)

    keep_k = pltpu.make_async_copy(ks_ref, k_ref, sems.at[4])
    keep_v = pltpu.make_async_copy(vs_ref, v_ref, sems.at[5])
    keep_k.start()
    keep_v.start()
    for kb in range(n_kb):
        keys = pl.ds(kb * KB, KB)
        k = ks_ref[keys, :]
        kx_ref[keys, :HD] = k
        kx_ref[keys, HD:] = k
        vt_ref[:HD, keys] = vs_ref[keys, :].T

    count = SHARE * per

    def score(i, s_ref):
        h, here = i // per, at((i % per) * KB, KB)
        q = q_ref[here, at((group * SHARE + h) * HD, HD)].astype(F32) * (SCALE * LOG2E)
        q_hi = q.astype(BF16)
        q_lo = (q - q_hi.astype(F32)).astype(BF16)
        qx = jnp.concatenate([q_hi, q_lo], axis=1)
        s = dot_nt(kx_ref[...], qx) + bias_ref[:, :, here].reshape(n_kb * KB, KB)
        s_ref[...] = s
        return jnp.max(s, axis=0, keepdims=True)

    def out(i, side):
        p_side, o_side = ((pa_ref, oa_ref), (pb_ref, ob_ref))[side]
        return (
            pltpu.make_async_copy(p_side, p_ref.at[i], sems.at[side]),
            pltpu.make_async_copy(o_side, o_ref.at[i], sems.at[2 + side]),
        )

    def soften(i, s_ref, top, side):
        p_side, o_side = ((pa_ref, oa_ref), (pb_ref, ob_ref))[side]
        e = jnp.exp2(s_ref[...] - top).astype(BF16)

        @pl.when(i >= 2)
        def _():
            for copy in out(i - 2, side):
                copy.wait()

        p_side[...] = e
        acc = dot(vt_ref[...], e)
        inv = 1.0 / acc[HD : HD + 1, :]
        o_side[:, :HD] = (acc[:HD] * inv).T
        o_side[:, HD:] = jnp.broadcast_to(inv, (HD, KB)).T
        for copy in out(i, side):
            copy.start()

    def step(j, top):
        later = score(2 * j + 1, t_ref)
        soften(2 * j, s_ref, top, 0)
        top = score(jnp.minimum(2 * j + 2, count - 1), s_ref)
        soften(2 * j + 1, t_ref, later, 1)
        return top

    lax.fori_loop(0, count // 2, step, score(0, s_ref))
    for side in range(2):
        for copy in out(count - 2 + side, side):
            copy.wait()
    keep_k.wait()
    keep_v.wait()


HBM = pl.BlockSpec(memory_space=pltpu.HBM)


def probs_call(group, groups, slots, q, near, far, bias, n_kb):
    rows = q.shape[0]
    keys = n_kb * KB
    blocks = SHARE * rows // KB
    return call(
        functools.partial(probs_kernel, n_kb, group, groups),
        (slots, q, near, far, bias),
        [SMEM, VMEM, VMEM, VMEM, VMEM],
        [
            pltpu.HBM((blocks, keys, KB), BF16),
            pltpu.HBM((blocks, KB, 2 * HD), F32),
            pltpu.HBM((keys, HD), BF16),
            pltpu.HBM((keys, HD), BF16),
        ],
        scratch=[
            pltpu.VMEM((keys, HD), BF16),
            pltpu.VMEM((keys, HD), BF16),
            pltpu.VMEM((keys, 2 * HD), BF16),
            pltpu.VMEM((HD + 16, keys), BF16),
            pltpu.VMEM((keys, KB), F32),
            pltpu.VMEM((keys, KB), F32),
            pltpu.VMEM((keys, KB), BF16),
            pltpu.VMEM((keys, KB), BF16),
            pltpu.VMEM((KB, 2 * HD), F32),
            pltpu.VMEM((KB, 2 * HD), F32),
            pltpu.SemaphoreType.DMA((6,)),
        ],
        out_specs=[HBM] * 4,
    )


def back_kernel(
    n_kb, n_send, first, live_ref, pos_ref, proj_ref, x1_ref, x2_ref, w_ref, adv_ref, o_ref,
    q_ref, k_ref, v_ref, p_ref,
    dq_ref, send_ref, keep_ref, dox_ref, qs_ref, ds_ref, dqt_ref,
):
    rows = proj_ref.shape[0]
    per = rows // KB
    lane = lax.broadcasted_iota(jnp.int32, (KB, HD), 1)
    minus = jnp.where(lane < 3, -1.0, 0.0).astype(BF16)
    x = x1_ref[...] + x2_ref[...]
    dqt_ref[...] = jnp.zeros_like(dqt_ref)
    for h in range(SHARE):
        cols = pl.ds((first + h) * HD, HD)
        fresh = dot_nt(x, w_ref[cols, :])
        for r in range(per):
            part = slice(r * KB, (r + 1) * KB)
            here = pl.ds((h * per + r) * KB, KB)
            out = o_ref[h * per + r]
            proj = proj_ref[part, cols] + fresh[part]
            grad = (proj * (adv_ref[part, :] * out[:, HD:])).astype(BF16)
            delta = jnp.sum(grad.astype(F32) * out[:, :HD], axis=1, keepdims=True)
            one = delta.astype(BF16).astype(F32)
            two = (delta - one).astype(BF16).astype(F32)
            three = delta - one - two
            ext = jnp.where(
                lane == 0, one, jnp.where(lane == 1, two, jnp.where(lane == 2, three, 0.0))
            )
            dox_ref[here, :HD] = grad
            dox_ref[here, HD:] = ext.astype(BF16)
            qs_ref[here, :] = q_ref[part, cols]

    def step(kb, carry):
        pos = pos_ref[kb]

        def put(value):
            @pl.when(pos < n_send)
            def _():
                send_ref[pos] = value

            @pl.when(pos >= n_send)
            def _():
                keep_ref[pos - n_send] = value

        @pl.when(live_ref[kb] != 0)
        def _():
            keys = at(kb * KB, KB)
            vx = jnp.concatenate([v_ref[keys, :], minus], axis=1)
            kt = k_ref[keys, :].T
            p = jnp.concatenate([p_ref[i, keys, :] for i in range(SHARE * per)], axis=1)
            dv = dot(p, dox_ref[:, :HD])
            for i in range(SHARE * per):
                here = pl.ds(i * KB, KB)
                dp = dot_nt(vx, dox_ref[here, :])
                ds_ref[:, here] = (p_ref[i, keys, :].astype(F32) * dp).astype(BF16)
            dqt_ref[...] += dot(kt, ds_ref[...])
            dk = dot(ds_ref[...], qs_ref[...])
            put(jnp.stack([dk, dv]).astype(BF16))

        @pl.when(live_ref[kb] == 0)
        def _():
            put(jnp.zeros((2, KB, HD), BF16))

        return carry

    lax.fori_loop(0, n_kb, step, 0)
    for h in range(SHARE):
        dq_ref[:, pl.ds(h * HD, HD)] = (
            (dqt_ref[:, h * rows : (h + 1) * rows] * SCALE).T.astype(BF16)
        )


def back_call(group, live, pos, proj, x1, x2, w, adv, o, q, k, v, p, n_kb, n_send):
    rows = q.shape[0]
    return call(
        functools.partial(back_kernel, n_kb, n_send, group * SHARE),
        (live, pos, proj, x1, x2, w, adv, o, q, k, v, p),
        [SMEM, SMEM] + [VMEM] * 10,
        [
            ((rows, SHARE * HD), BF16),
            ((max(n_send, 1), 2, KB, HD), BF16),
            ((n_kb - n_send, 2, KB, HD), BF16),
        ],
        scratch=[
            pltpu.VMEM((SHARE * rows, 2 * HD), BF16),
            pltpu.VMEM((SHARE * rows, HD), BF16),
            pltpu.VMEM((KB, SHARE * rows), BF16),
            pltpu.VMEM((HD, SHARE * rows), F32),
        ],
    )


def middle_kernel(me_ref, got_ref, keep_ref, base_ref, x_ref, y_ref, d_ref):
    me = me_ref[0]
    core, side, roll = me & 1, (me >> 1) & 1, me >= 4
    here = keep_ref[side].astype(F32) + got_ref[side].astype(F32)
    there = keep_ref[1 - side].astype(F32) + got_ref[1 - side].astype(F32)
    y_ref[...] = here.astype(BF16)
    d_ref[...] = there.astype(BF16)
    got = got_ref[2].astype(F32)
    late = (jnp.full(got.shape, core) == 1)

    @pl.when(roll)
    def _():
        x_ref[...] = (keep_ref[2].astype(F32) + jnp.where(late, got, 0.0)).astype(BF16)
        base_ref[...] = keep_ref[3].astype(F32) + jnp.where(late, 0.0, got)

    @pl.when(jnp.logical_not(roll))
    def _():
        x_ref[...] = there.astype(BF16)
        base_ref[...] = here


def last_kernel(groups, *refs):
    dk_ref, dv_ref = refs[-2:]
    for g in range(groups):
        base, x, y, d = refs[4 * g : 4 * g + 4]
        total = base[...] + x[...].astype(F32) + y[...].astype(F32) + d[...].astype(F32)
        dk_ref[:, g * HD : (g + 1) * HD] = (total[0] * SCALE).astype(BF16)
        dv_ref[:, g * HD : (g + 1) * HD] = total[1].astype(BF16)


def project_kernel(shard_ref, *refs):
    out_ref = refs[-1]
    pairs = (len(refs) - 1) // 2
    acc = dot_nt(refs[0][...], refs[pairs][...])
    for i in range(1, pairs):
        acc += dot_nt(refs[i][...], refs[pairs + i][...])
    out_ref[...] = acc


def project_add_kernel(shard_ref, acc_ref, *refs):
    project_kernel(shard_ref, *refs)
    refs[-1][...] += acc_ref[...]


def project_call(shards_of, xs, weight, acc=None):
    rows, depth = xs[0].shape
    wide = weight.shape[0]
    block = 512
    count = len(xs)
    tile = pl.BlockSpec((rows, block), lambda n, s: (0, n))
    return pl.pallas_call(
        project_kernel if acc is None else project_add_kernel,
        grid_spec=pltpu.PrefetchScalarGridSpec(
            num_scalar_prefetch=1,
            grid=(wide // block,),
            in_specs=([] if acc is None else [tile])
            + [pl.BlockSpec((rows, depth), lambda n, s: (0, 0))] * count
            + [pl.BlockSpec((block, depth), lambda n, s, i=i: (n, s[i])) for i in range(count)],
            out_specs=tile,
        ),
        out_shape=jax.ShapeDtypeStruct((rows, wide), F32),
        compiler_params=pltpu.CompilerParams(vmem_limit_bytes=VMEM_LIMIT),
        cost_estimate=pl.CostEstimate(
            flops=2 * rows * wide * depth * count,
            bytes_accessed=2 * wide * depth * count,
            transcendentals=0,
        ),
    )(shards_of, *([] if acc is None else [acc]), *xs, *([weight] * count))


def key_window(tok_rows, total):
    span = (total - total // 2) // ROLLOUTS
    reach = 3 * span + TILE + JITTER
    reach = reach // TILE * TILE
    return -(-reach // tok_rows)


def shards(
    upstream, advantage, out_weight, query_heads, key_heads, value_heads, segment_ids, tile_mask
):
    rows = query_heads.shape[0]
    n_ctx = lax.axis_size("ctx")
    n_tp = lax.axis_size("tp")
    total = rows * n_ctx
    prompt = total // 2
    groups = key_heads.shape[1] // HD
    me = lax.axis_index("ctx").astype(jnp.int32)
    z = lax.axis_index("tp").astype(jnp.int32)
    per = rows // KB
    back = key_window(rows, total)
    prompt_kb = prompt // KB
    n_kb = prompt_kb + (back + 1) * per
    fast = n_ctx == 8 and n_tp == 4 and per == 1 and back == 2
    own = jnp.concatenate([key_heads, value_heads], axis=1)
    weight = pltpu.with_memory_space_constraint(out_weight, pltpu.HBM)

    def hop(value, pairs):
        return lax.ppermute(value, "tp", pairs)

    def flip(value, bit, pairs=None):
        return lax.ppermute(value, "ctx", pairs or [(i, i ^ bit) for i in range(n_ctx)])

    if fast:
        near = jnp.stack([own] + [flip(own, d) for d in (2, 4, 6)])
        ends, middle, out = [(0, 1), (1, 0), (2, 3), (3, 2)], [(1, 2), (2, 1)], [(1, 0), (2, 3)]
        up_a = hop(upstream, ends)
        up_c = hop(upstream, middle)
    else:
        near = lax.all_gather(own, "ctx", axis=0)
        near = far = near.reshape(n_ctx * per, KB, 2 * groups * HD)

    bias, live = mask_call(me, segment_ids, tile_mask, rows, n_kb, prompt, back)
    block = jnp.arange(n_kb, dtype=jnp.int32)
    holder = jnp.where(
        block < prompt_kb,
        block // per,
        jnp.where(me * rows >= prompt, me - back + (block - prompt_kb) // per, me),
    )
    if fast:
        away = holder ^ me
        slots = away // 2 + (away % 2) * 4
        core = me & 1
        pos = jnp.where(
            block < 4,
            jnp.where(block % 2 == core, 3 + block // 2, block // 2),
            jnp.array([0, 0, 0, 0, 5, 2, 6], jnp.int32),
        )
        n_send = 3
        half = z // 2
        second, shard = 2 - half, 3 - 3 * half
        acc = project_call(z[None], [upstream], weight)
    else:
        slots = holder * per + block % per
        pos = block
        n_send = 0
        whole = lax.all_gather(upstream, "tp", axis=0)
        shard = z
        acc = jnp.zeros((rows, out_weight.shape[0]), F32)
        for i in range(n_tp - 1):
            other = (z + 1 + i) % n_tp
            x = lax.dynamic_index_in_dim(whole, other, 0, keepdims=False)
            acc = project_call(other[None], [x], weight, acc)
        x1, x2 = upstream, jnp.zeros_like(upstream)
    depth = upstream.shape[1]
    w_last = lax.dynamic_slice_in_dim(out_weight, shard * depth, depth, 1)

    slots = slots.astype(jnp.int32)
    if fast:
        near, bias, w_last, acc, up_a, up_c = lax.optimization_barrier(
            (near, bias, w_last, acc, up_a, up_c)
        )
        far = flip(near, 1)
        up_e = hop(up_a, middle)
        up_f = hop(up_c, out)
    soft = [list(probs_call(0, groups, slots, query_heads, near, far, bias, n_kb))]
    if fast:
        up_e, soft[0][2] = lax.optimization_barrier((up_e, soft[0][2]))
        up_d = hop(up_e, out)
        x1, x2 = up_d, up_e
    soft += [
        list(probs_call(g, groups, slots, query_heads, near, far, bias, n_kb))
        for g in range(1, groups)
    ]
    if fast:
        acc, soft[-1][2] = lax.optimization_barrier((acc, soft[-1][2]))
        acc = project_call(jnp.stack([z ^ 1, second]), [up_a, up_c + up_f], weight, acc)
    outs = []
    for g in range(groups):
        probs, attn, keys, values = soft[g]
        outs.append(
            back_call(
                g, live, pos.astype(jnp.int32), acc, x1, x2, w_last, advantage[:, None], attn,
                query_heads, keys, values, probs, n_kb, n_send,
            )
        )
    grad_queries = jnp.concatenate([dq for dq, _, _ in outs], axis=1)

    if fast:
        final = []
        shape = (2, KB, HD)
        for _, send, keep in outs:
            base, to_x, to_y, to_d = call(
                middle_kernel,
                (me[None], flip(send, 1), keep),
                [SMEM, VMEM, VMEM],
                [(shape, F32), (shape, BF16), (shape, BF16), (shape, BF16)],
            )
            by_y = flip(to_y, 4, [(4, 0), (5, 1), (6, 2), (7, 3)])
            by_d = flip(to_d, 6, [(4, 2), (5, 3), (6, 0), (7, 1)])
            by_x = flip(to_x, 2, [(0, 2), (2, 0), (1, 3), (3, 1), (6, 4), (7, 5)])
            final += [base, by_x, by_y, by_d]
        grad_keys, grad_values = call(
            functools.partial(last_kernel, groups),
            final,
            [VMEM] * len(final),
            [((rows, groups * HD), BF16)] * 2,
        )
        return grad_queries, grad_keys, grad_values

    win = (back + 1) * rows
    win_start = jnp.maximum(me - back, 0) * rows
    part = jnp.concatenate([keep for _, _, keep in outs], axis=3).astype(F32)
    part = part.transpose(0, 2, 1, 3).reshape(prompt + win, 2, groups * HD)
    full = jnp.zeros((total, 2, groups * HD), F32).at[:prompt].set(part[:prompt])
    old = lax.dynamic_slice_in_dim(full, win_start, win, 0)
    full = lax.dynamic_update_slice_in_dim(full, old + part[prompt:], win_start, 0)
    reduced = lax.psum_scatter(full, "ctx", scatter_dimension=0, tiled=True)
    return (
        grad_queries,
        (reduced[:, 0] * SCALE).astype(BF16),
        reduced[:, 1].astype(BF16),
    )


def solution(mesh):
    placed = (
        P("ctx", "tp"),
        P("ctx"),
        P("tp", None),
        P("ctx", "tp"),
        P("ctx", "tp"),
        P("ctx", "tp"),
        P(),
        P("ctx", None),
    )
    return jax.shard_map(
        shards,
        mesh=mesh,
        in_specs=placed,
        out_specs=(P("ctx", "tp"), P("ctx", "tp"), P("ctx", "tp")),
        check_vma=False,
    )
```

```python
import functools
import math

import jax
import jax.numpy as jnp
from jax import lax
from jax.experimental import pallas as pl
from jax.experimental.pallas import tpu as pltpu
from jax.sharding import PartitionSpec as P

HEADS = 64
KV_HEADS = 8
SHARE = HEADS // KV_HEADS
HD = 128
TILE = 128
ROLLOUTS = 8
JITTER = 64
KB = 256
CHUNK = 1
WB = 512
AHEAD = 2
VMEM_LIMIT = 26 << 20
SCALE = 1.0 / math.sqrt(HD)
LOG2E = 1.4426950408889634
F32 = jnp.float32
BF16 = jnp.bfloat16
NT = (((1,), (1,)), ((), ()))


def dot(a, b):
    return jnp.dot(a, b, preferred_element_type=F32)


def dot_nt(a, b):
    return lax.dot_general(a, b, NT, preferred_element_type=F32)


SMEM = pl.BlockSpec(memory_space=pltpu.SMEM)
VMEM = pl.BlockSpec(memory_space=pltpu.VMEM)
HBM = pl.BlockSpec(memory_space=pltpu.HBM)


def at(start, size):
    return pl.ds(pl.multiple_of(start, size), size)


def call(kernel, ins, in_specs, outs, scratch=(), out_specs=None, flops=0, size=0, exps=0):
    return pl.pallas_call(
        kernel,
        in_specs=in_specs,
        out_specs=out_specs or [VMEM] * len(outs),
        out_shape=[
            out if isinstance(out, pl.MemoryRef) else jax.ShapeDtypeStruct(*out) for out in outs
        ],
        scratch_shapes=list(scratch),
        compiler_params=pltpu.CompilerParams(vmem_limit_bytes=VMEM_LIMIT),
        cost_estimate=pl.CostEstimate(flops=flops, bytes_accessed=size, transcendentals=exps),
    )(*ins)


def mask_kernel(n_kb, prompt, back, total, me_ref, seg_ref, tile_ref, bias_ref, live_ref):
    rows = bias_ref.shape[2]
    per = rows // KB
    me = me_ref[0]
    row_start = me * rows
    key_at = lax.broadcasted_iota(jnp.int32, (KB, KB), 0)
    query_at = lax.broadcasted_iota(jnp.int32, (KB, KB), 1)
    for kb in range(n_kb):
        window = kb >= prompt // KB
        age, sub = divmod(kb - prompt // KB, per)
        block = jnp.maximum(me - age, 0) * per + sub if window else kb
        key_pos = block * KB + key_at
        seg_k = jnp.broadcast_to(seg_ref[block], (KB, KB)).T
        some = jnp.int32(0)
        for r in range(per):
            same = seg_k == jnp.broadcast_to(seg_ref[me * per + r], (KB, KB))
            for a in range(KB // TILE):
                for b in range(KB // TILE):
                    mark = tile_ref[r * (KB // TILE) + b, block * (KB // TILE) + a]
                    inside = (key_at // TILE == a) & (query_at // TILE == b)
                    same = same | (inside & (jnp.full((KB, KB), mark) == 1))
            seen = same & (key_pos <= row_start + r * KB + query_at)
            if window:
                seen = seen & (key_pos >= prompt) & (jnp.full((KB, KB), me) >= prompt // rows)
            bias_ref[kb, :, r * KB : (r + 1) * KB] = jnp.where(seen, 0.0, -1e30)
            some = jnp.maximum(some, jnp.max(seen.astype(jnp.int32)))
        live_ref[kb] = some


def mask_call(me, segment_ids, tile_mask, rows, n_kb, prompt, back):
    total = segment_ids.shape[0]
    return call(
        functools.partial(mask_kernel, n_kb, prompt, back, total),
        (me[None], segment_ids.reshape(total // KB, 1, KB), tile_mask),
        [SMEM, VMEM, SMEM],
        [((n_kb, KB, rows), F32), ((n_kb,), jnp.int32)],
        out_specs=[VMEM, SMEM],
        size=n_kb * KB * rows * 4,
    )


def probs_kernel(
    n_kb, group, groups, slot_ref, shard_ref, w_ref, q_ref, near_ref, far_ref, bias_ref,
    p_ref, o_ref, k_ref, v_ref, wl_ref,
    ks_ref, vs_ref, kx_ref, vt_ref, s_ref, t_ref, ps_ref, os_ref, ws_ref, sems,
):
    rows = q_ref.shape[0]
    per = rows // KB
    n_near = near_ref.shape[0]
    vt_ref[HD:, :] = jnp.ones((16, n_kb * KB), BF16)
    for kb in range(n_kb):
        slot = slot_ref[kb]
        keys = pl.ds(kb * KB, KB)

        def place(source, index):
            ks_ref[keys, :] = source[index, :, group * HD : (group + 1) * HD]
            vs_ref[keys, :] = source[index, :, (groups + group) * HD : (groups + group + 1) * HD]

        @pl.when(slot < n_near)
        def _():
            place(near_ref, slot)

        @pl.when(slot >= n_near)
        def _():
            place(far_ref, slot - n_near)

    depth = wl_ref.shape[1]
    wide = SHARE * HD
    keep_w = pltpu.make_async_copy(
        w_ref.at[
            pl.ds(group * wide, wide), pl.ds(pl.multiple_of(shard_ref[0] * depth, HD), depth)
        ],
        ws_ref,
        sems.at[10],
    )
    pass_w = pltpu.make_async_copy(ws_ref, wl_ref, sems.at[11])
    keep_w.start()
    keep_k = pltpu.make_async_copy(ks_ref, k_ref, sems.at[8])
    keep_v = pltpu.make_async_copy(vs_ref, v_ref, sems.at[9])
    keep_k.start()
    keep_v.start()
    for kb in range(n_kb):
        keys = pl.ds(kb * KB, KB)
        k = ks_ref[keys, :]
        kx_ref[keys, :HD] = k
        kx_ref[keys, HD:] = k
        vt_ref[:HD, keys] = vs_ref[keys, :].T

    count = SHARE * per

    def score(i, s_ref):
        h, here = i // per, at((i % per) * KB, KB)
        q = q_ref[here, at((group * SHARE + h) * HD, HD)].astype(F32) * (SCALE * LOG2E)
        q_hi = q.astype(BF16)
        q_lo = (q - q_hi.astype(F32)).astype(BF16)
        qx = jnp.concatenate([q_hi, q_lo], axis=1)
        s = dot_nt(kx_ref[...], qx) + bias_ref[:, :, here].reshape(n_kb * KB, KB)
        s_ref[...] = s
        return jnp.max(s, axis=0, keepdims=True)

    def out(j, side):
        at_side = (j % 2) * 2 + side
        i = 2 * j + side
        return (
            pltpu.make_async_copy(ps_ref.at[at_side], p_ref.at[i], sems.at[at_side]),
            pltpu.make_async_copy(os_ref.at[at_side], o_ref.at[i], sems.at[4 + at_side]),
        )

    def soften(j, s_ref, top, side):
        at_side = (j % 2) * 2 + side
        e = jnp.exp2(s_ref[...] - top).astype(BF16)
        ps_ref[at_side] = e
        acc = dot(vt_ref[...], e)
        inv = 1.0 / acc[HD : HD + 1, :]
        os_ref[at_side, :, :HD] = (acc[:HD] * inv).T
        os_ref[at_side, :, HD:] = jnp.broadcast_to(inv, (HD, KB)).T

    def step(j, top):
        @pl.when(j == 1)
        def _():
            keep_w.wait()
            pass_w.start()

        @pl.when(j >= 2)
        def _():
            for copy in out(j - 2, 0) + out(j - 2, 1):
                copy.wait()

        later = score(2 * j + 1, t_ref)
        soften(j, s_ref, top, 0)
        top = score(jnp.minimum(2 * j + 2, count - 1), s_ref)
        soften(j, t_ref, later, 1)
        for copy in out(j, 0) + out(j, 1):
            copy.start()
        return top

    lax.fori_loop(0, count // 2, step, score(0, s_ref))
    for j in range(max(count // 2 - 2, 0), count // 2):
        for copy in out(j, 0) + out(j, 1):
            copy.wait()
    keep_k.wait()
    keep_v.wait()
    pass_w.wait()


def probs_call(group, groups, slots, shard, weight, depth, q, near, far, bias, n_kb):
    rows = q.shape[0]
    keys = n_kb * KB
    blocks = SHARE * rows // KB
    return call(
        functools.partial(probs_kernel, n_kb, group, groups),
        (slots, shard, weight, q, near, far, bias),
        [SMEM, SMEM, HBM] + [VMEM] * 4,
        [
            pltpu.HBM((blocks, keys, KB), BF16),
            pltpu.HBM((blocks, KB, 2 * HD), F32),
            pltpu.HBM((keys, HD), BF16),
            pltpu.HBM((keys, HD), BF16),
            pltpu.HBM((SHARE * HD, depth), BF16),
        ],
        scratch=[
            pltpu.VMEM((keys, HD), BF16),
            pltpu.VMEM((keys, HD), BF16),
            pltpu.VMEM((keys, 2 * HD), BF16),
            pltpu.VMEM((HD + 16, keys), BF16),
            pltpu.VMEM((keys, KB), F32),
            pltpu.VMEM((keys, KB), F32),
            pltpu.VMEM((4, keys, KB), BF16),
            pltpu.VMEM((4, KB, 2 * HD), F32),
            pltpu.VMEM((SHARE * HD, depth), BF16),
            pltpu.SemaphoreType.DMA((12,)),
        ],
        out_specs=[HBM] * 5,
    )


def back_kernel(
    n_kb, n_send, first, live_ref, pos_ref, proj_ref, x1_ref, x2_ref, w_ref, adv_ref,
    o_ref, q_ref, k_ref, v_ref, p_ref,
    dq_ref, send_ref, keep_ref, dox_ref, qs_ref, ds_ref, dqt_ref,
):
    rows = proj_ref.shape[0]
    per = rows // KB
    lane = lax.broadcasted_iota(jnp.int32, (KB, HD), 1)
    minus = jnp.where(lane < 3, -1.0, 0.0).astype(BF16)
    x = x1_ref[...] + x2_ref[...]
    dqt_ref[...] = jnp.zeros_like(dqt_ref)
    for h in range(SHARE):
        cols = pl.ds((first + h) * HD, HD)
        fresh = dot_nt(x, w_ref[h * HD : (h + 1) * HD, :])
        for r in range(per):
            part = slice(r * KB, (r + 1) * KB)
            here = pl.ds((h * per + r) * KB, KB)
            out = o_ref[h * per + r]
            proj = proj_ref[part, cols] + fresh[part]
            grad = (proj * (adv_ref[part, :] * out[:, HD:])).astype(BF16)
            delta = jnp.sum(grad.astype(F32) * out[:, :HD], axis=1, keepdims=True)
            one = delta.astype(BF16).astype(F32)
            two = (delta - one).astype(BF16).astype(F32)
            three = delta - one - two
            ext = jnp.where(
                lane == 0, one, jnp.where(lane == 1, two, jnp.where(lane == 2, three, 0.0))
            )
            dox_ref[here, :HD] = grad
            dox_ref[here, HD:] = ext.astype(BF16)
            qs_ref[here, :] = q_ref[part, cols]

    def put(kb, value):
        pos = pos_ref[kb]

        @pl.when(pos < n_send)
        def _():
            send_ref[pos] = value

        @pl.when(pos >= n_send)
        def _():
            keep_ref[pos - n_send] = value

    def chunk(start, count):
        keys = pl.ds(start * KB, count * KB)
        blocks = range(start, start + count)
        live = functools.reduce(jnp.bitwise_or, [live_ref[kb] for kb in blocks])

        @pl.when(live != 0)
        def _():
            vx = jnp.concatenate(
                [v_ref[keys, :], jnp.concatenate([minus] * count, axis=0)], axis=1
            )
            p = jnp.concatenate([p_ref[i, keys, :] for i in range(SHARE * per)], axis=1)
            dv = dot(p, dox_ref[:, :HD])
            for i in range(SHARE * per):
                here = pl.ds(i * KB, KB)
                dp = dot_nt(vx, dox_ref[here, :])
                ds_ref[: count * KB, here] = (p_ref[i, keys, :].astype(F32) * dp).astype(BF16)
            dqt_ref[...] += dot(k_ref[keys, :].T, ds_ref[: count * KB, :])
            dk = dot(ds_ref[: count * KB, :], qs_ref[...])
            for j, kb in enumerate(blocks):
                part = slice(j * KB, (j + 1) * KB)
                put(kb, jnp.stack([dk[part], dv[part]]).astype(BF16))

        @pl.when(live == 0)
        def _():
            for kb in blocks:
                put(kb, jnp.zeros((2, KB, HD), BF16))

    for start in range(0, n_kb, CHUNK):
        chunk(start, min(CHUNK, n_kb - start))
    for h in range(SHARE):
        dq_ref[:, pl.ds(h * HD, HD)] = (
            (dqt_ref[:, h * rows : (h + 1) * rows] * SCALE).T.astype(BF16)
        )


def back_call(group, live, pos, proj, x1, x2, w, adv, o, q, k, v, p, n_kb, n_send):
    rows = q.shape[0]
    return call(
        functools.partial(back_kernel, n_kb, n_send, group * SHARE),
        (live, pos, proj, x1, x2, w, adv, o, q, k, v, p),
        [SMEM] * 2 + [VMEM] * 10,
        [
            ((rows, SHARE * HD), BF16),
            ((max(n_send, 1), 2, KB, HD), BF16),
            ((n_kb - n_send, 2, KB, HD), BF16),
        ],
        scratch=[
            pltpu.VMEM((SHARE * rows, 2 * HD), BF16),
            pltpu.VMEM((SHARE * rows, HD), BF16),
            pltpu.VMEM((CHUNK * KB, SHARE * rows), BF16),
            pltpu.VMEM((HD, SHARE * rows), F32),
        ],
    )


def middle_kernel(me_ref, got_ref, keep_ref, base_ref, x_ref, y_ref, d_ref):
    me = me_ref[0]
    core, side, roll = me & 1, (me >> 1) & 1, me >= 4
    here = keep_ref[side].astype(F32) + got_ref[side].astype(F32)
    there = keep_ref[1 - side].astype(F32) + got_ref[1 - side].astype(F32)
    y_ref[...] = here.astype(BF16)
    d_ref[...] = there.astype(BF16)
    got = got_ref[2].astype(F32)
    late = (jnp.full(got.shape, core) == 1)

    @pl.when(roll)
    def _():
        x_ref[...] = (keep_ref[2].astype(F32) + jnp.where(late, got, 0.0)).astype(BF16)
        base_ref[...] = keep_ref[3].astype(F32) + jnp.where(late, 0.0, got)

    @pl.when(jnp.logical_not(roll))
    def _():
        x_ref[...] = there.astype(BF16)
        base_ref[...] = here


def last_kernel(groups, *refs):
    dk_ref, dv_ref = refs[-2:]
    for g in range(groups):
        base, x, y, d = refs[4 * g : 4 * g + 4]
        total = base[...] + x[...].astype(F32) + y[...].astype(F32) + d[...].astype(F32)
        dk_ref[:, g * HD : (g + 1) * HD] = (total[0] * SCALE).astype(BF16)
        dv_ref[:, g * HD : (g + 1) * HD] = total[1].astype(BF16)


def project_kernel(count, added, halves, shard_ref, w_ref, *refs):
    xs, refs = refs[:count], refs[count:]
    if added:
        acc_ref, refs = refs[0], refs[1:]
    values = [x[...] for x in xs]
    if halves:
        values[-1] = values[-1] + refs[0][...]
        refs = refs[1:]
    out_ref, held_ref, sems = refs
    depth = xs[0].shape[1]
    blocks = w_ref.shape[0] // WB

    def fetch(i, n):
        return pltpu.make_async_copy(
            w_ref.at[pl.ds(n * WB, WB), pl.ds(pl.multiple_of(shard_ref[i] * depth, HD), depth)],
            held_ref.at[i, n],
            sems.at[i, n],
        )

    def start(n):
        for i in range(count):
            fetch(i, n).start()

    for n in range(min(AHEAD, blocks)):
        start(n)
    for n in range(blocks):
        here = slice(n * WB, (n + 1) * WB)
        total = acc_ref[:, here] if added else None
        for i in range(count):
            fetch(i, n).wait()
        if n + AHEAD < blocks:
            start(n + AHEAD)
        for i in range(count):
            part = dot_nt(values[i], held_ref[i, n])
            total = part if total is None else total + part
        out_ref[:, here] = total


def project_call(shards_of, xs, weight, acc=None, rest=None):
    rows, depth = xs[0].shape
    wide = weight.shape[0]
    count = len(xs)
    added, halves = acc is not None, rest is not None
    return call(
        functools.partial(project_kernel, count, added, halves),
        (shards_of, weight, *xs, *([acc] if added else []), *([rest] if halves else [])),
        [SMEM, HBM] + [VMEM] * (count + added + halves),
        [((rows, wide), F32)],
        scratch=[
            pltpu.VMEM((count, wide // WB, WB, depth), BF16),
            pltpu.SemaphoreType.DMA((count, wide // WB)),
        ],
    )[0]


def key_window(tok_rows, total):
    span = (total - total // 2) // ROLLOUTS
    reach = 3 * span + TILE + JITTER
    reach = reach // TILE * TILE
    return -(-reach // tok_rows)


def shards(
    upstream, advantage, out_weight, query_heads, key_heads, value_heads, segment_ids, tile_mask
):
    rows = query_heads.shape[0]
    n_ctx = lax.axis_size("ctx")
    n_tp = lax.axis_size("tp")
    total = rows * n_ctx
    prompt = total // 2
    groups = key_heads.shape[1] // HD
    me = lax.axis_index("ctx").astype(jnp.int32)
    z = lax.axis_index("tp").astype(jnp.int32)
    per = rows // KB
    back = key_window(rows, total)
    prompt_kb = prompt // KB
    n_kb = prompt_kb + (back + 1) * per
    fast = n_ctx == 8 and n_tp == 4 and per == 1 and back == 2
    own = jnp.concatenate([key_heads, value_heads], axis=1)
    weight = pltpu.with_memory_space_constraint(out_weight, pltpu.HBM)

    def hop(value, pairs):
        return lax.ppermute(value, "tp", pairs)

    def flip(value, bit, pairs=None):
        return lax.ppermute(value, "ctx", pairs or [(i, i ^ bit) for i in range(n_ctx)])

    if fast:
        near = jnp.stack([own] + [flip(own, d) for d in (2, 4, 6)])
        ends, middle, out = [(0, 1), (1, 0), (2, 3), (3, 2)], [(1, 2), (2, 1)], [(1, 0), (2, 3)]
        up_a = hop(upstream, ends)
        up_c = hop(upstream, middle)
    else:
        near = lax.all_gather(own, "ctx", axis=0)
        near = far = near.reshape(n_ctx * per, KB, 2 * groups * HD)

    bias, live = mask_call(me, segment_ids, tile_mask, rows, n_kb, prompt, back)
    block = jnp.arange(n_kb, dtype=jnp.int32)
    holder = jnp.where(
        block < prompt_kb,
        block // per,
        jnp.where(me * rows >= prompt, me - (block - prompt_kb) // per, me),
    )
    if fast:
        away = holder ^ me
        slots = away // 2 + (away % 2) * 4
        core = me & 1
        pos = jnp.where(
            block < 4,
            jnp.where(block % 2 == core, 3 + block // 2, block // 2),
            jnp.array([0, 0, 0, 0, 6, 2, 5], jnp.int32),
        )
        n_send = 3
        half = z // 2
        second, shard = 2 - half, 3 - 3 * half
        acc = project_call(z[None], [upstream], weight)
    else:
        slots = holder * per + block % per
        pos = block
        n_send = 0
        whole = lax.all_gather(upstream, "tp", axis=0)
        shard = z
        acc = jnp.zeros((rows, out_weight.shape[0]), F32)
        for i in range(n_tp - 1):
            other = (z + 1 + i) % n_tp
            x = lax.dynamic_index_in_dim(whole, other, 0, keepdims=False)
            acc = project_call(other[None], [x], weight, acc)
        x1, x2 = upstream, jnp.zeros_like(upstream)

    slots = slots.astype(jnp.int32)
    depth = upstream.shape[1]
    if fast:
        near, bias, acc, up_a, up_c = lax.optimization_barrier((near, bias, acc, up_a, up_c))
        far = flip(near, 1)
        up_e = hop(up_a, middle)
        up_f = hop(up_c, out)
    soft = [list(probs_call(0, groups, slots, shard[None], weight, depth, query_heads, near, far, bias, n_kb))]
    if fast:
        up_e, soft[0][2] = lax.optimization_barrier((up_e, soft[0][2]))
        up_d = hop(up_e, out)
        x1, x2 = up_d, up_e
    soft += [
        list(probs_call(g, groups, slots, shard[None], weight, depth, query_heads, near, far, bias, n_kb))
        for g in range(1, groups)
    ]
    if fast:
        acc, soft[-1][2] = lax.optimization_barrier((acc, soft[-1][2]))
        acc = project_call(jnp.stack([z ^ 1, second]), [up_a, up_c], weight, acc, up_f)
    outs = []
    for g in range(groups):
        probs, attn, keys, values, w_last = soft[g]
        outs.append(
            back_call(
                g, live, pos.astype(jnp.int32), acc, x1, x2, w_last, advantage[:, None], attn,
                query_heads, keys, values, probs, n_kb, n_send,
            )
        )
    grad_queries = jnp.concatenate([dq for dq, _, _ in outs], axis=1)

    if fast:
        final = []
        shape = (2, KB, HD)
        for _, send, keep in outs:
            base, to_x, to_y, to_d = call(
                middle_kernel,
                (me[None], flip(send, 1), keep),
                [SMEM, VMEM, VMEM],
                [(shape, F32), (shape, BF16), (shape, BF16), (shape, BF16)],
            )
            by_y = flip(to_y, 4, [(4, 0), (5, 1), (6, 2), (7, 3)])
            by_d = flip(to_d, 6, [(4, 2), (5, 3), (6, 0), (7, 1)])
            by_x = flip(to_x, 2, [(0, 2), (2, 0), (1, 3), (3, 1), (6, 4), (7, 5)])
            final += [base, by_x, by_y, by_d]
        grad_keys, grad_values = call(
            functools.partial(last_kernel, groups),
            final,
            [VMEM] * len(final),
            [((rows, groups * HD), BF16)] * 2,
        )
        return grad_queries, grad_keys, grad_values

    win = (back + 1) * rows
    win_start = jnp.maximum(me - back, 0) * rows
    part = jnp.concatenate([keep for _, _, keep in outs], axis=3).astype(F32)
    part = part.transpose(0, 2, 1, 3).reshape(prompt + win, 2, groups * HD)
    rear = part[prompt:].reshape(back + 1, rows, 2, groups * HD)[::-1].reshape(win, 2, -1)
    full = jnp.zeros((total, 2, groups * HD), F32).at[:prompt].set(part[:prompt])
    old = lax.dynamic_slice_in_dim(full, win_start, win, 0)
    full = lax.dynamic_update_slice_in_dim(full, old + rear, win_start, 0)
    reduced = lax.psum_scatter(full, "ctx", scatter_dimension=0, tiled=True)
    return (
        grad_queries,
        (reduced[:, 0] * SCALE).astype(BF16),
        reduced[:, 1].astype(BF16),
    )


def solution(mesh):
    placed = (
        P("ctx", "tp"),
        P("ctx"),
        P("tp", None),
        P("ctx", "tp"),
        P("ctx", "tp"),
        P("ctx", "tp"),
        P(),
        P("ctx", None),
    )
    return jax.shard_map(
        shards,
        mesh=mesh,
        in_specs=placed,
        out_specs=(P("ctx", "tp"), P("ctx", "tp"), P("ctx", "tp")),
        check_vma=False,
    )
```

```python
import functools
import math

import jax
import jax.numpy as jnp
from jax import lax
from jax.experimental import pallas as pl
from jax.experimental.pallas import tpu as pltpu
from jax.sharding import PartitionSpec as P

HEADS = 64
KV_HEADS = 8
SHARE = HEADS // KV_HEADS
HD = 128
TILE = 128
ROLLOUTS = 8
JITTER = 64
KB = 256
CHUNK = 1
WB = 512
AHEAD = 2
VMEM_LIMIT = 26 << 20
SCALE = 1.0 / math.sqrt(HD)
LOG2E = 1.4426950408889634
F32 = jnp.float32
BF16 = jnp.bfloat16
NT = (((1,), (1,)), ((), ()))


def dot(a, b):
    return jnp.dot(a, b, preferred_element_type=F32)


def dot_nt(a, b):
    return lax.dot_general(a, b, NT, preferred_element_type=F32)


SMEM = pl.BlockSpec(memory_space=pltpu.SMEM)
VMEM = pl.BlockSpec(memory_space=pltpu.VMEM)
HBM = pl.BlockSpec(memory_space=pltpu.HBM)


def at(start, size):
    return pl.ds(pl.multiple_of(start, size), size)


def call(kernel, ins, in_specs, outs, scratch=(), out_specs=None, flops=0, size=0, exps=0):
    return pl.pallas_call(
        kernel,
        in_specs=in_specs,
        out_specs=out_specs or [VMEM] * len(outs),
        out_shape=[
            out if isinstance(out, pl.MemoryRef) else jax.ShapeDtypeStruct(*out) for out in outs
        ],
        scratch_shapes=list(scratch),
        compiler_params=pltpu.CompilerParams(vmem_limit_bytes=VMEM_LIMIT),
        cost_estimate=pl.CostEstimate(flops=flops, bytes_accessed=size, transcendentals=exps),
    )(*ins)


def join_kernel(k_ref, v_ref, out_ref):
    width = k_ref.shape[1]
    out_ref[:, :width] = k_ref[...]
    out_ref[:, width:] = v_ref[...]


def stack_kernel(*refs):
    for i, ref in enumerate(refs[:-1]):
        refs[-1][i] = ref[...]


def mask_kernel(n_kb, prompt, back, total, me_ref, seg_ref, tile_ref, bias_ref, live_ref):
    rows = bias_ref.shape[2]
    per = rows // KB
    me = me_ref[0]
    row_start = me * rows
    key_at = lax.broadcasted_iota(jnp.int32, (KB, KB), 0)
    query_at = lax.broadcasted_iota(jnp.int32, (KB, KB), 1)
    for kb in range(n_kb):
        window = kb >= prompt // KB
        age, sub = divmod(kb - prompt // KB, per)
        block = jnp.maximum(me - age, 0) * per + sub if window else kb
        key_pos = block * KB + key_at
        seg_k = jnp.broadcast_to(seg_ref[block], (KB, KB)).T
        some = jnp.int32(0)
        for r in range(per):
            same = seg_k == jnp.broadcast_to(seg_ref[me * per + r], (KB, KB))
            for a in range(KB // TILE):
                for b in range(KB // TILE):
                    mark = tile_ref[r * (KB // TILE) + b, block * (KB // TILE) + a]
                    inside = (key_at // TILE == a) & (query_at // TILE == b)
                    same = same | (inside & (jnp.full((KB, KB), mark) == 1))
            seen = same & (key_pos <= row_start + r * KB + query_at)
            if window:
                seen = seen & (key_pos >= prompt) & (jnp.full((KB, KB), me) >= prompt // rows)
            bias_ref[kb, :, r * KB : (r + 1) * KB] = jnp.where(seen, 0.0, -1e30)
            some = jnp.maximum(some, jnp.max(seen.astype(jnp.int32)))
        live_ref[kb] = some


def mask_call(me, segment_ids, tile_mask, rows, n_kb, prompt, back):
    total = segment_ids.shape[0]
    return call(
        functools.partial(mask_kernel, n_kb, prompt, back, total),
        (me[None], segment_ids.reshape(total // KB, 1, KB), tile_mask),
        [SMEM, VMEM, SMEM],
        [((n_kb, KB, rows), F32), ((n_kb,), jnp.int32)],
        out_specs=[VMEM, SMEM],
        size=n_kb * KB * rows * 4,
    )


def probs_kernel(
    n_kb, group, groups, slot_ref, shard_ref, w_ref, q_ref, near_ref, far_ref, bias_ref,
    p_ref, o_ref, k_ref, v_ref, wl_ref,
    ks_ref, vs_ref, kx_ref, vt_ref, s_ref, t_ref, ps_ref, os_ref, ws_ref, sems,
):
    rows = q_ref.shape[0]
    per = rows // KB
    n_near = near_ref.shape[0]
    vt_ref[HD:, :] = jnp.ones((16, n_kb * KB), BF16)
    for kb in range(n_kb):
        slot = slot_ref[kb]
        keys = pl.ds(kb * KB, KB)

        def place(source, index):
            ks_ref[keys, :] = source[index, :, group * HD : (group + 1) * HD]
            vs_ref[keys, :] = source[index, :, (groups + group) * HD : (groups + group + 1) * HD]

        @pl.when(slot < n_near)
        def _():
            place(near_ref, slot)

        @pl.when(slot >= n_near)
        def _():
            place(far_ref, slot - n_near)

    depth = wl_ref.shape[1]
    wide = SHARE * HD
    keep_w = pltpu.make_async_copy(
        w_ref.at[
            pl.ds(group * wide, wide), pl.ds(pl.multiple_of(shard_ref[0] * depth, HD), depth)
        ],
        ws_ref,
        sems.at[10],
    )
    pass_w = pltpu.make_async_copy(ws_ref, wl_ref, sems.at[11])
    keep_w.start()
    keep_k = pltpu.make_async_copy(ks_ref, k_ref, sems.at[8])
    keep_v = pltpu.make_async_copy(vs_ref, v_ref, sems.at[9])
    keep_k.start()
    keep_v.start()
    for kb in range(n_kb):
        keys = pl.ds(kb * KB, KB)
        k = ks_ref[keys, :]
        kx_ref[keys, :HD] = k
        kx_ref[keys, HD:] = k
        vt_ref[:HD, keys] = vs_ref[keys, :].T

    count = SHARE * per

    def score(i, s_ref):
        h, here = i // per, at((i % per) * KB, KB)
        q = q_ref[here, at((group * SHARE + h) * HD, HD)].astype(F32) * (SCALE * LOG2E)
        q_hi = q.astype(BF16)
        q_lo = (q - q_hi.astype(F32)).astype(BF16)
        qx = jnp.concatenate([q_hi, q_lo], axis=1)
        s = dot_nt(kx_ref[...], qx) + bias_ref[:, :, here].reshape(n_kb * KB, KB)
        s_ref[...] = s
        return jnp.max(s, axis=0, keepdims=True)

    def out(j, side):
        at_side = (j % 2) * 2 + side
        i = 2 * j + side
        return (
            pltpu.make_async_copy(ps_ref.at[at_side], p_ref.at[i], sems.at[at_side]),
            pltpu.make_async_copy(os_ref.at[at_side], o_ref.at[i], sems.at[4 + at_side]),
        )

    def soften(j, s_ref, top, side):
        at_side = (j % 2) * 2 + side
        e = jnp.exp2(s_ref[...] - top).astype(BF16)
        ps_ref[at_side] = e
        acc = dot(vt_ref[...], e)
        inv = 1.0 / acc[HD : HD + 1, :]
        os_ref[at_side, :, :HD] = (acc[:HD] * inv).T
        os_ref[at_side, :, HD:] = jnp.broadcast_to(inv, (HD, KB)).T

    def step(j, top):
        @pl.when(j == 1)
        def _():
            keep_w.wait()
            pass_w.start()

        @pl.when(j >= 2)
        def _():
            for copy in out(j - 2, 0) + out(j - 2, 1):
                copy.wait()

        later = score(2 * j + 1, t_ref)
        soften(j, s_ref, top, 0)
        top = score(jnp.minimum(2 * j + 2, count - 1), s_ref)
        soften(j, t_ref, later, 1)
        for copy in out(j, 0) + out(j, 1):
            copy.start()
        return top

    lax.fori_loop(0, count // 2, step, score(0, s_ref))
    for j in range(max(count // 2 - 2, 0), count // 2):
        for copy in out(j, 0) + out(j, 1):
            copy.wait()
    keep_k.wait()
    keep_v.wait()
    pass_w.wait()


def probs_call(group, groups, slots, shard, weight, depth, q, near, far, bias, n_kb):
    rows = q.shape[0]
    keys = n_kb * KB
    blocks = SHARE * rows // KB
    return call(
        functools.partial(probs_kernel, n_kb, group, groups),
        (slots, shard, weight, q, near, far, bias),
        [SMEM, SMEM, HBM] + [VMEM] * 4,
        [
            pltpu.HBM((blocks, keys, KB), BF16),
            pltpu.HBM((blocks, KB, 2 * HD), F32),
            pltpu.HBM((keys, HD), BF16),
            pltpu.HBM((keys, HD), BF16),
            pltpu.HBM((SHARE * HD, depth), BF16),
        ],
        scratch=[
            pltpu.VMEM((keys, HD), BF16),
            pltpu.VMEM((keys, HD), BF16),
            pltpu.VMEM((keys, 2 * HD), BF16),
            pltpu.VMEM((HD + 16, keys), BF16),
            pltpu.VMEM((keys, KB), F32),
            pltpu.VMEM((keys, KB), F32),
            pltpu.VMEM((4, keys, KB), BF16),
            pltpu.VMEM((4, KB, 2 * HD), F32),
            pltpu.VMEM((SHARE * HD, depth), BF16),
            pltpu.SemaphoreType.DMA((12,)),
        ],
        out_specs=[HBM] * 5,
    )


def back_kernel(
    n_kb, n_send, first, live_ref, pos_ref, edge_ref, proj_ref, x1_ref, x2_ref, w_ref, adv_ref,
    o_ref, q_ref, k_ref, v_ref, p_ref,
    dq_ref, send_ref, keep_ref, dox_ref, qs_ref, ds_ref, dqt_ref,
):
    rows = proj_ref.shape[0]
    per = rows // KB
    lane = lax.broadcasted_iota(jnp.int32, (KB, HD), 1)
    minus = jnp.where(lane < 3, -1.0, 0.0).astype(BF16)
    x = choose(edge_ref[0], x1_ref[...], x2_ref[...])
    dqt_ref[...] = jnp.zeros_like(dqt_ref)
    adv = jnp.broadcast_to(adv_ref[...], (HD, rows)).T
    for h in range(SHARE):
        cols = pl.ds((first + h) * HD, HD)
        fresh = dot_nt(x, w_ref[h * HD : (h + 1) * HD, :])
        for r in range(per):
            part = slice(r * KB, (r + 1) * KB)
            here = pl.ds((h * per + r) * KB, KB)
            out = o_ref[h * per + r]
            proj = proj_ref[part, cols] + fresh[part]
            grad = (proj * (adv[part] * out[:, HD:])).astype(BF16)
            delta = jnp.sum(grad.astype(F32) * out[:, :HD], axis=1, keepdims=True)
            one = delta.astype(BF16).astype(F32)
            two = (delta - one).astype(BF16).astype(F32)
            three = delta - one - two
            ext = jnp.where(
                lane == 0, one, jnp.where(lane == 1, two, jnp.where(lane == 2, three, 0.0))
            )
            dox_ref[here, :HD] = grad
            dox_ref[here, HD:] = ext.astype(BF16)
            qs_ref[here, :] = q_ref[part, cols]

    def put(kb, value):
        pos = pos_ref[kb]

        @pl.when(pos < n_send)
        def _():
            send_ref[pos] = value

        @pl.when(pos >= n_send)
        def _():
            keep_ref[pos - n_send] = value

    def chunk(start, count):
        keys = pl.ds(start * KB, count * KB)
        blocks = range(start, start + count)
        live = functools.reduce(jnp.bitwise_or, [live_ref[kb] for kb in blocks])

        @pl.when(live != 0)
        def _():
            vx = jnp.concatenate(
                [v_ref[keys, :], jnp.concatenate([minus] * count, axis=0)], axis=1
            )
            p = jnp.concatenate([p_ref[i, keys, :] for i in range(SHARE * per)], axis=1)
            dv = dot(p, dox_ref[:, :HD])
            for i in range(SHARE * per):
                here = pl.ds(i * KB, KB)
                dp = dot_nt(vx, dox_ref[here, :])
                ds_ref[: count * KB, here] = (p_ref[i, keys, :].astype(F32) * dp).astype(BF16)
            dqt_ref[...] += dot(k_ref[keys, :].T, ds_ref[: count * KB, :])
            dk = dot(ds_ref[: count * KB, :], qs_ref[...])
            for j, kb in enumerate(blocks):
                part = slice(j * KB, (j + 1) * KB)
                put(kb, jnp.stack([dk[part], dv[part]]).astype(BF16))

        @pl.when(live == 0)
        def _():
            for kb in blocks:
                put(kb, jnp.zeros((2, KB, HD), BF16))

    for start in range(0, n_kb, CHUNK):
        chunk(start, min(CHUNK, n_kb - start))
    for h in range(SHARE):
        dq_ref[:, pl.ds(h * HD, HD)] = (
            (dqt_ref[:, h * rows : (h + 1) * rows] * SCALE).T.astype(BF16)
        )


def back_call(group, live, pos, edge, proj, x1, x2, w, adv, o, q, k, v, p, n_kb, n_send):
    rows = q.shape[0]
    return call(
        functools.partial(back_kernel, n_kb, n_send, group * SHARE),
        (live, pos, edge, proj, x1, x2, w, adv, o, q, k, v, p),
        [SMEM] * 3 + [VMEM] * 10,
        [
            ((rows, SHARE * HD), BF16),
            ((max(n_send, 1), 2, KB, HD), BF16),
            ((n_kb - n_send, 2, KB, HD), BF16),
        ],
        scratch=[
            pltpu.VMEM((SHARE * rows, 2 * HD), BF16),
            pltpu.VMEM((SHARE * rows, HD), BF16),
            pltpu.VMEM((CHUNK * KB, SHARE * rows), BF16),
            pltpu.VMEM((HD, SHARE * rows), F32),
        ],
    )


def middle_kernel(me_ref, got_ref, keep_ref, base_ref, x_ref, y_ref, d_ref):
    me = me_ref[0]
    core, side, roll = me & 1, (me >> 1) & 1, me >= 4
    here = keep_ref[side].astype(F32) + got_ref[side].astype(F32)
    there = keep_ref[1 - side].astype(F32) + got_ref[1 - side].astype(F32)
    y_ref[...] = here.astype(BF16)
    d_ref[...] = there.astype(BF16)
    got = got_ref[2].astype(F32)
    late = (jnp.full(got.shape, core) == 1)

    @pl.when(roll)
    def _():
        x_ref[...] = (keep_ref[2].astype(F32) + jnp.where(late, got, 0.0)).astype(BF16)
        base_ref[...] = keep_ref[3].astype(F32) + jnp.where(late, 0.0, got)

    @pl.when(jnp.logical_not(roll))
    def _():
        x_ref[...] = there.astype(BF16)
        base_ref[...] = here


def last_kernel(groups, me_ref, *refs):
    dk_ref, dv_ref = refs[-2:]
    me = jnp.full((2, KB, HD), me_ref[0])
    across, beside = me < 4, me < 6
    for g in range(groups):
        base, x, y, d = refs[4 * g : 4 * g + 4]
        total = base[...] + jnp.where(beside, x[...].astype(F32), 0.0)
        total += jnp.where(across, y[...].astype(F32) + d[...].astype(F32), 0.0)
        dk_ref[:, g * HD : (g + 1) * HD] = (total[0] * SCALE).astype(BF16)
        dv_ref[:, g * HD : (g + 1) * HD] = total[1].astype(BF16)


def choose(flag, first, second):
    return jnp.where(jnp.full(first.shape, flag) != 0, first, second)


def project_kernel(count, added, halves, shard_ref, w_ref, *refs):
    xs, refs = refs[:count], refs[count:]
    if added:
        acc_ref, refs = refs[0], refs[1:]
    values = [x[...] for x in xs]
    if halves:
        values[-1] = choose(shard_ref[count], refs[0][...], values[-1])
        refs = refs[1:]
    out_ref, held_ref, sems = refs
    depth = xs[0].shape[1]
    blocks = w_ref.shape[0] // WB

    def fetch(i, n):
        return pltpu.make_async_copy(
            w_ref.at[pl.ds(n * WB, WB), pl.ds(pl.multiple_of(shard_ref[i] * depth, HD), depth)],
            held_ref.at[i, n],
            sems.at[i, n],
        )

    def start(n):
        for i in range(count):
            fetch(i, n).start()

    for n in range(min(AHEAD, blocks)):
        start(n)
    for n in range(blocks):
        here = slice(n * WB, (n + 1) * WB)
        total = acc_ref[:, here] if added else None
        for i in range(count):
            fetch(i, n).wait()
        if n + AHEAD < blocks:
            start(n + AHEAD)
        for i in range(count):
            part = dot_nt(values[i], held_ref[i, n])
            total = part if total is None else total + part
        out_ref[:, here] = total


def project_call(shards_of, xs, weight, acc=None, rest=None):
    rows, depth = xs[0].shape
    wide = weight.shape[0]
    count = len(xs)
    added, halves = acc is not None, rest is not None
    return call(
        functools.partial(project_kernel, count, added, halves),
        (shards_of, weight, *xs, *([acc] if added else []), *([rest] if halves else [])),
        [SMEM, HBM] + [VMEM] * (count + added + halves),
        [((rows, wide), F32)],
        scratch=[
            pltpu.VMEM((count, wide // WB, WB, depth), BF16),
            pltpu.SemaphoreType.DMA((count, wide // WB)),
        ],
    )[0]


def key_window(tok_rows, total):
    span = (total - total // 2) // ROLLOUTS
    reach = 3 * span + TILE + JITTER
    reach = reach // TILE * TILE
    return -(-reach // tok_rows)


def shards(
    upstream, advantage, out_weight, query_heads, key_heads, value_heads, segment_ids, tile_mask
):
    rows = query_heads.shape[0]
    n_ctx = lax.axis_size("ctx")
    n_tp = lax.axis_size("tp")
    total = rows * n_ctx
    prompt = total // 2
    groups = key_heads.shape[1] // HD
    me = lax.axis_index("ctx").astype(jnp.int32)
    z = lax.axis_index("tp").astype(jnp.int32)
    per = rows // KB
    back = key_window(rows, total)
    prompt_kb = prompt // KB
    n_kb = prompt_kb + (back + 1) * per
    fast = n_ctx == 8 and n_tp == 4 and per == 1 and back == 2
    shape = (rows, 2 * groups * HD)
    own = call(join_kernel, (key_heads, value_heads), [VMEM] * 2, [(shape, BF16)])[0]
    weight = pltpu.with_memory_space_constraint(out_weight, pltpu.HBM)

    def hop(value, pairs):
        return lax.ppermute(value, "tp", pairs)

    def flip(value, bit):
        return lax.ppermute(value, "ctx", [(i, i ^ bit) for i in range(n_ctx)])

    if fast:
        pieces = [own] + [flip(own, d) for d in (2, 4, 6)]
        near = call(stack_kernel, pieces, [VMEM] * 4, [((4,) + shape, BF16)])[0]
        ends, middle = [(0, 1), (1, 0), (2, 3), (3, 2)], [(1, 2), (2, 1), (0, 0), (3, 3)]
        up_a = hop(upstream, ends)
        up_c = hop(upstream, middle)
    else:
        near = lax.all_gather(own, "ctx", axis=0)
        near = far = near.reshape(n_ctx * per, KB, 2 * groups * HD)

    bias, live = mask_call(me, segment_ids, tile_mask, rows, n_kb, prompt, back)
    block = jnp.arange(n_kb, dtype=jnp.int32)
    holder = jnp.where(
        block < prompt_kb,
        block // per,
        jnp.where(me * rows >= prompt, me - (block - prompt_kb) // per, me),
    )
    if fast:
        away = holder ^ me
        slots = away // 2 + (away % 2) * 4
        core = me & 1
        pos = jnp.where(
            block < 4,
            jnp.where(block % 2 == core, 3 + block // 2, block // 2),
            jnp.array([0, 0, 0, 0, 6, 2, 5], jnp.int32),
        )
        n_send = 3
        half, edge = z // 2, (z % 3 == 0).astype(jnp.int32)
        second, shard = 2 - half, 3 - 3 * half
        acc = project_call(z[None], [upstream], weight)
    else:
        slots = holder * per + block % per
        pos = block
        n_send = 0
        whole = lax.all_gather(upstream, "tp", axis=0)
        shard = z
        acc = jnp.zeros((rows, out_weight.shape[0]), F32)
        for i in range(n_tp - 1):
            other = (z + 1 + i) % n_tp
            x = lax.dynamic_index_in_dim(whole, other, 0, keepdims=False)
            acc = project_call(other[None], [x], weight, acc)
        x1, x2, edge = upstream, upstream, jnp.int32(1)

    slots = slots.astype(jnp.int32)
    depth = upstream.shape[1]
    if fast:
        up_a, up_c, bias, acc = lax.optimization_barrier((up_a, up_c, bias, acc))
        up_e = hop(up_a, middle)
        up_f = hop(up_c, ends)
        near, up_a = lax.optimization_barrier((near, up_a))
        far = flip(near, 1)
    soft = [list(probs_call(0, groups, slots, shard[None], weight, depth, query_heads, near, far, bias, n_kb))]
    if fast:
        up_e, soft[0][2] = lax.optimization_barrier((up_e, soft[0][2]))
        up_d = hop(up_e, ends)
        x1, x2 = up_d, up_e
    soft += [
        list(probs_call(g, groups, slots, shard[None], weight, depth, query_heads, near, far, bias, n_kb))
        for g in range(1, groups)
    ]
    if fast:
        acc, soft[-1][2] = lax.optimization_barrier((acc, soft[-1][2]))
        acc = project_call(jnp.stack([z ^ 1, second, edge]), [up_a, up_c], weight, acc, up_f)
    outs = []
    for g in range(groups):
        probs, attn, keys, values, w_last = soft[g]
        outs.append(
            back_call(
                g, live, pos.astype(jnp.int32), edge[None], acc, x1, x2, w_last, advantage[None, :], attn,
                query_heads, keys, values, probs, n_kb, n_send,
            )
        )
    grad_queries = jnp.concatenate([dq for dq, _, _ in outs], axis=1)

    if fast:
        final = []
        shape = (2, KB, HD)
        for _, send, keep in outs:
            base, to_x, to_y, to_d = call(
                middle_kernel,
                (me[None], flip(send, 1), keep),
                [SMEM, VMEM, VMEM],
                [(shape, F32), (shape, BF16), (shape, BF16), (shape, BF16)],
            )
            by_y = flip(to_y, 4)
            by_d = flip(to_d, 6)
            by_x = flip(to_x, 2)
            final += [base, by_x, by_y, by_d]
        grad_keys, grad_values = call(
            functools.partial(last_kernel, groups),
            [me[None]] + final,
            [SMEM] + [VMEM] * len(final),
            [((rows, groups * HD), BF16)] * 2,
        )
        return grad_queries, grad_keys, grad_values

    win = (back + 1) * rows
    win_start = jnp.maximum(me - back, 0) * rows
    part = jnp.concatenate([keep for _, _, keep in outs], axis=3).astype(F32)
    part = part.transpose(0, 2, 1, 3).reshape(prompt + win, 2, groups * HD)
    rear = part[prompt:].reshape(back + 1, rows, 2, groups * HD)[::-1].reshape(win, 2, -1)
    full = jnp.zeros((total, 2, groups * HD), F32).at[:prompt].set(part[:prompt])
    old = lax.dynamic_slice_in_dim(full, win_start, win, 0)
    full = lax.dynamic_update_slice_in_dim(full, old + rear, win_start, 0)
    reduced = lax.psum_scatter(full, "ctx", scatter_dimension=0, tiled=True)
    return (
        grad_queries,
        (reduced[:, 0] * SCALE).astype(BF16),
        reduced[:, 1].astype(BF16),
    )


def solution(mesh):
    placed = (
        P("ctx", "tp"),
        P("ctx"),
        P("tp", None),
        P("ctx", "tp"),
        P("ctx", "tp"),
        P("ctx", "tp"),
        P(),
        P("ctx", None),
    )
    return jax.shard_map(
        shards,
        mesh=mesh,
        in_specs=placed,
        out_specs=(P("ctx", "tp"), P("ctx", "tp"), P("ctx", "tp")),
        check_vma=False,
    )
```

```python
import functools
import math

import jax
import jax.numpy as jnp
from jax import lax
from jax.experimental import pallas as pl
from jax.experimental.pallas import tpu as pltpu
from jax.sharding import PartitionSpec as P

HEADS = 64
KV_HEADS = 8
SHARE = HEADS // KV_HEADS
HD = 128
TILE = 128
ROLLOUTS = 8
JITTER = 64
KB = 256
CHUNK = 1
WB = 512
AHEAD = 2
VMEM_LIMIT = 26 << 20
SCALE = 1.0 / math.sqrt(HD)
LOG2E = 1.4426950408889634
F32 = jnp.float32
BF16 = jnp.bfloat16
NT = (((1,), (1,)), ((), ()))


def dot(a, b):
    return jnp.dot(a, b, preferred_element_type=F32)


def dot_nt(a, b):
    return lax.dot_general(a, b, NT, preferred_element_type=F32)


SMEM = pl.BlockSpec(memory_space=pltpu.SMEM)
VMEM = pl.BlockSpec(memory_space=pltpu.VMEM)
HBM = pl.BlockSpec(memory_space=pltpu.HBM)


def at(start, size):
    return pl.ds(pl.multiple_of(start, size), size)


def call(kernel, ins, in_specs, outs, scratch=(), out_specs=None, flops=0, size=0, exps=0):
    return pl.pallas_call(
        kernel,
        in_specs=in_specs,
        out_specs=out_specs or [VMEM] * len(outs),
        out_shape=[
            out if isinstance(out, pl.MemoryRef) else jax.ShapeDtypeStruct(*out) for out in outs
        ],
        scratch_shapes=list(scratch),
        compiler_params=pltpu.CompilerParams(vmem_limit_bytes=VMEM_LIMIT),
        cost_estimate=pl.CostEstimate(flops=flops, bytes_accessed=size, transcendentals=exps),
    )(*ins)


def join_kernel(k_ref, v_ref, out_ref, sems):
    width = k_ref.shape[1]
    copies = [
        pltpu.make_async_copy(ref, out_ref.at[:, i * width : (i + 1) * width], sems.at[i])
        for i, ref in enumerate((k_ref, v_ref))
    ]
    for copy in copies:
        copy.start()
    for copy in copies:
        copy.wait()


def stack_kernel(*refs):
    for i, ref in enumerate(refs[:-1]):
        refs[-1][i] = ref[...]


def mask_kernel(n_kb, prompt, back, total, me_ref, seg_ref, tile_ref, bias_ref, live_ref):
    rows = bias_ref.shape[2]
    per = rows // KB
    me = me_ref[0]
    row_start = me * rows
    key_at = lax.broadcasted_iota(jnp.int32, (KB, KB), 0)
    query_at = lax.broadcasted_iota(jnp.int32, (KB, KB), 1)
    for kb in range(n_kb):
        window = kb >= prompt // KB
        age, sub = divmod(kb - prompt // KB, per)
        block = jnp.maximum(me - age, 0) * per + sub if window else kb
        key_pos = block * KB + key_at
        seg_k = jnp.broadcast_to(seg_ref[block], (KB, KB)).T
        some = jnp.int32(0)
        for r in range(per):
            same = seg_k == jnp.broadcast_to(seg_ref[me * per + r], (KB, KB))
            for a in range(KB // TILE):
                for b in range(KB // TILE):
                    mark = tile_ref[r * (KB // TILE) + b, block * (KB // TILE) + a]
                    inside = (key_at // TILE == a) & (query_at // TILE == b)
                    same = same | (inside & (jnp.full((KB, KB), mark) == 1))
            seen = same & (key_pos <= row_start + r * KB + query_at)
            if window:
                seen = seen & (key_pos >= prompt) & (jnp.full((KB, KB), me) >= prompt // rows)
            bias_ref[kb, :, r * KB : (r + 1) * KB] = jnp.where(seen, 0.0, -1e30)
            some = jnp.maximum(some, jnp.max(seen.astype(jnp.int32)))
        live_ref[kb] = some


def mask_call(me, segment_ids, tile_mask, rows, n_kb, prompt, back):
    total = segment_ids.shape[0]
    return call(
        functools.partial(mask_kernel, n_kb, prompt, back, total),
        (me[None], segment_ids.reshape(total // KB, 1, KB), tile_mask),
        [SMEM, VMEM, SMEM],
        [((n_kb, KB, rows), F32), ((n_kb,), jnp.int32)],
        out_specs=[VMEM, SMEM],
        size=n_kb * KB * rows * 4,
    )


def probs_kernel(
    n_kb, group, groups, slot_ref, shard_ref, w_ref, q_ref, near_ref, far_ref, bias_ref,
    p_ref, o_ref, k_ref, v_ref, wl_ref,
    ks_ref, vs_ref, kx_ref, vt_ref, s_ref, t_ref, ps_ref, os_ref, ws_ref, sems,
):
    rows = q_ref.shape[0]
    per = rows // KB
    n_near = near_ref.shape[0]
    vt_ref[HD:, :] = jnp.ones((16, n_kb * KB), BF16)
    for kb in range(n_kb):
        slot = slot_ref[kb]
        keys = pl.ds(kb * KB, KB)

        def place(source, index):
            ks_ref[keys, :] = source[index, :, group * HD : (group + 1) * HD]
            vs_ref[keys, :] = source[index, :, (groups + group) * HD : (groups + group + 1) * HD]

        @pl.when(slot < n_near)
        def _():
            place(near_ref, slot)

        @pl.when(slot >= n_near)
        def _():
            place(far_ref, slot - n_near)

    depth = wl_ref.shape[1]
    wide = SHARE * HD
    keep_w = pltpu.make_async_copy(
        w_ref.at[
            pl.ds(group * wide, wide), pl.ds(pl.multiple_of(shard_ref[0] * depth, HD), depth)
        ],
        ws_ref,
        sems.at[10],
    )
    pass_w = pltpu.make_async_copy(ws_ref, wl_ref, sems.at[11])
    keep_w.start()
    keep_k = pltpu.make_async_copy(ks_ref, k_ref, sems.at[8])
    keep_v = pltpu.make_async_copy(vs_ref, v_ref, sems.at[9])
    keep_k.start()
    keep_v.start()
    for kb in range(n_kb):
        keys = pl.ds(kb * KB, KB)
        k = ks_ref[keys, :]
        kx_ref[keys, :HD] = k
        kx_ref[keys, HD:] = k
        vt_ref[:HD, keys] = vs_ref[keys, :].T

    count = SHARE * per

    def score(i, s_ref):
        h, here = i // per, at((i % per) * KB, KB)
        q = q_ref[here, at((group * SHARE + h) * HD, HD)].astype(F32) * (SCALE * LOG2E)
        q_hi = q.astype(BF16)
        q_lo = (q - q_hi.astype(F32)).astype(BF16)
        qx = jnp.concatenate([q_hi, q_lo], axis=1)
        s = dot_nt(kx_ref[...], qx) + bias_ref[:, :, here].reshape(n_kb * KB, KB)
        s_ref[...] = s
        return jnp.max(s, axis=0, keepdims=True)

    def out(j, side):
        at_side = (j % 2) * 2 + side
        i = 2 * j + side
        return (
            pltpu.make_async_copy(ps_ref.at[at_side], p_ref.at[i], sems.at[at_side]),
            pltpu.make_async_copy(os_ref.at[at_side], o_ref.at[i], sems.at[4 + at_side]),
        )

    def soften(j, s_ref, top, side):
        at_side = (j % 2) * 2 + side
        e = jnp.exp2(s_ref[...] - top).astype(BF16)
        ps_ref[at_side] = e
        acc = dot(vt_ref[...], e)
        inv = 1.0 / acc[HD : HD + 1, :]
        os_ref[at_side, :, :HD] = (acc[:HD] * inv).T
        os_ref[at_side, :, HD:] = jnp.broadcast_to(inv, (HD, KB)).T

    def step(j, top):
        @pl.when(j == 1)
        def _():
            keep_w.wait()
            pass_w.start()

        @pl.when(j >= 2)
        def _():
            for copy in out(j - 2, 0) + out(j - 2, 1):
                copy.wait()

        later = score(2 * j + 1, t_ref)
        soften(j, s_ref, top, 0)
        top = score(jnp.minimum(2 * j + 2, count - 1), s_ref)
        soften(j, t_ref, later, 1)
        for copy in out(j, 0) + out(j, 1):
            copy.start()
        return top

    lax.fori_loop(0, count // 2, step, score(0, s_ref))
    for j in range(max(count // 2 - 2, 0), count // 2):
        for copy in out(j, 0) + out(j, 1):
            copy.wait()
    keep_k.wait()
    keep_v.wait()
    pass_w.wait()


def probs_call(group, groups, slots, shard, weight, depth, q, near, far, bias, n_kb):
    rows = q.shape[0]
    keys = n_kb * KB
    blocks = SHARE * rows // KB
    return call(
        functools.partial(probs_kernel, n_kb, group, groups),
        (slots, shard, weight, q, near, far, bias),
        [SMEM, SMEM, HBM] + [VMEM] * 4,
        [
            pltpu.HBM((blocks, keys, KB), BF16),
            pltpu.HBM((blocks, KB, 2 * HD), F32),
            pltpu.HBM((keys, HD), BF16),
            pltpu.HBM((keys, HD), BF16),
            pltpu.HBM((SHARE * HD, depth), BF16),
        ],
        scratch=[
            pltpu.VMEM((keys, HD), BF16),
            pltpu.VMEM((keys, HD), BF16),
            pltpu.VMEM((keys, 2 * HD), BF16),
            pltpu.VMEM((HD + 16, keys), BF16),
            pltpu.VMEM((keys, KB), F32),
            pltpu.VMEM((keys, KB), F32),
            pltpu.VMEM((4, keys, KB), BF16),
            pltpu.VMEM((4, KB, 2 * HD), F32),
            pltpu.VMEM((SHARE * HD, depth), BF16),
            pltpu.SemaphoreType.DMA((12,)),
        ],
        out_specs=[HBM] * 5,
    )


def back_kernel(
    n_kb, n_send, first, live_ref, pos_ref, edge_ref, proj_ref, x1_ref, x2_ref, w_ref, adv_ref,
    o_ref, q_ref, k_ref, v_ref, p_ref,
    dq_ref, send_ref, keep_ref, dox_ref, qs_ref, ds_ref, dqt_ref,
):
    rows = proj_ref.shape[0]
    per = rows // KB
    lane = lax.broadcasted_iota(jnp.int32, (KB, HD), 1)
    minus = jnp.where(lane < 3, -1.0, 0.0).astype(BF16)
    x = choose(edge_ref[0], x1_ref[...], x2_ref[...])
    dqt_ref[...] = jnp.zeros_like(dqt_ref)
    adv = jnp.broadcast_to(adv_ref[...], (HD, rows)).T
    for h in range(SHARE):
        cols = pl.ds((first + h) * HD, HD)
        fresh = dot_nt(x, w_ref[h * HD : (h + 1) * HD, :])
        for r in range(per):
            part = slice(r * KB, (r + 1) * KB)
            here = pl.ds((h * per + r) * KB, KB)
            out = o_ref[h * per + r]
            proj = proj_ref[part, cols] + fresh[part]
            grad = (proj * (adv[part] * out[:, HD:])).astype(BF16)
            delta = jnp.sum(grad.astype(F32) * out[:, :HD], axis=1, keepdims=True)
            one = delta.astype(BF16).astype(F32)
            two = (delta - one).astype(BF16).astype(F32)
            three = delta - one - two
            ext = jnp.where(
                lane == 0, one, jnp.where(lane == 1, two, jnp.where(lane == 2, three, 0.0))
            )
            dox_ref[here, :HD] = grad
            dox_ref[here, HD:] = ext.astype(BF16)
            qs_ref[here, :] = q_ref[part, cols]

    def put(kb, value):
        pos = pos_ref[kb]

        @pl.when(pos < n_send)
        def _():
            send_ref[pos] = value

        @pl.when(pos >= n_send)
        def _():
            keep_ref[pos - n_send] = value

    def chunk(start, count):
        keys = pl.ds(start * KB, count * KB)
        blocks = range(start, start + count)
        live = functools.reduce(jnp.bitwise_or, [live_ref[kb] for kb in blocks])

        @pl.when(live != 0)
        def _():
            vx = jnp.concatenate(
                [v_ref[keys, :], jnp.concatenate([minus] * count, axis=0)], axis=1
            )
            p = jnp.concatenate([p_ref[i, keys, :] for i in range(SHARE * per)], axis=1)
            dv = dot(p, dox_ref[:, :HD])
            for i in range(SHARE * per):
                here = pl.ds(i * KB, KB)
                dp = dot_nt(vx, dox_ref[here, :])
                ds_ref[: count * KB, here] = (p_ref[i, keys, :].astype(F32) * dp).astype(BF16)
            dqt_ref[...] += dot(k_ref[keys, :].T, ds_ref[: count * KB, :])
            dk = dot(ds_ref[: count * KB, :], qs_ref[...])
            for j, kb in enumerate(blocks):
                part = slice(j * KB, (j + 1) * KB)
                put(kb, jnp.stack([dk[part], dv[part]]).astype(BF16))

        @pl.when(live == 0)
        def _():
            for kb in blocks:
                put(kb, jnp.zeros((2, KB, HD), BF16))

    for start in range(0, n_kb, CHUNK):
        chunk(start, min(CHUNK, n_kb - start))
    for h in range(SHARE):
        dq_ref[:, pl.ds(h * HD, HD)] = (
            (dqt_ref[:, h * rows : (h + 1) * rows] * SCALE).T.astype(BF16)
        )


def back_call(group, live, pos, edge, proj, x1, x2, w, adv, o, q, k, v, p, n_kb, n_send):
    rows = q.shape[0]
    return call(
        functools.partial(back_kernel, n_kb, n_send, group * SHARE),
        (live, pos, edge, proj, x1, x2, w, adv, o, q, k, v, p),
        [SMEM] * 3 + [VMEM] * 10,
        [
            ((rows, SHARE * HD), BF16),
            ((max(n_send, 1), 2, KB, HD), BF16),
            ((n_kb - n_send, 2, KB, HD), BF16),
        ],
        scratch=[
            pltpu.VMEM((SHARE * rows, 2 * HD), BF16),
            pltpu.VMEM((SHARE * rows, HD), BF16),
            pltpu.VMEM((CHUNK * KB, SHARE * rows), BF16),
            pltpu.VMEM((HD, SHARE * rows), F32),
        ],
    )


def middle_kernel(me_ref, got_ref, keep_ref, base_ref, x_ref, y_ref, d_ref):
    me = me_ref[0]
    core, side, roll = me & 1, (me >> 1) & 1, me >= 4
    here = keep_ref[side].astype(F32) + got_ref[side].astype(F32)
    there = keep_ref[1 - side].astype(F32) + got_ref[1 - side].astype(F32)
    y_ref[...] = here.astype(BF16)
    d_ref[...] = there.astype(BF16)
    got = got_ref[2].astype(F32)
    late = (jnp.full(got.shape, core) == 1)

    @pl.when(roll)
    def _():
        x_ref[...] = (keep_ref[2].astype(F32) + jnp.where(late, got, 0.0)).astype(BF16)
        base_ref[...] = keep_ref[3].astype(F32) + jnp.where(late, 0.0, got)

    @pl.when(jnp.logical_not(roll))
    def _():
        x_ref[...] = there.astype(BF16)
        base_ref[...] = here


def last_kernel(groups, me_ref, *refs):
    dk_ref, dv_ref = refs[-2:]
    me = jnp.full((2, KB, HD), me_ref[0])
    across, beside = me < 4, me < 6
    for g in range(groups):
        base, x, y, d = refs[4 * g : 4 * g + 4]
        total = base[...] + jnp.where(beside, x[...].astype(F32), 0.0)
        total += jnp.where(across, y[...].astype(F32) + d[...].astype(F32), 0.0)
        dk_ref[:, g * HD : (g + 1) * HD] = (total[0] * SCALE).astype(BF16)
        dv_ref[:, g * HD : (g + 1) * HD] = total[1].astype(BF16)


def choose(flag, first, second):
    return jnp.where(jnp.full(first.shape, flag) != 0, first, second)


def project_kernel(count, added, halves, shard_ref, w_ref, *refs):
    xs, refs = refs[:count], refs[count:]
    if added:
        acc_ref, refs = refs[0], refs[1:]
    values = [x[...] for x in xs]
    if halves:
        values[-1] = choose(shard_ref[count], refs[0][...], values[-1])
        refs = refs[1:]
    out_ref, held_ref, sems = refs
    depth = xs[0].shape[1]
    blocks = w_ref.shape[0] // WB

    def fetch(i, n):
        return pltpu.make_async_copy(
            w_ref.at[pl.ds(n * WB, WB), pl.ds(pl.multiple_of(shard_ref[i] * depth, HD), depth)],
            held_ref.at[i, n],
            sems.at[i, n],
        )

    def start(n):
        for i in range(count):
            fetch(i, n).start()

    for n in range(min(AHEAD, blocks)):
        start(n)
    for n in range(blocks):
        here = slice(n * WB, (n + 1) * WB)
        total = acc_ref[:, here] if added else None
        for i in range(count):
            fetch(i, n).wait()
        if n + AHEAD < blocks:
            start(n + AHEAD)
        for i in range(count):
            part = dot_nt(values[i], held_ref[i, n])
            total = part if total is None else total + part
        out_ref[:, here] = total


def project_call(shards_of, xs, weight, acc=None, rest=None):
    rows, depth = xs[0].shape
    wide = weight.shape[0]
    count = len(xs)
    added, halves = acc is not None, rest is not None
    return call(
        functools.partial(project_kernel, count, added, halves),
        (shards_of, weight, *xs, *([acc] if added else []), *([rest] if halves else [])),
        [SMEM, HBM] + [VMEM] * (count + added + halves),
        [((rows, wide), F32)],
        scratch=[
            pltpu.VMEM((count, wide // WB, WB, depth), BF16),
            pltpu.SemaphoreType.DMA((count, wide // WB)),
        ],
    )[0]


def key_window(tok_rows, total):
    span = (total - total // 2) // ROLLOUTS
    reach = 3 * span + TILE + JITTER
    reach = reach // TILE * TILE
    return -(-reach // tok_rows)


def shards(
    upstream, advantage, out_weight, query_heads, key_heads, value_heads, segment_ids, tile_mask
):
    rows = query_heads.shape[0]
    n_ctx = lax.axis_size("ctx")
    n_tp = lax.axis_size("tp")
    total = rows * n_ctx
    prompt = total // 2
    groups = key_heads.shape[1] // HD
    me = lax.axis_index("ctx").astype(jnp.int32)
    z = lax.axis_index("tp").astype(jnp.int32)
    per = rows // KB
    back = key_window(rows, total)
    prompt_kb = prompt // KB
    n_kb = prompt_kb + (back + 1) * per
    fast = n_ctx == 8 and n_tp == 4 and per == 1 and back == 2
    shape = (rows, 2 * groups * HD)
    own = call(
        join_kernel,
        [pltpu.with_memory_space_constraint(x, pltpu.HBM) for x in (key_heads, value_heads)],
        [HBM] * 2,
        [(shape, BF16)],
        scratch=[pltpu.SemaphoreType.DMA((2,))],
    )[0]
    weight = pltpu.with_memory_space_constraint(out_weight, pltpu.HBM)

    def hop(value, pairs):
        return lax.ppermute(value, "tp", pairs)

    def flip(value, bit):
        return lax.ppermute(value, "ctx", [(i, i ^ bit) for i in range(n_ctx)])

    if fast:
        pieces = [own] + [flip(own, d) for d in (2, 4, 6)]
        near = call(stack_kernel, pieces, [VMEM] * 4, [((4,) + shape, BF16)])[0]
        ends, middle = [(0, 1), (1, 0), (2, 3), (3, 2)], [(1, 2), (2, 1)]
        up_a = hop(upstream, ends)
        up_c = hop(upstream, middle)
    else:
        near = lax.all_gather(own, "ctx", axis=0)
        near = far = near.reshape(n_ctx * per, KB, 2 * groups * HD)

    bias, live = mask_call(me, segment_ids, tile_mask, rows, n_kb, prompt, back)
    block = jnp.arange(n_kb, dtype=jnp.int32)
    holder = jnp.where(
        block < prompt_kb,
        block // per,
        jnp.where(me * rows >= prompt, me - (block - prompt_kb) // per, me),
    )
    if fast:
        away = holder ^ me
        slots = away // 2 + (away % 2) * 4
        core = me & 1
        pos = jnp.where(
            block < 4,
            jnp.where(block % 2 == core, 3 + block // 2, block // 2),
            jnp.array([0, 0, 0, 0, 6, 2, 5], jnp.int32),
        )
        n_send = 3
        half, edge = z // 2, (z % 3 == 0).astype(jnp.int32)
        second, shard = 2 - half, 3 - 3 * half
        acc = project_call(z[None], [upstream], weight)
    else:
        slots = holder * per + block % per
        pos = block
        n_send = 0
        whole = lax.all_gather(upstream, "tp", axis=0)
        shard = z
        acc = jnp.zeros((rows, out_weight.shape[0]), F32)
        for i in range(n_tp - 1):
            other = (z + 1 + i) % n_tp
            x = lax.dynamic_index_in_dim(whole, other, 0, keepdims=False)
            acc = project_call(other[None], [x], weight, acc)
        x1, x2, edge = upstream, upstream, jnp.int32(1)

    slots = slots.astype(jnp.int32)
    depth = upstream.shape[1]
    if fast:
        up_a, up_c, bias, acc = lax.optimization_barrier((up_a, up_c, bias, acc))
        up_e = hop(up_a, middle)
        up_f = hop(up_c, ends)
        near, up_a = lax.optimization_barrier((near, up_a))
        far = flip(near, 1)
    soft = [list(probs_call(0, groups, slots, shard[None], weight, depth, query_heads, near, far, bias, n_kb))]
    if fast:
        up_e, soft[0][2] = lax.optimization_barrier((up_e, soft[0][2]))
        up_d = hop(up_e, ends)
        x1, x2 = up_d, up_e
    soft += [
        list(probs_call(g, groups, slots, shard[None], weight, depth, query_heads, near, far, bias, n_kb))
        for g in range(1, groups)
    ]
    if fast:
        acc, soft[-1][2] = lax.optimization_barrier((acc, soft[-1][2]))
        acc = project_call(jnp.stack([z ^ 1, second, edge]), [up_a, up_c], weight, acc, up_f)
    outs = []
    for g in range(groups):
        probs, attn, keys, values, w_last = soft[g]
        outs.append(
            back_call(
                g, live, pos.astype(jnp.int32), edge[None], acc, x1, x2, w_last, advantage[None, :], attn,
                query_heads, keys, values, probs, n_kb, n_send,
            )
        )
    grad_queries = jnp.concatenate([dq for dq, _, _ in outs], axis=1)

    if fast:
        final = []
        shape = (2, KB, HD)
        for _, send, keep in outs:
            base, to_x, to_y, to_d = call(
                middle_kernel,
                (me[None], flip(send, 1), keep),
                [SMEM, VMEM, VMEM],
                [(shape, F32), (shape, BF16), (shape, BF16), (shape, BF16)],
            )
            by_y = flip(to_y, 4)
            by_d = flip(to_d, 6)
            by_x = flip(to_x, 2)
            final += [base, by_x, by_y, by_d]
        grad_keys, grad_values = call(
            functools.partial(last_kernel, groups),
            [me[None]] + final,
            [SMEM] + [VMEM] * len(final),
            [((rows, groups * HD), BF16)] * 2,
        )
        return grad_queries, grad_keys, grad_values

    win = (back + 1) * rows
    win_start = jnp.maximum(me - back, 0) * rows
    part = jnp.concatenate([keep for _, _, keep in outs], axis=3).astype(F32)
    part = part.transpose(0, 2, 1, 3).reshape(prompt + win, 2, groups * HD)
    rear = part[prompt:].reshape(back + 1, rows, 2, groups * HD)[::-1].reshape(win, 2, -1)
    full = jnp.zeros((total, 2, groups * HD), F32).at[:prompt].set(part[:prompt])
    old = lax.dynamic_slice_in_dim(full, win_start, win, 0)
    full = lax.dynamic_update_slice_in_dim(full, old + rear, win_start, 0)
    reduced = lax.psum_scatter(full, "ctx", scatter_dimension=0, tiled=True)
    return (
        grad_queries,
        (reduced[:, 0] * SCALE).astype(BF16),
        reduced[:, 1].astype(BF16),
    )


def solution(mesh):
    placed = (
        P("ctx", "tp"),
        P("ctx"),
        P("tp", None),
        P("ctx", "tp"),
        P("ctx", "tp"),
        P("ctx", "tp"),
        P(),
        P("ctx", None),
    )
    return jax.shard_map(
        shards,
        mesh=mesh,
        in_specs=placed,
        out_specs=(P("ctx", "tp"), P("ctx", "tp"), P("ctx", "tp")),
        check_vma=False,
    )
```

```python
import functools
import math

import jax
import jax.numpy as jnp
from jax import lax
from jax.experimental import pallas as pl
from jax.experimental.pallas import tpu as pltpu
from jax.sharding import PartitionSpec as P

HEADS = 64
KV_HEADS = 8
SHARE = HEADS // KV_HEADS
HD = 128
TILE = 128
ROLLOUTS = 8
JITTER = 64
KB = 256
CHUNK = 1
WB = 512
AHEAD = 2
VMEM_LIMIT = 26 << 20
SCALE = 1.0 / math.sqrt(HD)
LOG2E = 1.4426950408889634
F32 = jnp.float32
BF16 = jnp.bfloat16
NT = (((1,), (1,)), ((), ()))


def dot(a, b):
    return jnp.dot(a, b, preferred_element_type=F32)


def dot_nt(a, b):
    return lax.dot_general(a, b, NT, preferred_element_type=F32)


SMEM = pl.BlockSpec(memory_space=pltpu.SMEM)
VMEM = pl.BlockSpec(memory_space=pltpu.VMEM)
HBM = pl.BlockSpec(memory_space=pltpu.HBM)


def at(start, size):
    return pl.ds(pl.multiple_of(start, size), size)


def call(kernel, ins, in_specs, outs, scratch=(), out_specs=None, flops=0, size=0, exps=0):
    return pl.pallas_call(
        kernel,
        in_specs=in_specs,
        out_specs=out_specs or [VMEM] * len(outs),
        out_shape=[
            out if isinstance(out, pl.MemoryRef) else jax.ShapeDtypeStruct(*out) for out in outs
        ],
        scratch_shapes=list(scratch),
        compiler_params=pltpu.CompilerParams(vmem_limit_bytes=VMEM_LIMIT),
        cost_estimate=pl.CostEstimate(flops=flops, bytes_accessed=size, transcendentals=exps),
    )(*ins)


def join_kernel(k_ref, v_ref, out_ref, sems):
    width = k_ref.shape[1]
    copies = [
        pltpu.make_async_copy(ref, out_ref.at[:, i * width : (i + 1) * width], sems.at[i])
        for i, ref in enumerate((k_ref, v_ref))
    ]
    for copy in copies:
        copy.start()
    for copy in copies:
        copy.wait()


def stack_kernel(*refs):
    for i, ref in enumerate(refs[:-1]):
        refs[-1][i] = ref[...]


def mask_kernel(n_kb, prompt, back, total, me_ref, seg_ref, tile_ref, bias_ref, live_ref):
    rows = bias_ref.shape[2]
    per = rows // KB
    me = me_ref[0]
    row_start = me * rows
    key_at = lax.broadcasted_iota(jnp.int32, (KB, KB), 0)
    query_at = lax.broadcasted_iota(jnp.int32, (KB, KB), 1)
    for kb in range(n_kb):
        window = kb >= prompt // KB
        age, sub = divmod(kb - prompt // KB, per)
        block = jnp.maximum(me - age, 0) * per + sub if window else kb
        key_pos = block * KB + key_at
        seg_k = jnp.broadcast_to(seg_ref[block], (KB, KB)).T
        some = jnp.int32(0)
        for r in range(per):
            same = seg_k == jnp.broadcast_to(seg_ref[me * per + r], (KB, KB))
            for a in range(KB // TILE):
                for b in range(KB // TILE):
                    mark = tile_ref[r * (KB // TILE) + b, block * (KB // TILE) + a]
                    inside = (key_at // TILE == a) & (query_at // TILE == b)
                    same = same | (inside & (jnp.full((KB, KB), mark) == 1))
            seen = same & (key_pos <= row_start + r * KB + query_at)
            if window:
                seen = seen & (key_pos >= prompt) & (jnp.full((KB, KB), me) >= prompt // rows)
            bias_ref[kb, :, r * KB : (r + 1) * KB] = jnp.where(seen, 0.0, -1e30)
            some = jnp.maximum(some, jnp.max(seen.astype(jnp.int32)))
        live_ref[kb] = some


def mask_call(me, segment_ids, tile_mask, rows, n_kb, prompt, back):
    total = segment_ids.shape[0]
    return call(
        functools.partial(mask_kernel, n_kb, prompt, back, total),
        (me[None], segment_ids.reshape(total // KB, 1, KB), tile_mask),
        [SMEM, VMEM, SMEM],
        [((n_kb, KB, rows), F32), ((n_kb,), jnp.int32)],
        out_specs=[VMEM, SMEM],
        size=n_kb * KB * rows * 4,
    )


def probs_kernel(
    n_kb, group, groups, slot_ref, shard_ref, w_ref, q_ref, near_ref, far_ref, bias_ref,
    p_ref, o_ref, k_ref, v_ref, wl_ref,
    ks_ref, vs_ref, kx_ref, vt_ref, s_ref, t_ref, ps_ref, os_ref, ws_ref, sems,
):
    rows = q_ref.shape[0]
    per = rows // KB
    n_near = near_ref.shape[0]
    vt_ref[HD:, :] = jnp.ones((16, n_kb * KB), BF16)
    for kb in range(n_kb):
        slot = slot_ref[kb]
        keys = pl.ds(kb * KB, KB)

        def place(source, index):
            ks_ref[keys, :] = source[index, :, group * HD : (group + 1) * HD]
            vs_ref[keys, :] = source[index, :, (groups + group) * HD : (groups + group + 1) * HD]

        @pl.when(slot < n_near)
        def _():
            place(near_ref, slot)

        @pl.when(slot >= n_near)
        def _():
            place(far_ref, slot - n_near)

    depth = wl_ref.shape[1]
    wide = SHARE * HD
    keep_w = pltpu.make_async_copy(
        w_ref.at[
            pl.ds(group * wide, wide), pl.ds(pl.multiple_of(shard_ref[0] * depth, HD), depth)
        ],
        ws_ref,
        sems.at[10],
    )
    pass_w = pltpu.make_async_copy(ws_ref, wl_ref, sems.at[11])
    keep_w.start()
    keep_k = pltpu.make_async_copy(ks_ref, k_ref, sems.at[8])
    keep_v = pltpu.make_async_copy(vs_ref, v_ref, sems.at[9])
    keep_k.start()
    keep_v.start()
    for kb in range(n_kb):
        keys = pl.ds(kb * KB, KB)
        k = ks_ref[keys, :]
        kx_ref[keys, :HD] = k
        kx_ref[keys, HD:] = k
        vt_ref[:HD, keys] = vs_ref[keys, :].T

    count = SHARE * per

    def score(i, s_ref):
        h, here = i // per, at((i % per) * KB, KB)
        q = q_ref[here, at((group * SHARE + h) * HD, HD)].astype(F32) * (SCALE * LOG2E)
        q_hi = q.astype(BF16)
        q_lo = (q - q_hi.astype(F32)).astype(BF16)
        qx = jnp.concatenate([q_hi, q_lo], axis=1)
        s = dot_nt(kx_ref[...], qx) + bias_ref[:, :, here].reshape(n_kb * KB, KB)
        s_ref[...] = s
        return jnp.max(s, axis=0, keepdims=True)

    def out(j, side):
        at_side = (j % 2) * 2 + side
        i = 2 * j + side
        return (
            pltpu.make_async_copy(ps_ref.at[at_side], p_ref.at[i], sems.at[at_side]),
            pltpu.make_async_copy(os_ref.at[at_side], o_ref.at[i], sems.at[4 + at_side]),
        )

    def soften(j, s_ref, top, side):
        at_side = (j % 2) * 2 + side
        e = jnp.exp2(s_ref[...] - top).astype(BF16)
        ps_ref[at_side] = e
        acc = dot(vt_ref[...], e)
        inv = 1.0 / acc[HD : HD + 1, :]
        os_ref[at_side, :, :HD] = (acc[:HD] * inv).T
        os_ref[at_side, :, HD:] = jnp.broadcast_to(inv, (HD, KB)).T

    def step(j, top):
        @pl.when(j == 1)
        def _():
            keep_w.wait()
            pass_w.start()

        @pl.when(j >= 2)
        def _():
            for copy in out(j - 2, 0) + out(j - 2, 1):
                copy.wait()

        later = score(2 * j + 1, t_ref)
        soften(j, s_ref, top, 0)
        top = score(jnp.minimum(2 * j + 2, count - 1), s_ref)
        soften(j, t_ref, later, 1)
        for copy in out(j, 0) + out(j, 1):
            copy.start()
        return top

    lax.fori_loop(0, count // 2, step, score(0, s_ref))
    for j in range(max(count // 2 - 2, 0), count // 2):
        for copy in out(j, 0) + out(j, 1):
            copy.wait()
    keep_k.wait()
    keep_v.wait()
    pass_w.wait()


def probs_call(group, groups, slots, shard, weight, depth, q, near, far, bias, n_kb):
    rows = q.shape[0]
    keys = n_kb * KB
    blocks = SHARE * rows // KB
    return call(
        functools.partial(probs_kernel, n_kb, group, groups),
        (slots, shard, weight, q, near, far, bias),
        [SMEM, SMEM, HBM] + [VMEM] * 4,
        [
            pltpu.HBM((blocks, keys, KB), BF16),
            pltpu.HBM((blocks, KB, 2 * HD), F32),
            pltpu.HBM((keys, HD), BF16),
            pltpu.HBM((keys, HD), BF16),
            pltpu.HBM((SHARE * HD, depth), BF16),
        ],
        scratch=[
            pltpu.VMEM((keys, HD), BF16),
            pltpu.VMEM((keys, HD), BF16),
            pltpu.VMEM((keys, 2 * HD), BF16),
            pltpu.VMEM((HD + 16, keys), BF16),
            pltpu.VMEM((keys, KB), F32),
            pltpu.VMEM((keys, KB), F32),
            pltpu.VMEM((4, keys, KB), BF16),
            pltpu.VMEM((4, KB, 2 * HD), F32),
            pltpu.VMEM((SHARE * HD, depth), BF16),
            pltpu.SemaphoreType.DMA((12,)),
        ],
        out_specs=[HBM] * 5,
    )


def back_kernel(
    n_kb, n_send, first, live_ref, pos_ref, edge_ref, proj_ref, x1_ref, x2_ref, w_ref, adv_ref,
    o_ref, q_ref, k_ref, v_ref, p_ref,
    dq_ref, send_ref, keep_ref, dox_ref, qs_ref, ds_ref, dqt_ref,
):
    rows = proj_ref.shape[0]
    per = rows // KB
    lane = lax.broadcasted_iota(jnp.int32, (KB, HD), 1)
    minus = jnp.where(lane < 3, -1.0, 0.0).astype(BF16)
    x = choose(edge_ref[0], x1_ref[...], x2_ref[...])
    dqt_ref[...] = jnp.zeros_like(dqt_ref)
    adv = jnp.broadcast_to(adv_ref[...], (HD, rows)).T
    for h in range(SHARE):
        cols = pl.ds((first + h) * HD, HD)
        fresh = dot_nt(x, w_ref[h * HD : (h + 1) * HD, :])
        for r in range(per):
            part = slice(r * KB, (r + 1) * KB)
            here = pl.ds((h * per + r) * KB, KB)
            out = o_ref[h * per + r]
            proj = proj_ref[part, cols] + fresh[part]
            grad = (proj * (adv[part] * out[:, HD:])).astype(BF16)
            delta = jnp.sum(grad.astype(F32) * out[:, :HD], axis=1, keepdims=True)
            one = delta.astype(BF16).astype(F32)
            two = (delta - one).astype(BF16).astype(F32)
            three = delta - one - two
            ext = jnp.where(
                lane == 0, one, jnp.where(lane == 1, two, jnp.where(lane == 2, three, 0.0))
            )
            dox_ref[here, :HD] = grad
            dox_ref[here, HD:] = ext.astype(BF16)
            qs_ref[here, :] = q_ref[part, cols]

    def put(kb, value):
        pos = pos_ref[kb]

        @pl.when(pos < n_send)
        def _():
            send_ref[pos] = value

        @pl.when(pos >= n_send)
        def _():
            keep_ref[pos - n_send] = value

    def chunk(start, count):
        keys = pl.ds(start * KB, count * KB)
        blocks = range(start, start + count)
        live = functools.reduce(jnp.bitwise_or, [live_ref[kb] for kb in blocks])

        @pl.when(live != 0)
        def _():
            vx = jnp.concatenate(
                [v_ref[keys, :], jnp.concatenate([minus] * count, axis=0)], axis=1
            )
            p = jnp.concatenate([p_ref[i, keys, :] for i in range(SHARE * per)], axis=1)
            dv = dot(p, dox_ref[:, :HD])
            for i in range(SHARE * per):
                here = pl.ds(i * KB, KB)
                dp = dot_nt(vx, dox_ref[here, :])
                ds_ref[: count * KB, here] = (p_ref[i, keys, :].astype(F32) * dp).astype(BF16)
            dqt_ref[...] += dot(k_ref[keys, :].T, ds_ref[: count * KB, :])
            dk = dot(ds_ref[: count * KB, :], qs_ref[...])
            for j, kb in enumerate(blocks):
                part = slice(j * KB, (j + 1) * KB)
                put(kb, jnp.stack([dk[part], dv[part]]).astype(BF16))

        @pl.when(live == 0)
        def _():
            for kb in blocks:
                put(kb, jnp.zeros((2, KB, HD), BF16))

    for start in range(0, n_kb, CHUNK):
        chunk(start, min(CHUNK, n_kb - start))
    for h in range(SHARE):
        dq_ref[:, pl.ds(h * HD, HD)] = (
            (dqt_ref[:, h * rows : (h + 1) * rows] * SCALE).T.astype(BF16)
        )


def back_call(group, live, pos, edge, proj, x1, x2, w, adv, o, q, k, v, p, n_kb, n_send):
    rows = q.shape[0]
    return call(
        functools.partial(back_kernel, n_kb, n_send, group * SHARE),
        (live, pos, edge, proj, x1, x2, w, adv, o, q, k, v, p),
        [SMEM] * 3 + [VMEM] * 10,
        [
            ((rows, SHARE * HD), BF16),
            ((max(n_send, 1), 2, KB, HD), BF16),
            ((n_kb - n_send, 2, KB, HD), BF16),
        ],
        scratch=[
            pltpu.VMEM((SHARE * rows, 2 * HD), BF16),
            pltpu.VMEM((SHARE * rows, HD), BF16),
            pltpu.VMEM((CHUNK * KB, SHARE * rows), BF16),
            pltpu.VMEM((HD, SHARE * rows), F32),
        ],
    )


def middle_kernel(me_ref, got_ref, keep_ref, base_ref, x_ref, y_ref, d_ref):
    me = me_ref[0]
    core, side, roll = me & 1, (me >> 1) & 1, me >= 4
    here = keep_ref[side].astype(F32) + got_ref[side].astype(F32)
    there = keep_ref[1 - side].astype(F32) + got_ref[1 - side].astype(F32)
    y_ref[...] = here.astype(BF16)
    d_ref[...] = there.astype(BF16)
    got = got_ref[2].astype(F32)
    late = (jnp.full(got.shape, core) == 1)

    @pl.when(roll)
    def _():
        x_ref[...] = (keep_ref[2].astype(F32) + jnp.where(late, got, 0.0)).astype(BF16)
        base_ref[...] = keep_ref[3].astype(F32) + jnp.where(late, 0.0, got)

    @pl.when(jnp.logical_not(roll))
    def _():
        x_ref[...] = there.astype(BF16)
        base_ref[...] = here


def last_kernel(groups, me_ref, *refs):
    dk_ref, dv_ref = refs[-2:]
    me = jnp.full((2, KB, HD), me_ref[0])
    across, beside = me < 4, me < 6
    for g in range(groups):
        base, x, y, d = refs[4 * g : 4 * g + 4]
        total = base[...] + jnp.where(beside, x[...].astype(F32), 0.0)
        total += jnp.where(across, y[...].astype(F32) + d[...].astype(F32), 0.0)
        dk_ref[:, g * HD : (g + 1) * HD] = (total[0] * SCALE).astype(BF16)
        dv_ref[:, g * HD : (g + 1) * HD] = total[1].astype(BF16)


def choose(flag, first, second):
    return jnp.where(jnp.full(first.shape, flag) != 0, first, second)


def project_kernel(count, added, halves, shard_ref, w_ref, *refs):
    xs, refs = refs[:count], refs[count:]
    if added:
        acc_ref, refs = refs[0], refs[1:]
    values = [x[...] for x in xs]
    if halves:
        values[-1] = choose(shard_ref[count], refs[0][...], values[-1])
        refs = refs[1:]
    out_ref, held_ref, sems = refs
    depth = xs[0].shape[1]
    blocks = w_ref.shape[0] // WB

    def fetch(i, n):
        return pltpu.make_async_copy(
            w_ref.at[pl.ds(n * WB, WB), pl.ds(pl.multiple_of(shard_ref[i] * depth, HD), depth)],
            held_ref.at[i, n],
            sems.at[i, n],
        )

    def start(n):
        for i in range(count):
            fetch(i, n).start()

    for n in range(min(AHEAD, blocks)):
        start(n)
    for n in range(blocks):
        here = slice(n * WB, (n + 1) * WB)
        total = acc_ref[:, here] if added else None
        for i in range(count):
            fetch(i, n).wait()
        if n + AHEAD < blocks:
            start(n + AHEAD)
        for i in range(count):
            part = dot_nt(values[i], held_ref[i, n])
            total = part if total is None else total + part
        out_ref[:, here] = total


def project_call(shards_of, xs, weight, acc=None, rest=None):
    rows, depth = xs[0].shape
    wide = weight.shape[0]
    count = len(xs)
    added, halves = acc is not None, rest is not None
    return call(
        functools.partial(project_kernel, count, added, halves),
        (shards_of, weight, *xs, *([acc] if added else []), *([rest] if halves else [])),
        [SMEM, HBM] + [VMEM] * (count + added + halves),
        [((rows, wide), F32)],
        scratch=[
            pltpu.VMEM((count, wide // WB, WB, depth), BF16),
            pltpu.SemaphoreType.DMA((count, wide // WB)),
        ],
    )[0]


def key_window(tok_rows, total):
    span = (total - total // 2) // ROLLOUTS
    reach = 3 * span + TILE + JITTER
    reach = reach // TILE * TILE
    return -(-reach // tok_rows)


def shards(
    upstream, advantage, out_weight, query_heads, key_heads, value_heads, segment_ids, tile_mask
):
    rows = query_heads.shape[0]
    n_ctx = lax.axis_size("ctx")
    n_tp = lax.axis_size("tp")
    total = rows * n_ctx
    prompt = total // 2
    groups = key_heads.shape[1] // HD
    me = lax.axis_index("ctx").astype(jnp.int32)
    z = lax.axis_index("tp").astype(jnp.int32)
    per = rows // KB
    back = key_window(rows, total)
    prompt_kb = prompt // KB
    n_kb = prompt_kb + (back + 1) * per
    fast = n_ctx == 8 and n_tp == 4 and per == 1 and back == 2
    shape = (rows, 2 * groups * HD)
    own = call(
        join_kernel,
        [pltpu.with_memory_space_constraint(x, pltpu.HBM) for x in (key_heads, value_heads)],
        [HBM] * 2,
        [(shape, BF16)],
        scratch=[pltpu.SemaphoreType.DMA((2,))],
    )[0]
    weight = pltpu.with_memory_space_constraint(out_weight, pltpu.HBM)

    def hop(value, pairs):
        return lax.ppermute(value, "tp", pairs)

    def flip(value, bit):
        return lax.ppermute(value, "ctx", [(i, i ^ bit) for i in range(n_ctx)])

    if fast:
        pieces = [own] + [flip(own, d) for d in (2, 4, 6)]
        near = call(stack_kernel, pieces, [VMEM] * 4, [((4,) + shape, BF16)])[0]
        ends, middle, out = [(0, 1), (1, 0), (2, 3), (3, 2)], [(1, 2), (2, 1)], [(1, 0), (2, 3)]
        up_a = hop(upstream, ends)
        up_c = hop(upstream, middle)
    else:
        near = lax.all_gather(own, "ctx", axis=0)
        near = far = near.reshape(n_ctx * per, KB, 2 * groups * HD)

    bias, live = mask_call(me, segment_ids, tile_mask, rows, n_kb, prompt, back)
    block = jnp.arange(n_kb, dtype=jnp.int32)
    holder = jnp.where(
        block < prompt_kb,
        block // per,
        jnp.where(me * rows >= prompt, me - (block - prompt_kb) // per, me),
    )
    if fast:
        away = holder ^ me
        slots = away // 2 + (away % 2) * 4
        core = me & 1
        pos = jnp.where(
            block < 4,
            jnp.where(block % 2 == core, 3 + block // 2, block // 2),
            jnp.array([0, 0, 0, 0, 6, 2, 5], jnp.int32),
        )
        n_send = 3
        half, edge = z // 2, (z % 3 == 0).astype(jnp.int32)
        second, shard = 2 - half, 3 - 3 * half
        acc = project_call(z[None], [upstream], weight)
    else:
        slots = holder * per + block % per
        pos = block
        n_send = 0
        whole = lax.all_gather(upstream, "tp", axis=0)
        shard = z
        acc = jnp.zeros((rows, out_weight.shape[0]), F32)
        for i in range(n_tp - 1):
            other = (z + 1 + i) % n_tp
            x = lax.dynamic_index_in_dim(whole, other, 0, keepdims=False)
            acc = project_call(other[None], [x], weight, acc)
        x1, x2, edge = upstream, upstream, jnp.int32(1)

    slots = slots.astype(jnp.int32)
    depth = upstream.shape[1]
    if fast:
        up_a, up_c, bias, acc = lax.optimization_barrier((up_a, up_c, bias, acc))
        up_e = hop(up_a, middle)
        up_f = hop(up_c, out)
        near, up_a = lax.optimization_barrier((near, up_a))
        far = flip(near, 1)
    soft = [list(probs_call(0, groups, slots, shard[None], weight, depth, query_heads, near, far, bias, n_kb))]
    if fast:
        up_e, soft[0][2] = lax.optimization_barrier((up_e, soft[0][2]))
        up_d = hop(up_e, out)
        x1, x2 = up_d, up_e
    soft += [
        list(probs_call(g, groups, slots, shard[None], weight, depth, query_heads, near, far, bias, n_kb))
        for g in range(1, groups)
    ]
    if fast:
        acc, soft[-1][2] = lax.optimization_barrier((acc, soft[-1][2]))
        acc = project_call(jnp.stack([z ^ 1, second, edge]), [up_a, up_c], weight, acc, up_f)
    outs = []
    for g in range(groups):
        probs, attn, keys, values, w_last = soft[g]
        outs.append(
            back_call(
                g, live, pos.astype(jnp.int32), edge[None], acc, x1, x2, w_last, advantage[None, :], attn,
                query_heads, keys, values, probs, n_kb, n_send,
            )
        )
    grad_queries = jnp.concatenate([dq for dq, _, _ in outs], axis=1)

    if fast:
        final = []
        shape = (2, KB, HD)
        for _, send, keep in outs:
            base, to_x, to_y, to_d = call(
                middle_kernel,
                (me[None], flip(send, 1), keep),
                [SMEM, VMEM, VMEM],
                [(shape, F32), (shape, BF16), (shape, BF16), (shape, BF16)],
            )
            by_y = flip(to_y, 4)
            by_d = flip(to_d, 6)
            by_x = flip(to_x, 2)
            final += [base, by_x, by_y, by_d]
        grad_keys, grad_values = call(
            functools.partial(last_kernel, groups),
            [me[None]] + final,
            [SMEM] + [VMEM] * len(final),
            [((rows, groups * HD), BF16)] * 2,
        )
        return grad_queries, grad_keys, grad_values

    win = (back + 1) * rows
    win_start = jnp.maximum(me - back, 0) * rows
    part = jnp.concatenate([keep for _, _, keep in outs], axis=3).astype(F32)
    part = part.transpose(0, 2, 1, 3).reshape(prompt + win, 2, groups * HD)
    rear = part[prompt:].reshape(back + 1, rows, 2, groups * HD)[::-1].reshape(win, 2, -1)
    full = jnp.zeros((total, 2, groups * HD), F32).at[:prompt].set(part[:prompt])
    old = lax.dynamic_slice_in_dim(full, win_start, win, 0)
    full = lax.dynamic_update_slice_in_dim(full, old + rear, win_start, 0)
    reduced = lax.psum_scatter(full, "ctx", scatter_dimension=0, tiled=True)
    return (
        grad_queries,
        (reduced[:, 0] * SCALE).astype(BF16),
        reduced[:, 1].astype(BF16),
    )


def solution(mesh):
    placed = (
        P("ctx", "tp"),
        P("ctx"),
        P("tp", None),
        P("ctx", "tp"),
        P("ctx", "tp"),
        P("ctx", "tp"),
        P(),
        P("ctx", None),
    )
    return jax.shard_map(
        shards,
        mesh=mesh,
        in_specs=placed,
        out_specs=(P("ctx", "tp"), P("ctx", "tp"), P("ctx", "tp")),
        check_vma=False,
    )
```

```python
import functools
import math

import jax
import jax.numpy as jnp
from jax import lax
from jax.experimental import pallas as pl
from jax.experimental.pallas import tpu as pltpu
from jax.sharding import PartitionSpec as P

HEADS = 64
KV_HEADS = 8
SHARE = HEADS // KV_HEADS
HD = 128
TILE = 128
ROLLOUTS = 8
JITTER = 64
KB = 256
CHUNK = 1
WB = 512
AHEAD = 2
VMEM_LIMIT = 26 << 20
SCALE = 1.0 / math.sqrt(HD)
LOG2E = 1.4426950408889634
F32 = jnp.float32
BF16 = jnp.bfloat16
NT = (((1,), (1,)), ((), ()))


def dot(a, b):
    return jnp.dot(a, b, preferred_element_type=F32)


def dot_nt(a, b):
    return lax.dot_general(a, b, NT, preferred_element_type=F32)


SMEM = pl.BlockSpec(memory_space=pltpu.SMEM)
VMEM = pl.BlockSpec(memory_space=pltpu.VMEM)
HBM = pl.BlockSpec(memory_space=pltpu.HBM)


def at(start, size):
    return pl.ds(pl.multiple_of(start, size), size)


def call(kernel, ins, in_specs, outs, scratch=(), out_specs=None, flops=0, size=0, exps=0):
    return pl.pallas_call(
        kernel,
        in_specs=in_specs,
        out_specs=out_specs or [VMEM] * len(outs),
        out_shape=[
            out if isinstance(out, pl.MemoryRef) else jax.ShapeDtypeStruct(*out) for out in outs
        ],
        scratch_shapes=list(scratch),
        compiler_params=pltpu.CompilerParams(vmem_limit_bytes=VMEM_LIMIT),
        cost_estimate=pl.CostEstimate(flops=flops, bytes_accessed=size, transcendentals=exps),
    )(*ins)


def join_kernel(k_ref, v_ref, out_ref, sems):
    width = k_ref.shape[1]
    copies = [
        pltpu.make_async_copy(ref, out_ref.at[:, i * width : (i + 1) * width], sems.at[i])
        for i, ref in enumerate((k_ref, v_ref))
    ]
    for copy in copies:
        copy.start()
    for copy in copies:
        copy.wait()


def stack_kernel(*refs):
    for i, ref in enumerate(refs[:-1]):
        refs[-1][i] = ref[...]


def mask_kernel(n_kb, prompt, back, total, me_ref, seg_ref, tile_ref, bias_ref, live_ref):
    rows = bias_ref.shape[2]
    per = rows // KB
    me = me_ref[0]
    row_start = me * rows
    key_at = lax.broadcasted_iota(jnp.int32, (KB, KB), 0)
    query_at = lax.broadcasted_iota(jnp.int32, (KB, KB), 1)
    for kb in range(n_kb):
        window = kb >= prompt // KB
        age, sub = divmod(kb - prompt // KB, per)
        block = jnp.maximum(me - age, 0) * per + sub if window else kb
        key_pos = block * KB + key_at
        seg_k = jnp.broadcast_to(seg_ref[block], (KB, KB)).T
        some = jnp.int32(0)
        for r in range(per):
            same = seg_k == jnp.broadcast_to(seg_ref[me * per + r], (KB, KB))
            for a in range(KB // TILE):
                for b in range(KB // TILE):
                    mark = tile_ref[r * (KB // TILE) + b, block * (KB // TILE) + a]
                    inside = (key_at // TILE == a) & (query_at // TILE == b)
                    same = same | (inside & (jnp.full((KB, KB), mark) == 1))
            seen = same & (key_pos <= row_start + r * KB + query_at)
            if window:
                seen = seen & (key_pos >= prompt) & (jnp.full((KB, KB), me) >= prompt // rows)
            bias_ref[kb, :, r * KB : (r + 1) * KB] = jnp.where(seen, 0.0, -1e30)
            some = jnp.maximum(some, jnp.max(seen.astype(jnp.int32)))
        live_ref[kb] = some


def mask_call(me, segment_ids, tile_mask, rows, n_kb, prompt, back):
    total = segment_ids.shape[0]
    return call(
        functools.partial(mask_kernel, n_kb, prompt, back, total),
        (me[None], segment_ids.reshape(total // KB, 1, KB), tile_mask),
        [SMEM, VMEM, SMEM],
        [((n_kb, KB, rows), F32), ((n_kb,), jnp.int32)],
        out_specs=[VMEM, SMEM],
        size=n_kb * KB * rows * 4,
    )


def probs_kernel(
    n_kb, group, groups, slot_ref, shard_ref, w_ref, q_ref, near_ref, far_ref, bias_ref,
    p_ref, o_ref, k_ref, v_ref, wl_ref,
    ks_ref, vs_ref, kx_ref, vt_ref, s_ref, t_ref, ps_ref, os_ref, ws_ref, sems,
):
    rows = q_ref.shape[0]
    per = rows // KB
    n_near = near_ref.shape[0]
    vt_ref[HD:, :] = jnp.ones((16, n_kb * KB), BF16)
    for kb in range(n_kb):
        slot = slot_ref[kb]
        keys = pl.ds(kb * KB, KB)

        def place(source, index):
            ks_ref[keys, :] = source[index, :, group * HD : (group + 1) * HD]
            vs_ref[keys, :] = source[index, :, (groups + group) * HD : (groups + group + 1) * HD]

        @pl.when(slot < n_near)
        def _():
            place(near_ref, slot)

        @pl.when(slot >= n_near)
        def _():
            place(far_ref, slot - n_near)

    depth = wl_ref.shape[1]
    wide = SHARE * HD
    keep_w = pltpu.make_async_copy(
        w_ref.at[
            pl.ds(group * wide, wide), pl.ds(pl.multiple_of(shard_ref[0] * depth, HD), depth)
        ],
        ws_ref,
        sems.at[10],
    )
    pass_w = pltpu.make_async_copy(ws_ref, wl_ref, sems.at[11])
    keep_w.start()
    keep_k = pltpu.make_async_copy(ks_ref, k_ref, sems.at[8])
    keep_v = pltpu.make_async_copy(vs_ref, v_ref, sems.at[9])
    keep_k.start()
    keep_v.start()
    for kb in range(n_kb):
        keys = pl.ds(kb * KB, KB)
        k = ks_ref[keys, :]
        kx_ref[keys, :HD] = k
        kx_ref[keys, HD:] = k
        vt_ref[:HD, keys] = vs_ref[keys, :].T

    count = SHARE * per

    def score(i, s_ref):
        h, here = i // per, at((i % per) * KB, KB)
        q = q_ref[here, at((group * SHARE + h) * HD, HD)].astype(F32) * (SCALE * LOG2E)
        q_hi = q.astype(BF16)
        q_lo = (q - q_hi.astype(F32)).astype(BF16)
        qx = jnp.concatenate([q_hi, q_lo], axis=1)
        s = dot_nt(kx_ref[...], qx) + bias_ref[:, :, here].reshape(n_kb * KB, KB)
        s_ref[...] = s
        return jnp.max(s, axis=0, keepdims=True)

    def out(j, side):
        at_side = (j % 2) * 2 + side
        i = 2 * j + side
        return (
            pltpu.make_async_copy(ps_ref.at[at_side], p_ref.at[i], sems.at[at_side]),
            pltpu.make_async_copy(os_ref.at[at_side], o_ref.at[i], sems.at[4 + at_side]),
        )

    def soften(j, s_ref, top, side):
        at_side = (j % 2) * 2 + side
        e = jnp.exp2(s_ref[...] - top).astype(BF16)
        ps_ref[at_side] = e
        acc = dot(vt_ref[...], e)
        inv = 1.0 / acc[HD : HD + 1, :]
        os_ref[at_side, :, :HD] = (acc[:HD] * inv).T
        os_ref[at_side, :, HD:] = jnp.broadcast_to(inv, (HD, KB)).T

    def step(j, top):
        @pl.when(j == 1)
        def _():
            keep_w.wait()
            pass_w.start()

        @pl.when(j >= 2)
        def _():
            for copy in out(j - 2, 0) + out(j - 2, 1):
                copy.wait()

        later = score(2 * j + 1, t_ref)
        soften(j, s_ref, top, 0)
        top = score(jnp.minimum(2 * j + 2, count - 1), s_ref)
        soften(j, t_ref, later, 1)
        for copy in out(j, 0) + out(j, 1):
            copy.start()
        return top

    lax.fori_loop(0, count // 2, step, score(0, s_ref))
    for j in range(max(count // 2 - 2, 0), count // 2):
        for copy in out(j, 0) + out(j, 1):
            copy.wait()
    keep_k.wait()
    keep_v.wait()
    pass_w.wait()


def probs_call(group, groups, slots, shard, weight, depth, q, near, far, bias, n_kb):
    rows = q.shape[0]
    keys = n_kb * KB
    blocks = SHARE * rows // KB
    return call(
        functools.partial(probs_kernel, n_kb, group, groups),
        (slots, shard, weight, q, near, far, bias),
        [SMEM, SMEM, HBM] + [VMEM] * 4,
        [
            pltpu.HBM((blocks, keys, KB), BF16),
            pltpu.HBM((blocks, KB, 2 * HD), F32),
            pltpu.HBM((keys, HD), BF16),
            pltpu.HBM((keys, HD), BF16),
            pltpu.HBM((SHARE * HD, depth), BF16),
        ],
        scratch=[
            pltpu.VMEM((keys, HD), BF16),
            pltpu.VMEM((keys, HD), BF16),
            pltpu.VMEM((keys, 2 * HD), BF16),
            pltpu.VMEM((HD + 16, keys), BF16),
            pltpu.VMEM((keys, KB), F32),
            pltpu.VMEM((keys, KB), F32),
            pltpu.VMEM((4, keys, KB), BF16),
            pltpu.VMEM((4, KB, 2 * HD), F32),
            pltpu.VMEM((SHARE * HD, depth), BF16),
            pltpu.SemaphoreType.DMA((12,)),
        ],
        out_specs=[HBM] * 5,
    )


def back_kernel(
    n_kb, n_send, first, live_ref, pos_ref, edge_ref, proj_ref, x1_ref, x2_ref, w_ref, adv_ref,
    o_ref, q_ref, k_ref, v_ref, p_ref,
    dq_ref, send_ref, keep_ref, dox_ref, qs_ref, ds_ref, dqt_ref,
):
    rows = proj_ref.shape[0]
    per = rows // KB
    lane = lax.broadcasted_iota(jnp.int32, (KB, HD), 1)
    minus = jnp.where(lane < 3, -1.0, 0.0).astype(BF16)
    x = choose(edge_ref[0], x1_ref[...], x2_ref[...])
    dqt_ref[...] = jnp.zeros_like(dqt_ref)
    adv = jnp.broadcast_to(adv_ref[...], (HD, rows)).T
    for h in range(SHARE):
        cols = pl.ds((first + h) * HD, HD)
        fresh = dot_nt(x, w_ref[h * HD : (h + 1) * HD, :])
        for r in range(per):
            part = slice(r * KB, (r + 1) * KB)
            here = pl.ds((h * per + r) * KB, KB)
            out = o_ref[h * per + r]
            proj = proj_ref[part, cols] + fresh[part]
            grad = (proj * (adv[part] * out[:, HD:])).astype(BF16)
            delta = jnp.sum(grad.astype(F32) * out[:, :HD], axis=1, keepdims=True)
            one = delta.astype(BF16).astype(F32)
            two = (delta - one).astype(BF16).astype(F32)
            three = delta - one - two
            ext = jnp.where(
                lane == 0, one, jnp.where(lane == 1, two, jnp.where(lane == 2, three, 0.0))
            )
            dox_ref[here, :HD] = grad
            dox_ref[here, HD:] = ext.astype(BF16)
            qs_ref[here, :] = q_ref[part, cols]

    def put(kb, value):
        pos = pos_ref[kb]

        @pl.when(pos < n_send)
        def _():
            send_ref[pos] = value

        @pl.when(pos >= n_send)
        def _():
            keep_ref[pos - n_send] = value

    def chunk(start, count):
        keys = pl.ds(start * KB, count * KB)
        blocks = range(start, start + count)
        live = functools.reduce(jnp.bitwise_or, [live_ref[kb] for kb in blocks])

        @pl.when(live != 0)
        def _():
            vx = jnp.concatenate(
                [v_ref[keys, :], jnp.concatenate([minus] * count, axis=0)], axis=1
            )
            p = jnp.concatenate([p_ref[i, keys, :] for i in range(SHARE * per)], axis=1)
            dv = dot(p, dox_ref[:, :HD])
            for i in range(SHARE * per):
                here = pl.ds(i * KB, KB)
                dp = dot_nt(vx, dox_ref[here, :])
                ds_ref[: count * KB, here] = (p_ref[i, keys, :].astype(F32) * dp).astype(BF16)
            dqt_ref[...] += dot(k_ref[keys, :].T, ds_ref[: count * KB, :])
            dk = dot(ds_ref[: count * KB, :], qs_ref[...])
            for j, kb in enumerate(blocks):
                part = slice(j * KB, (j + 1) * KB)
                put(kb, jnp.stack([dk[part], dv[part]]).astype(BF16))

        @pl.when(live == 0)
        def _():
            for kb in blocks:
                put(kb, jnp.zeros((2, KB, HD), BF16))

    for start in range(0, n_kb, CHUNK):
        chunk(start, min(CHUNK, n_kb - start))
    for h in range(SHARE):
        dq_ref[:, pl.ds(h * HD, HD)] = (
            (dqt_ref[:, h * rows : (h + 1) * rows] * SCALE).T.astype(BF16)
        )


def back_call(group, live, pos, edge, proj, x1, x2, w, adv, o, q, k, v, p, n_kb, n_send):
    rows = q.shape[0]
    return call(
        functools.partial(back_kernel, n_kb, n_send, group * SHARE),
        (live, pos, edge, proj, x1, x2, w, adv, o, q, k, v, p),
        [SMEM] * 3 + [VMEM] * 10,
        [
            ((rows, SHARE * HD), BF16),
            ((max(n_send, 1), 2, KB, HD), BF16),
            ((n_kb - n_send, 2, KB, HD), BF16),
        ],
        scratch=[
            pltpu.VMEM((SHARE * rows, 2 * HD), BF16),
            pltpu.VMEM((SHARE * rows, HD), BF16),
            pltpu.VMEM((CHUNK * KB, SHARE * rows), BF16),
            pltpu.VMEM((HD, SHARE * rows), F32),
        ],
        flops=10 * SHARE * rows * n_kb * KB * HD,
        size=SHARE * rows * n_kb * KB * 2,
    )


def middle_kernel(me_ref, got_ref, keep_ref, base_ref, x_ref, y_ref, d_ref):
    me = me_ref[0]
    core, side, roll = me & 1, (me >> 1) & 1, me >= 4
    here = keep_ref[side].astype(F32) + got_ref[side].astype(F32)
    there = keep_ref[1 - side].astype(F32) + got_ref[1 - side].astype(F32)
    y_ref[...] = here.astype(BF16)
    d_ref[...] = there.astype(BF16)
    got = got_ref[2].astype(F32)
    late = (jnp.full(got.shape, core) == 1)

    @pl.when(roll)
    def _():
        x_ref[...] = (keep_ref[2].astype(F32) + jnp.where(late, got, 0.0)).astype(BF16)
        base_ref[...] = keep_ref[3].astype(F32) + jnp.where(late, 0.0, got)

    @pl.when(jnp.logical_not(roll))
    def _():
        x_ref[...] = there.astype(BF16)
        base_ref[...] = here


def last_kernel(groups, me_ref, *refs):
    dk_ref, dv_ref = refs[-2:]
    me = jnp.full((2, KB, HD), me_ref[0])
    across, beside = me < 4, me < 6
    for g in range(groups):
        base, x, y, d = refs[4 * g : 4 * g + 4]
        total = base[...] + jnp.where(beside, x[...].astype(F32), 0.0)
        total += jnp.where(across, y[...].astype(F32) + d[...].astype(F32), 0.0)
        dk_ref[:, g * HD : (g + 1) * HD] = (total[0] * SCALE).astype(BF16)
        dv_ref[:, g * HD : (g + 1) * HD] = total[1].astype(BF16)


def choose(flag, first, second):
    return jnp.where(jnp.full(first.shape, flag) != 0, first, second)


def project_kernel(count, added, halves, shard_ref, w_ref, *refs):
    xs, refs = refs[:count], refs[count:]
    if added:
        acc_ref, refs = refs[0], refs[1:]
    values = [x[...] for x in xs]
    if halves:
        values[-1] = choose(shard_ref[count], refs[0][...], values[-1])
        refs = refs[1:]
    out_ref, held_ref, sems = refs
    depth = xs[0].shape[1]
    blocks = w_ref.shape[0] // WB

    def fetch(i, n):
        return pltpu.make_async_copy(
            w_ref.at[pl.ds(n * WB, WB), pl.ds(pl.multiple_of(shard_ref[i] * depth, HD), depth)],
            held_ref.at[i, n],
            sems.at[i, n],
        )

    def start(n):
        for i in range(count):
            fetch(i, n).start()

    for n in range(min(AHEAD, blocks)):
        start(n)
    for n in range(blocks):
        here = slice(n * WB, (n + 1) * WB)
        total = acc_ref[:, here] if added else None
        for i in range(count):
            fetch(i, n).wait()
        if n + AHEAD < blocks:
            start(n + AHEAD)
        for i in range(count):
            part = dot_nt(values[i], held_ref[i, n])
            total = part if total is None else total + part
        out_ref[:, here] = total


def project_call(shards_of, xs, weight, acc=None, rest=None):
    rows, depth = xs[0].shape
    wide = weight.shape[0]
    count = len(xs)
    added, halves = acc is not None, rest is not None
    return call(
        functools.partial(project_kernel, count, added, halves),
        (shards_of, weight, *xs, *([acc] if added else []), *([rest] if halves else [])),
        [SMEM, HBM] + [VMEM] * (count + added + halves),
        [((rows, wide), F32)],
        scratch=[
            pltpu.VMEM((count, wide // WB, WB, depth), BF16),
            pltpu.SemaphoreType.DMA((count, wide // WB)),
        ],
    )[0]


def key_window(tok_rows, total):
    span = (total - total // 2) // ROLLOUTS
    reach = 3 * span + TILE + JITTER
    reach = reach // TILE * TILE
    return -(-reach // tok_rows)


def shards(
    upstream, advantage, out_weight, query_heads, key_heads, value_heads, segment_ids, tile_mask
):
    rows = query_heads.shape[0]
    n_ctx = lax.axis_size("ctx")
    n_tp = lax.axis_size("tp")
    total = rows * n_ctx
    prompt = total // 2
    groups = key_heads.shape[1] // HD
    me = lax.axis_index("ctx").astype(jnp.int32)
    z = lax.axis_index("tp").astype(jnp.int32)
    per = rows // KB
    back = key_window(rows, total)
    prompt_kb = prompt // KB
    n_kb = prompt_kb + (back + 1) * per
    fast = n_ctx == 8 and n_tp == 4 and per == 1 and back == 2
    shape = (rows, 2 * groups * HD)
    own = call(
        join_kernel,
        [pltpu.with_memory_space_constraint(x, pltpu.HBM) for x in (key_heads, value_heads)],
        [HBM] * 2,
        [(shape, BF16)],
        scratch=[pltpu.SemaphoreType.DMA((2,))],
    )[0]
    weight = pltpu.with_memory_space_constraint(out_weight, pltpu.HBM)

    def hop(value, pairs):
        return lax.ppermute(value, "tp", pairs)

    def flip(value, bit):
        return lax.ppermute(value, "ctx", [(i, i ^ bit) for i in range(n_ctx)])

    if fast:
        pieces = [own] + [flip(own, d) for d in (2, 4, 6)]
        near = call(stack_kernel, pieces, [VMEM] * 4, [((4,) + shape, BF16)])[0]
        ends, middle, out = [(0, 1), (1, 0), (2, 3), (3, 2)], [(1, 2), (2, 1)], [(1, 0), (2, 3)]
        up_a = hop(upstream, ends)
        up_c = hop(upstream, middle)
    else:
        near = lax.all_gather(own, "ctx", axis=0)
        near = far = near.reshape(n_ctx * per, KB, 2 * groups * HD)

    bias, live = mask_call(me, segment_ids, tile_mask, rows, n_kb, prompt, back)
    block = jnp.arange(n_kb, dtype=jnp.int32)
    holder = jnp.where(
        block < prompt_kb,
        block // per,
        jnp.where(me * rows >= prompt, me - (block - prompt_kb) // per, me),
    )
    if fast:
        away = holder ^ me
        slots = away // 2 + (away % 2) * 4
        core = me & 1
        pos = jnp.where(
            block < 4,
            jnp.where(block % 2 == core, 3 + block // 2, block // 2),
            jnp.array([0, 0, 0, 0, 6, 2, 5], jnp.int32),
        )
        n_send = 3
        half, edge = z // 2, (z % 3 == 0).astype(jnp.int32)
        second, shard = 2 - half, 3 - 3 * half
        acc = project_call(z[None], [upstream], weight)
    else:
        slots = holder * per + block % per
        pos = block
        n_send = 0
        whole = lax.all_gather(upstream, "tp", axis=0)
        shard = z
        acc = jnp.zeros((rows, out_weight.shape[0]), F32)
        for i in range(n_tp - 1):
            other = (z + 1 + i) % n_tp
            x = lax.dynamic_index_in_dim(whole, other, 0, keepdims=False)
            acc = project_call(other[None], [x], weight, acc)
        x1, x2, edge = upstream, upstream, jnp.int32(1)

    slots = slots.astype(jnp.int32)
    depth = upstream.shape[1]
    if fast:
        up_a, up_c, bias, acc = lax.optimization_barrier((up_a, up_c, bias, acc))
        up_e = hop(up_a, middle)
        up_f = hop(up_c, out)
        near, up_a = lax.optimization_barrier((near, up_a))
        far = flip(near, 1)
    soft = [list(probs_call(0, groups, slots, shard[None], weight, depth, query_heads, near, far, bias, n_kb))]
    if fast:
        up_e, soft[0][2] = lax.optimization_barrier((up_e, soft[0][2]))
        up_d = hop(up_e, out)
        x1, x2 = up_d, up_e
    soft += [
        list(probs_call(g, groups, slots, shard[None], weight, depth, query_heads, near, far, bias, n_kb))
        for g in range(1, groups)
    ]
    if fast:
        acc, soft[-1][2] = lax.optimization_barrier((acc, soft[-1][2]))
        acc = project_call(jnp.stack([z ^ 1, second, edge]), [up_a, up_c], weight, acc, up_f)
    outs, final, turn = [], [], edge[None]
    for g in range(groups):
        probs, attn, keys, values, w_last = soft[g]
        outs.append(
            back_call(
                g, live, pos.astype(jnp.int32), turn, acc, x1, x2, w_last, advantage[None, :],
                attn, query_heads, keys, values, probs, n_kb, n_send,
            )
        )
        if fast:
            block = (2, KB, HD)
            send, *final = lax.optimization_barrier((outs[g][1], *final))
            base, to_x, to_y, to_d = call(
                middle_kernel,
                (me[None], flip(send, 1), outs[g][2]),
                [SMEM, VMEM, VMEM],
                [(block, F32), (block, BF16), (block, BF16), (block, BF16)],
            )
            base, turn = lax.optimization_barrier((base, turn))
            final += [base, flip(to_x, 2), flip(to_y, 4), flip(to_d, 6)]
    grad_queries = jnp.concatenate([dq for dq, _, _ in outs], axis=1)

    if fast:
        grad_keys, grad_values = call(
            functools.partial(last_kernel, groups),
            [me[None]] + final,
            [SMEM] + [VMEM] * len(final),
            [((rows, groups * HD), BF16)] * 2,
        )
        return grad_queries, grad_keys, grad_values

    win = (back + 1) * rows
    win_start = jnp.maximum(me - back, 0) * rows
    part = jnp.concatenate([keep for _, _, keep in outs], axis=3).astype(F32)
    part = part.transpose(0, 2, 1, 3).reshape(prompt + win, 2, groups * HD)
    rear = part[prompt:].reshape(back + 1, rows, 2, groups * HD)[::-1].reshape(win, 2, -1)
    full = jnp.zeros((total, 2, groups * HD), F32).at[:prompt].set(part[:prompt])
    old = lax.dynamic_slice_in_dim(full, win_start, win, 0)
    full = lax.dynamic_update_slice_in_dim(full, old + rear, win_start, 0)
    reduced = lax.psum_scatter(full, "ctx", scatter_dimension=0, tiled=True)
    return (
        grad_queries,
        (reduced[:, 0] * SCALE).astype(BF16),
        reduced[:, 1].astype(BF16),
    )


def solution(mesh):
    placed = (
        P("ctx", "tp"),
        P("ctx"),
        P("tp", None),
        P("ctx", "tp"),
        P("ctx", "tp"),
        P("ctx", "tp"),
        P(),
        P("ctx", None),
    )
    return jax.shard_map(
        shards,
        mesh=mesh,
        in_specs=placed,
        out_specs=(P("ctx", "tp"), P("ctx", "tp"), P("ctx", "tp")),
        check_vma=False,
    )
```
